32 devices in a mesh: dp: 4 (over z), lat: 2 (over core), lon: 4 (over y, x).
Axes of the slice: x: 2, y: 2, z: 4, core: 2. Of those that a mesh axis runs over, the one named last changes fastest.
Arguments:
- inputs: bfloat16 [48, 32, 64, 128], P('dp', 'lat', 'lon'), may hold values from -24 to 24
- lead_time: int32 [48], P('dp'), may hold values from 1 to 20
- cotangent: bfloat16 [48, 32, 64, 128], P('dp', 'lat', 'lon'), may hold values from -6 to 6
- conv_weight: float32 [2, 1152, 128], P(None, 'dp'), may hold values from -0.1875 to 0.1875
- conv_first: float32 [2, 1152, 128], P(None, 'dp'), may hold values from -0.01171875 to 0.01171875
- conv_second: float32 [2, 1152, 128], P(None, 'dp'), may hold values from 0 to 1, as said below
- vectors: float32 [6, 128], P(None, 'dp'), may hold values from -2 to 5, as said below
- vec_first: float32 [6, 128], P(None, 'dp'), may hold values from -0.005859375 to 0.005859375
- vec_second: float32 [6, 128], P(None, 'dp'), may hold values from 0 to 1, as said below
Outputs:
- outputs: bfloat16 [48, 32, 64, 128], P('dp', 'lat', 'lon')
- grad_inputs: bfloat16 [48, 32, 64, 128], P('dp', 'lat', 'lon')
- grad_norm: float32 [], replicated
- conv_new: float32 [2, 1152, 128], P(None, 'dp')
- conv_first_new: float32 [2, 1152, 128], P(None, 'dp')
- conv_second_new: float32 [2, 1152, 128], P(None, 'dp')
- conv_low: bfloat16 [2, 1152, 128], P(None, 'dp')
- vec_new: float32 [6, 128], P(None, 'dp')
- vec_first_new: float32 [6, 128], P(None, 'dp')
- vec_second_new: float32 [6, 128], P(None, 'dp')
The draws below stay inside these ranges and needn't reach their ends.
Inputs may be any that keep to these rules, and one draw needn't show every extreme that they name: `conv_second`: positive. `vectors`: rows 1 and 4 are positive. `vec_second`: positive.
All inputs are finite; a program needn't handle non-finite values.
Results may differ from the reference program's by a relative error of at most 0.01.
Values may be sent and summed in bfloat16 or wider, within the bound.
No kernel may reach another device: no remote copies, remote signals or barrier semaphores. Data moves between devices by JAX's collectives and lax.ppermute only.
A program may use at most 128 MiB of HBM per device.

```python
import jax
import jax.numpy as jnp
from jax import lax

C = 128
SB = 4
MB = 3
STEP = 5
SAMPLES = 48
NLAT = 32
NLON = 64
N_DP = 4


def ramp_of(length):
    return jnp.arange(length, dtype=jnp.float32) / max(length - 1, 1)


def draw_inputs(key, part):
    key = jax.random.fold_in(key, 21)
    shape_all = (SAMPLES, NLAT, NLON, C)
    base_vals = jnp.clip(jax.random.normal(key, shape_all, jnp.float32), -6.0, 6.0)
    power_exp = 0.5
    spread = ramp_of(SAMPLES)[:, None, None, None] + ramp_of(NLAT)[None, :, None, None] + ramp_of(NLON)[None, None, :, None]
    exponent = power_exp * spread + ramp_of(C) - (1.5 * power_exp + 0.5)
    return (base_vals * jnp.exp(exponent * 1.0986123)).astype(jnp.bfloat16)


def draw_vectors(key, part):
    key_offs = jax.random.fold_in(key, 11)
    key_gain = jax.random.fold_in(key, 12)
    offsets = 0.3 * jnp.clip(jax.random.normal(key_offs, (6, C), jnp.float32), -4.0, 4.0)
    gains = jnp.exp(jax.random.uniform(key_gain, (2, C), jnp.float32, -0.2, 0.2)) * jnp.exp(ramp_of(C) * 1.0986123)
    return jnp.stack([offsets[0], gains[0], offsets[2], offsets[3], gains[1], offsets[5]])


def draw_conv_second(key, part):
    key = jax.random.fold_in(key, 22)
    params_total = 18 * C * C + 6 * C
    return jnp.exp(jax.random.uniform(key, (2, 9 * C, C), jnp.float32, 0.0, 1.3862944)) / params_total


def draw_vec_second(key, part):
    key = jax.random.fold_in(key, 23)
    params_total = 18 * C * C + 6 * C
    return 0.25 * jnp.exp(jax.random.uniform(key, (6, C), jnp.float32, 0.0, 1.3862944)) / params_total


def touch_ends(entries, rng, smallest, high):
    longest = entries.shape.index(max(entries.shape))
    spots = []
    for shift in (0, 1):
        where = [jax.random.randint(jax.random.fold_in(rng, axis), (), 0, length) for axis, length in enumerate(entries.shape)]
        where[longest] = (where[longest] + shift) % entries.shape[longest]
        spots.append(tuple(where))
    return entries.at[spots[0]].set(smallest).at[spots[1]].set(high)


def steps_of(own_key, dims, cuts, smallest, high):
    loudness = 1.0
    for axis_at, parts in cuts:
        heights = jax.random.uniform(jax.random.fold_in(jax.random.fold_in(own_key, 6), axis_at), (parts,), jnp.float32, smallest / len(cuts), high / len(cuts))
        loudness = loudness * jnp.repeat(jnp.exp(heights), dims[axis_at] // parts).reshape((-1,) + (1,) * (len(dims) - 1 - axis_at))
    return loudness


def gaussian(key, shape, scale, limit, pieces=(), kind=jnp.bfloat16):
    factor_of = steps_of(key, shape, pieces, -0.22, 0.18) if pieces else 1.0
    array = jax.random.normal(key, shape, jnp.float32) * scale * factor_of
    return jnp.minimum(jnp.maximum(array, -limit), limit).astype(kind)


def setup_inputs(seed: int = 0) -> dict:
    keys = jax.random.split(jax.random.key(seed), 10)
    inputs = draw_inputs(jax.random.fold_in(keys[9], 71), 0)
    lead_time = touch_ends(jax.random.randint(keys[1], (SAMPLES,), 1, 21), jax.random.fold_in(keys[1], 1), 1, 20).astype(jnp.int32)
    cotangent = gaussian(keys[2], (SAMPLES, NLAT, NLON, C), 1.0, 6.0, ((0, 4), (1, 2), (2, 4)))
    conv_weight = gaussian(keys[3], (2, 9 * C, C), (9 * C) ** -0.5, 0.1875, ((1, 4),), jnp.float32)
    conv_first = gaussian(keys[4], (2, 9 * C, C), (18 * C * C + 6 * C) ** -0.5, 0.01171875, ((1, 4),), jnp.float32)
    conv_second = draw_conv_second(jax.random.fold_in(keys[9], 71), 0)
    vectors = draw_vectors(jax.random.fold_in(keys[9], 71), 0)
    vec_first = gaussian(keys[7], (6, C), (4 * (18 * C * C + 6 * C)) ** -0.5, 0.005859375, ((1, 4),), jnp.float32)
    vec_second = draw_vec_second(jax.random.fold_in(keys[9], 71), 0)
    return {"inputs": inputs, "lead_time": lead_time, "cotangent": cotangent, "conv_weight": conv_weight, "conv_first": conv_first, "conv_second": conv_second, "vectors": vectors, "vec_first": vec_first, "vec_second": vec_second}


EPS = 1e-05
CLIP = 1.0
BETA_ONE = 0.5
BETA_TWO = 0.5
RATE_CONV = 0.03
RATE_VEC = 0.3
DECAY_CONV = 0.01
ADAM_EPS = 1e-08
HIGH = lax.Precision.HIGHEST

@jax.custom_vjp
def low(v):
    return lax.optimization_barrier(v.astype(jnp.bfloat16)).astype(jnp.float32)

@jax.custom_vjp
def low_back(v):
    return v

def low_keep(v):
    return (low(v), None)

def low_pass(kept, grad):
    return (grad,)

def back_keep(v):
    return (v, None)

def back_low(kept, grad):
    return (low(grad),)
low.defvjp(low_keep, low_pass)
low_back.defvjp(back_keep, back_low)

def padded_grid(grid_in):
    wrapped = jnp.concatenate([grid_in[:, :, -1:], grid_in, grid_in[:, :, :1]], axis=2)
    return jnp.pad(wrapped, ((0, 0), (1, 1), (0, 0), (0, 0)))

def convolve(grid_in, weight):
    channels = grid_in.shape[-1]
    kernel = weight.reshape(channels, 3, 3, -1).transpose(1, 2, 0, 3)
    return lax.conv_general_dilated(padded_grid(grid_in), kernel, (1, 1), 'VALID', dimension_numbers=('NHWC', 'HWIO', 'NHWC'), precision=HIGH)

def batch_norm(active, gain_row, shift_row):
    mean_val = lax.optimization_barrier(jnp.mean(active, axis=(0, 1, 2)))
    mean_sq = lax.optimization_barrier(jnp.mean(active * active, axis=(0, 1, 2)))
    inverse = lax.rsqrt(mean_sq - mean_val * mean_val + EPS)
    return (active - mean_val) * inverse * gain_row + shift_row

def block_forward(sample_in, weights, params):
    weights_low = low(weights)
    params_low = low(params)
    pre_one = low_back(convolve(sample_in, weights_low[0]) + params_low[0])
    norm_one = low(batch_norm(jax.nn.gelu(pre_one), params_low[1], params_low[2]))
    pre_two = low_back(convolve(norm_one, weights_low[1]) + params_low[3])
    return sample_in + batch_norm(jax.nn.gelu(pre_two), params_low[4], params_low[5])

def adam_step(weight, first, second, grad, rate, decay):
    first_new = BETA_ONE * first + (1.0 - BETA_ONE) * grad
    second_new = BETA_TWO * second + (1.0 - BETA_TWO) * grad * grad
    first_hat = first_new / (1.0 - BETA_ONE ** STEP)
    second_hat = second_new / (1.0 - BETA_TWO ** STEP)
    weight_new = weight - rate * (first_hat / (jnp.sqrt(second_hat) + ADAM_EPS) + decay * weight)
    return (weight_new, first_new, second_new)

def reference(inputs, lead_time, cotangent, conv_weight, conv_first, conv_second, vectors, vec_first, vec_second):
    shape_grid = (N_DP, MB, SB, NLAT, NLON, C)
    grid_all = inputs.astype(jnp.float32).reshape(shape_grid)
    lead_scale = (0.5 * jnp.sqrt(lead_time.astype(jnp.float32))).reshape(N_DP, MB, SB, 1, 1, 1)
    grad_all = cotangent.astype(jnp.float32).reshape(shape_grid) * lead_scale
    grad_conv = jnp.zeros(conv_weight.shape, jnp.float32)
    grad_vec = jnp.zeros(vectors.shape, jnp.float32)
    result_list = []
    grads_list = []
    for batch_index in range(MB):
        sample_in = grid_all[:, batch_index].reshape(N_DP * SB, NLAT, NLON, C)
        result, pullback = jax.vjp(block_forward, sample_in, conv_weight, vectors)
        grad_in, grad_weight, grad_params = pullback(grad_all[:, batch_index].reshape(N_DP * SB, NLAT, NLON, C))
        result_list.append(result.reshape(N_DP, SB, NLAT, NLON, C))
        grads_list.append(grad_in.reshape(N_DP, SB, NLAT, NLON, C))
        grad_conv = grad_conv + grad_weight
        grad_vec = grad_vec + grad_params
    outputs = jnp.stack(result_list, axis=1).reshape(SAMPLES, NLAT, NLON, C).astype(jnp.bfloat16)
    grad_inputs = jnp.stack(grads_list, axis=1).reshape(SAMPLES, NLAT, NLON, C).astype(jnp.bfloat16)
    grad_norm = jnp.sqrt(jnp.sum(grad_conv * grad_conv) + jnp.sum(grad_vec * grad_vec))
    clip_factor = jnp.minimum(1.0, CLIP / (grad_norm + 1e-06))
    conv_new, conv_first_new, conv_second_new = adam_step(conv_weight, conv_first, conv_second, grad_conv * clip_factor, RATE_CONV, DECAY_CONV)
    vec_new, vec_first_new, vec_second_new = adam_step(vectors, vec_first, vec_second, grad_vec * clip_factor, RATE_VEC, 0.0)
    return (outputs, grad_inputs, grad_norm, conv_new, conv_first_new, conv_second_new, conv_new.astype(jnp.bfloat16), vec_new, vec_first_new, vec_second_new)
```

```python
import math

import jax
import jax.numpy as jnp
from jax import lax
from jax.experimental import pallas as pl
from jax.experimental.pallas import tpu as pltpu
from jax.sharding import PartitionSpec as P

MB = 3
STEP = 5
EPS = 1e-05
CLIP = 1.0
BETA_ONE = 0.5
BETA_TWO = 0.5
RATE_CONV = 0.03
RATE_VEC = 0.3
DECAY_CONV = 0.01
ADAM_EPS = 1e-08
ALL = ("dp", "lat", "lon")
F32 = jnp.float32
BF16 = jnp.bfloat16
GELU_A = math.sqrt(2.0 / math.pi)
GELU_B = GELU_A * 0.044715

S, R, C = 12, 16, 128
TI = S * R
NH = S + 1
TH = 8 * (NH + NH % 2)
T = TI + TH
W3 = 3 * C
PER = S // MB
FLAT = 24 + 24 * S
VM = pl.BlockSpec(memory_space=pltpu.VMEM)


def call(kernel, outs, args, scratch=(), flops=0, limit=16, scalars=0):
    return pl.pallas_call(
        kernel,
        out_shape=tuple(jax.ShapeDtypeStruct(shape, kind) for shape, kind in outs),
        in_specs=[pl.BlockSpec(memory_space=pltpu.SMEM)] * scalars + [VM] * (len(args) - scalars),
        out_specs=tuple([VM] * len(outs)),
        scratch_shapes=list(scratch),
        compiler_params=pltpu.CompilerParams(vmem_limit_bytes=limit << 20),
        cost_estimate=pl.CostEstimate(
            flops=flops,
            transcendentals=0,
            bytes_accessed=sum(math.prod(a.shape) * a.dtype.itemsize for a in args),
        ),
    )(*args)


def own_row(row):
    return jnp.where(lax.axis_index("lat") == 0, row, R - 1 - row)


def own_tap(tap):
    return jnp.where(lax.axis_index("lat") == 0, tap, 2 - tap)


def act(v):
    return 0.5 * v * (1.0 + jnp.tanh(v * (GELU_A + GELU_B * (v * v))))


def act_both(v):
    sq = v * v
    tan = jnp.tanh(v * (GELU_A + GELU_B * sq))
    half = 0.5 * (1.0 + tan)
    value = v * half
    slope = half + value * (1.0 - tan) * (GELU_A + (3.0 * GELU_B) * sq)
    return value, slope


def fold(v):
    return jnp.sum(v.reshape(v.shape[0] // 8, 8, C), axis=0)


def down(v):
    return jnp.sum(v, axis=0, keepdims=True)


def batch_sums(values):
    return [fold(values[PER * R * m : PER * R * (m + 1)]) for m in range(MB)]


def build(flat, out, place, tile, side):
    for n in range(S):
        value = tile(n)
        flat[16 + 24 * n : 32 + 24 * n, :] = value
        out[place + (slice(16 * n, 16 * n + 16), slice(C, 2 * C))] = value.astype(BF16)
    whole = out.shape[-2] == T
    for p in range(TH // 16):
        pair = [side(h) if h < NH else jnp.zeros((8, C), F32) for h in (2 * p, 2 * p + 1)]
        for h, value in zip((2 * p, 2 * p + 1), pair):
            if h < NH:
                flat[8 + 24 * h : 16 + 24 * h, :] = value
        if whole:
            at = TI + 16 * p
            out[place + (slice(at, at + 16), slice(C, 2 * C))] = jnp.concatenate(pair, axis=0).astype(BF16)
    emit_sides(flat, out, place)


def emit_sides(flat, out, place):
    for kx in (0, 2):
        columns = slice(C * kx, C * kx + C)
        for n in range(S):
            at = 15 + 24 * n + kx
            out[place + (slice(16 * n, 16 * n + 16), columns)] = flat[at : at + 16, :].astype(BF16)
        if out.shape[-2] != T:
            continue
        for p in range(TH // 16):
            at = 7 + 48 * p + kx
            first = flat[at : at + 8, :]
            second = flat[at + 24 : at + 32, :] if 2 * p + 1 < NH else jnp.zeros((8, C), F32)
            out[place + (slice(TI + 16 * p, TI + 16 * p + 16), columns)] = jnp.concatenate(
                [first, second], axis=0
            ).astype(BF16)


def place_of(i, odd):
    return (i + odd, 1 - odd)


def sided(rows):
    mixed = {}
    for h in range(NH):
        low, high = max(h - 1, 0) // PER, min(h, S - 1) // PER
        if low != high:
            mixed[h] = jnp.concatenate(
                [jnp.broadcast_to(rows[low], (4, C)), jnp.broadcast_to(rows[high], (4, C))], axis=0
            )
    return (
        lambda n: rows[n // PER],
        lambda h: mixed[h] if h in mixed else rows[min(h, S - 1) // PER],
    )


def put_all(ref, rows):
    block = jnp.concatenate(rows, axis=0)
    ref[...] = jnp.broadcast_to(block[None], ref.shape)


def taken(ref, count):
    total = jnp.sum(ref[...], axis=0)
    return [total[i : i + 1] for i in range(count)]


def vec_rows(ref):
    return [ref[i : i + 1, :] for i in range(6)]


def norm_of(sums, count):
    means = [sums[m] * (1.0 / count) for m in range(MB)]
    inverses = [lax.rsqrt(sums[MB + m] * (1.0 / count) - means[m] * means[m] + EPS) for m in range(MB)]
    return means, inverses


def fill_forward(block, pieces):
    size, count = C // len(pieces), len(pieces)
    zero = jnp.zeros((C, C), BF16)
    for kx in range(3):
        block[C * kx : C * kx + C, C:] = zero
        block[C * (9 + kx) : C * (10 + kx), :C] = zero
        for ky in range(3):
            source = pl.multiple_of((3 * own_tap(ky) + kx) * size, size)
            for k, piece in enumerate(pieces):
                owner = lax.rem(lax.axis_index("dp") + (count - k), count) if count > 1 else 0
                part = piece[pl.ds(source, size), :]
                for a in range(2):
                    top = pl.multiple_of((3 * (ky + a) + kx) * C + owner * size, size)
                    block[pl.ds(top, size), a * C : a * C + C] = part


def fill_backward(block, forward):
    zero = jnp.zeros((C, C), BF16)
    for kx in range(3):
        block[C * kx : C * kx + C, C:] = zero
        block[C * (9 + kx) : C * (10 + kx), :C] = zero
        for ky in range(3):
            source = (3 * (2 - ky) + 2 - kx) * C
            part = forward[source : source + C, :C].T
            for a in range(2):
                top = (3 * (ky + a) + kx) * C
                block[top : top + C, a * C : a * C + C] = part


def conv_rows(ref, low, high, weight, rows=T):
    pairs = [
        jnp.concatenate([ref[i, 0, :rows], ref[i, 1, :rows], ref[i + 1, 0, :rows], ref[i + 1, 1, :rows]], axis=1)
        for i in range(low, high)
    ]
    got = jnp.dot(jnp.concatenate(pairs, axis=0), weight, preferred_element_type=F32)
    return [
        got[n * rows : n * rows + rows, a * C : a * C + C] for n in range(high - low) for a in range(2)
    ]


def added(total, new):
    return new if total is None else [old + more for old, more in zip(total, new)]


def prep_kernel(x, cot, weight, vectors, m1, m2, lat_out):
    size = weight.shape[1] // 9
    for t in range(9):
        m1[size * t : size * t + size, :] = weight[0, pl.ds(t, size, stride=9), :].astype(BF16)
        m2[size * t : size * t + size, :] = weight[1, pl.ds(t, size, stride=9), :].astype(BF16)
    width = vectors.shape[1]
    pick = lax.broadcasted_iota(jnp.int32, (width, C), 1) - lax.axis_index("dp") * width
    pick = jnp.where(pick == lax.broadcasted_iota(jnp.int32, (width, C), 0), 1.0, 0.0).astype(BF16)
    placed = jnp.dot(vectors[...].astype(BF16), pick, preferred_element_type=F32)
    m1[size * 9 :, :] = jnp.concatenate([placed, jnp.zeros((10, C), F32)], axis=0).astype(BF16)
    for k in range(4):
        source = own_row(R - 1 - k)
        for s in range(S):
            lat_out[k, s] = x[s, source]
            if k < 2:
                lat_out[4 + k, s] = cot[s, source]


def edge_kernel(x, cot, lat_in, x_r, x_l, c_r, c_l):
    def cut(tiles, right, left, row):
        for m in range(MB):
            four = [tiles(s).astype(F32) for s in range(PER * m, PER * m + PER)]
            right[row, m] = jnp.concatenate([v[R - 4 :] for v in four], axis=0).astype(BF16)
            left[row, m] = jnp.concatenate([v[:4] for v in four], axis=0).astype(BF16)

    @pl.loop(0, R)
    def _(row):
        source = own_row(row)
        cut(lambda s: x[s, source], x_r, x_l, row)
        cut(lambda s: cot[s, source], c_r, c_l, row)

    for k in range(4):
        cut(lambda s: lat_in[k, s], x_r, x_l, R + k)
        if k < 2:
            cut(lambda s: lat_in[4 + k, s], c_r, c_l, R + k)


def fill_sides(flat, from_left, from_right, row, scale=None):
    for m in range(MB):
        left = from_left[row, m].astype(F32)
        right = from_right[row, m].astype(F32)
        for n in range(PER):
            s = PER * m + n
            low, high = left[4 * n : 4 * n + 4], right[4 * n : 4 * n + 4]
            if scale is not None:
                low, high = low * scale[s], high * scale[s]
            flat[12 + 24 * s : 16 + 24 * s, :] = low
            flat[32 + 24 * s : 36 + 24 * s, :] = high


def shift_kernel(x, lat_in, from_left, from_right, out, *flats):
    for flat in flats:
        flat[...] = jnp.zeros(flat.shape, F32)
    for edge in (0, R + 5):
        out[edge // 2, edge % 2] = jnp.zeros((T, W3), BF16)

    def one(flat, row, tile, place):
        for n in range(S):
            value = tile(n)
            flat[16 + 24 * n : 32 + 24 * n, :] = value.astype(F32)
            out[place + (slice(16 * n, 16 * n + 16), slice(C, 2 * C))] = value
        fill_sides(flat, from_left, from_right, row)
        for p in range(TH // 16):
            at = 8 + 48 * p
            second = flat[at + 24 : at + 32, :] if 2 * p + 1 < NH else jnp.zeros((8, C), F32)
            out[place + (slice(TI + 16 * p, TI + 16 * p + 16), slice(C, 2 * C))] = jnp.concatenate(
                [flat[at : at + 8, :], second], axis=0
            ).astype(BF16)
        emit_sides(flat, out, place)

    @pl.loop(0, R // 2)
    def _(i):
        for odd in range(2):
            source = own_row(2 * i + odd)
            one(flats[odd], 2 * i + odd, lambda n: x[n, source], place_of(i, odd))

    for k in range(4):
        one(flats[k % 2], R + k, lambda n: lat_in[k, n], place_of((R + k) // 2, k % 2))


def lead_kernel(lead, cot, lat_in, from_left, from_right, dn, sums, *flats):
    scale = [0.5 * jnp.sqrt(jnp.full((1, C), lead[n], jnp.int32).astype(F32)) for n in range(S)]
    for flat in flats:
        flat[...] = jnp.zeros(flat.shape, F32)

    def one(flat, row, tile):
        values = [tile(n).astype(F32) * scale[n] for n in range(S)]
        for n in range(S):
            dn[row, 16 * n : 16 * n + 16, :] = values[n]
        fill_sides(flat, from_left, from_right, row, scale)
        for h in range(NH):
            dn[row, TI + 8 * h : TI + 8 * h + 8, :] = flat[8 + 24 * h : 16 + 24 * h, :]
        dn[row, TI + 8 * NH :, :] = jnp.zeros((TH - 8 * NH, C), F32)
        return [sum(fold(values[n]) for n in range(PER * m, PER * m + PER)) for m in range(MB)]

    def body(i, total):
        for odd in range(2):
            source = own_row(2 * i + odd)
            total = added(total, one(flats[odd], 2 * i + odd, lambda n: cot[n, source]))
        return total

    total = lax.fori_loop(0, R // 2, body, [jnp.zeros((8, C), F32)] * MB)
    for k in range(2):
        one(flats[k], R + k, lambda n: lat_in[4 + k, n])
    sums[...] = jnp.concatenate([down(v) for v in total] + [jnp.zeros((8 - MB, C), F32)], axis=0)


def block_kernel(*rest):
    pieces, (block, vec) = rest[:-2], rest[-2:]
    fill_forward(block, pieces)
    total = pieces[0][-16:, :].astype(F32)
    for piece in pieces[1:]:
        total = total + piece[-16:, :].astype(F32)
    vec[...] = total


def weight_kernel(block_one, *rest):
    pieces, (block_two, two_back, one_back) = rest[:-3], rest[-3:]
    fill_forward(block_two, pieces)
    fill_backward(two_back, block_two)
    fill_backward(one_back, block_one)


def first_kernel(x_all, block, vec, pre, sums):
    bias = vec[0:1, :]
    total = None
    for low, high in ((0, 5), (5, 10)):
        for n, v in enumerate(conv_rows(x_all, low, high, block[...])):
            row = 2 * low + n
            pre[row] = v + bias
            if row < R:
                value = act(v[:TI] + bias)
                total = added(total, batch_sums(value) + batch_sums(value * value))
    put_all(sums, [down(v) for v in total] + [jnp.zeros((2, C), F32)])


def second_kernel(count, pre, sums_in, dn, dn_sums, block, vec_in, n_all, pre_two, sums, *flats):
    vec = vec_rows(vec_in)
    means, inverses = norm_of(taken(sums_in, 2 * MB), count)
    gains = [inverses[m] * vec[1] for m in range(MB)]
    gain, gain_side = sided(gains)
    shift, shift_side = sided([vec[2] - means[m] * gains[m] for m in range(MB)])
    for flat in flats:
        flat[...] = jnp.zeros(flat.shape, F32)
    n_all[0, 0] = jnp.zeros((T, W3), BF16)

    def one(i, odd):
        row = 2 * i + odd
        build(
            flats[odd],
            n_all,
            place_of(i, odd),
            lambda n: act(pre[row, 16 * n : 16 * n + 16, :]) * gain(n) + shift(n),
            lambda h: act(pre[row, TI + 8 * h : TI + 8 * h + 8, :]) * gain_side(h) + shift_side(h),
        )

    @pl.loop(0, R // 2 + 1)
    def _(i):
        for odd in range(2):
            one(i, odd)

    one(R // 2 + 1, 0)
    total = None
    for low, high in ((0, 5), (5, 9)):
        for n, v in enumerate(conv_rows(n_all, low, high, block[...])):
            row = 2 * low + n
            pre_two[row] = v + vec[3]
            if row < R:
                value = act(v[:TI] + vec[3])
                new = batch_sums(value) + batch_sums(value * value) + batch_sums(value * dn[row, :TI, :])
                total = added(total, new)
    block_out = jnp.concatenate([down(v) for v in total] + [dn_sums[0:MB, :]], axis=0)
    for g in range(3):
        part = block_out[4 * g : 4 * g + 4]
        for n in range(sums.shape[0]):
            sums[n, g] = part


def second_stats(sums_in, count):
    total = jnp.sum(sums_in[...], axis=0)
    rows = [total[i // 4, i % 4 : i % 4 + 1, :] for i in range(4 * MB)]
    means, inverses = norm_of(rows[: 2 * MB], count)
    dots, plain = rows[2 * MB : 3 * MB], rows[3 * MB :]
    dgain = [inverses[m] * (dots[m] - means[m] * plain[m]) for m in range(MB)]
    return means, inverses, dgain, plain


def back_terms(means, inverses, gain, dgain, dshift, count):
    lin = [inverses[m] * gain for m in range(MB)]
    slope = [-lin[m] * inverses[m] * (dgain[m] * (1.0 / count)) for m in range(MB)]
    const = [-lin[m] * (dshift[m] * (1.0 / count)) - slope[m] * means[m] for m in range(MB)]
    return [sided(rows) for rows in (lin, const, slope)]


def build_back(flat, out, place, pre, incoming, row, terms):
    def at(start, size, which, index):
        value, deriv = act_both(pre[row, start : start + size, :])
        lin, const, slope = [term[which](index) for term in terms]
        return deriv * (lin * incoming[row, start : start + size, :] + const + slope * value)

    build(
        flat,
        out,
        place,
        lambda n: at(16 * n, 16, 0, n),
        lambda h: at(TI + 8 * h, 8, 1, h),
    )


def back_two_kernel(count, pre_two, dn, sums_in, pre, block, vec, grad, mid, sums, g_all, *flats):
    means, inverses, dgain, dshift = second_stats(sums_in, count)
    terms = back_terms(means, inverses, vec[4:5, :], dgain, dshift, count)
    for flat in flats:
        flat[...] = jnp.zeros(flat.shape, F32)
    for edge in (0, R + 3):
        g_all[edge // 2, edge % 2] = jnp.zeros((T, W3), BF16)

    def body(i, total):
        for odd in range(2):
            place = place_of(i, odd)
            build_back(flats[odd], g_all, place, pre_two, dn, 2 * i + odd, terms)
            own = g_all[place + (slice(0, TI), slice(C, 2 * C))]
            grad[2 * i + odd] = own
            total = total + fold(own.astype(F32))
        return total

    bias = lax.fori_loop(0, R // 2, body, jnp.zeros((8, C), F32))
    for odd in range(2):
        build_back(flats[odd], g_all, place_of(R // 2, odd), pre_two, dn, R + odd, terms)
    total = None
    for low, high in ((0, 5), (5, 9)):
        for n, v in enumerate(conv_rows(g_all, low, high, block[...])):
            row = 2 * low + n
            mid[row] = v
            if row < R:
                own = v[:TI]
                total = added(total, batch_sums(own) + batch_sums(own * act(pre[row, :TI, :])))
    put_all(sums, [down(v) for v in total] + [down(bias), jnp.zeros((1, C), F32)])


def wgrad(inner, grad, ky):
    total = None
    for low in range(0, R, 4):
        left = jnp.concatenate([grad(row) for row in range(low, low + 4)], axis=0)
        right = jnp.concatenate(
            [inner[(row + ky) // 2, (row + ky) % 2, :TI] for row in range(low, low + 4)], axis=0
        )
        part = lax.dot_general(left, right, (((0,), (0,)), ((), ())), preferred_element_type=F32)
        total = part if total is None else total + part
    return total


def split_out(ky, got, keep, send):
    lat = lax.axis_index("lat")
    for kx in range(3):
        tap = 3 * own_tap(ky) + kx
        for d in range(4):
            for half in range(2):
                start = C * kx + 32 * d + 16 * half

                def store(ref):
                    for n in range(4):
                        ref[4 * d + n, pl.ds(4 * tap, 4), :] = got[start + 4 * n : start + 4 * n + 4]

                pl.when(lat == half)(lambda: store(keep))
                pl.when(lat != half)(lambda: store(send))


def plain_out(ky, got, out):
    for kx in range(3):
        out[3 * own_tap(ky) + kx] = got[C * kx : C * kx + C, :]


def wgrad_out(split, inner, grad, outs):
    for ky in range(3):
        got = wgrad(inner, grad, ky)
        got = jnp.concatenate([got[:, C * kx : C * kx + C].T for kx in range(3)], axis=0)
        (split_out if split else plain_out)(ky, got, *outs)


def wgrad_two_kernel(split, inner, grad, *outs):
    wgrad_out(split, inner, lambda row: grad[row], outs)


def output_kernel(count, x, pre_two, sums_in, vec_in, out):
    vec = vec_rows(vec_in)
    means, inverses, _, _ = second_stats(sums_in, count)
    gains = [inverses[m] * vec[4] for m in range(MB)]
    shifts = [vec[5] - means[m] * gains[m] for m in range(MB)]

    @pl.loop(0, R)
    def _(row):
        source = own_row(row)
        for s in range(S):
            value = act(pre_two[row, 16 * s : 16 * s + 16, :])
            out[s, source] = (x[s, source].astype(F32) + value * gains[s // PER] + shifts[s // PER]).astype(BF16)


def first_back_stats(first_in, sums_in, count):
    means, inverses = norm_of(taken(first_in, 2 * MB), count)
    rows = taken(sums_in, 2 * MB + 1)
    dshift = rows[:MB]
    dgain = [inverses[m] * (rows[MB + m] - means[m] * dshift[m]) for m in range(MB)]
    return means, inverses, dgain, dshift, rows[2 * MB]


def back_one_kernel(split, count, pre, mid, first_in, sums_in, x_all, vec, g_inner, bias, *rest):
    outs, flats = rest[:-2], rest[-2:]
    means, inverses, dgain, dshift, _ = first_back_stats(first_in, sums_in, count)
    terms = back_terms(means, inverses, vec[1:2, :], dgain, dshift, count)
    for flat in flats:
        flat[...] = jnp.zeros(flat.shape, F32)
    g_inner[0, 0] = jnp.zeros((TI, W3), BF16)

    def body(i, total):
        for odd in range(2):
            place = place_of(i, odd)
            build_back(flats[odd], g_inner, place, pre, mid, 2 * i + odd, terms)
            total = total + fold(g_inner[place + (slice(None), slice(C, 2 * C))].astype(F32))
        return total

    total = lax.fori_loop(0, R // 2, body, jnp.zeros((8, C), F32))
    build_back(flats[0], g_inner, place_of(R // 2, 0), pre, mid, R, terms)
    bias[...] = jnp.concatenate([down(total), jnp.zeros((7, C), F32)], axis=0)
    wgrad_out(split, x_all, lambda row: g_inner[(row + 1) // 2, (row + 1) % 2, :, C : 2 * C], outs)


def input_grad_kernel(g_inner, dn, block, out):
    for row, v in enumerate(conv_rows(g_inner, 0, R // 2, block[...], TI)):
        source = own_row(row)
        value = v + dn[row, :TI, :]
        for n in range(S):
            out[n, source] = value[16 * n : 16 * n + 16].astype(BF16)


def merge_kernel(keep_one, got_one, keep_two, got_two, out):
    for n in range(out.shape[0]):
        out[n] = jnp.concatenate(
            [keep_one[n] + got_one[n], keep_two[n] + got_two[n], jnp.zeros((8, C), F32)], axis=0
        ).astype(BF16)


def owned_kernel(parts, bias, chunk, sums):
    total = parts[0].astype(F32)
    for n in range(1, parts.shape[0]):
        total = total + parts[n].astype(F32)
    own = total[:72]
    chunk[...] = jnp.broadcast_to(own[None], chunk.shape)
    put_all(sums, [down(fold(own * own)), bias[0:1, :]])


def adam(weight, first, second, grad, rate, decay):
    first_new = BETA_ONE * first + (1.0 - BETA_ONE) * grad
    second_new = BETA_TWO * second + (1.0 - BETA_TWO) * grad * grad
    first_hat = first_new * (1.0 / (1.0 - BETA_ONE**STEP))
    second_hat = second_new * (1.0 / (1.0 - BETA_TWO**STEP))
    weight_new = weight - rate * (first_hat / (jnp.sqrt(second_hat) + ADAM_EPS) + decay * weight)
    return weight_new, first_new, second_new


def vector_grads(first_in, second_in, third_in, bias_one, count):
    _, _, dgain_two, dshift_two = second_stats(second_in, count)
    _, _, dgain_one, dshift_one, bias_two = first_back_stats(first_in, third_in, count)
    rows = [bias_one, sum(dgain_one), sum(dshift_one), bias_two, sum(dgain_two), sum(dshift_two)]
    return jnp.concatenate(rows, axis=0)


def update_kernel(
    count,
    chunks,
    sums_in,
    first_in,
    second_in,
    third_in,
    weight,
    first,
    second,
    vectors,
    vec_first,
    vec_second,
    norm_out,
    weight_new,
    first_new,
    second_new,
    weight_low,
    vectors_new,
    vec_first_new,
    vec_second_new,
    grad,
):
    total = jnp.sum(sums_in[...], axis=0)
    vec_grad = vector_grads(first_in, second_in, third_in, total[1:2], count)
    square = jnp.sum(total[0:1], axis=1, keepdims=True) + jnp.sum(
        down(vec_grad * vec_grad), axis=1, keepdims=True
    )
    norm = jnp.sqrt(square)
    norm_out[...] = norm
    clip = jnp.minimum(1.0, CLIP / (norm + 1e-06))
    for k in range(2):
        for n in range(8):
            for t in range(9):
                part = chunks[n, 36 * k + 4 * t : 36 * k + 4 * t + 4, :]
                grad[k, pl.ds(36 * n + t, 4, stride=9), :] = part
        new = adam(weight[k], first[k], second[k], grad[k] * clip, RATE_CONV, DECAY_CONV)
        weight_new[k], first_new[k], second_new[k] = new
        weight_low[k] = new[0].astype(BF16)
    width = vectors.shape[1]
    turned = pltpu.roll(
        jnp.concatenate([vec_grad, jnp.zeros((2, C), F32)], axis=0),
        lax.rem(C - lax.axis_index("dp") * width, C),
        axis=1,
    )
    new = adam(vectors[...], vec_first[...], vec_second[...], turned[:6, :width] * clip, RATE_VEC, 0.0)
    vectors_new[...], vec_first_new[...], vec_second_new[...] = new


def spread(block, axes):
    return lax.all_to_all(block, axes, 0, 0, tiled=True)


def turn(block, axis, by):
    size = lax.axis_size(axis)
    return lax.ppermute(block, axis, [(i, (i + by) % size) for i in range(size)])


def body(inputs, lead_time, cotangent, conv_weight, conv_first, conv_second, vectors, vec_first, vec_second):
    devices = lax.axis_size("dp") * lax.axis_size("lat") * lax.axis_size("lon")
    groups = lax.axis_size("dp")
    split = groups == 4 and lax.axis_size("lon") == 4
    count = float(PER * R * R * devices)
    size = conv_weight.shape[1] // 9
    flats = [pltpu.VMEM((FLAT, C), F32)] * 2
    conv_flops = 2 * T * 12 * C * 2 * C

    m1, m2, lat_out = call(
        prep_kernel,
        [((9 * size + 16, C), BF16), ((9 * size, C), BF16), ((6, S, R, C), BF16)],
        (inputs, cotangent, conv_weight, vectors),
    )
    lat_in = turn(lat_out, "lat", 1)

    def gathered(block):
        if split:
            return [block] + [turn(block, "dp", k) for k in range(1, groups)]
        whole = lax.all_gather(block, "dp")
        taps = whole[:, : 9 * size].reshape(groups, 9, size, C).transpose(1, 0, 2, 3).reshape(9 * C, C)
        if block.shape[0] == 9 * size:
            return [taps]
        return [jnp.concatenate([taps, jnp.sum(whole[:, 9 * size :], axis=0)], axis=0)]

    w1 = gathered(m1)
    x_r, x_l, c_r, c_l = call(
        edge_kernel,
        [((R + 4, MB, 16, C), BF16)] * 2 + [((R + 2, MB, 16, C), BF16)] * 2,
        (inputs, cotangent, lat_in),
    )
    x_left, x_right = turn(x_r, "lon", 1), turn(x_l, "lon", -1)
    w2 = gathered(m2)
    c_left, c_right = turn(c_r, "lon", 1), turn(c_l, "lon", -1)
    (x_all,) = call(
        shift_kernel, [((11, 2, T, W3), BF16)], (inputs, lat_in, x_left, x_right), flats, flops=10**8
    )
    block_one, vec = call(block_kernel, [((12 * C, 2 * C), BF16), ((16, C), F32)], w1, flops=10**8)
    pre_one, sums_one = call(
        first_kernel,
        [((R + 4, T, C), F32), ((devices, 8, C), F32)],
        (x_all, block_one, vec),
        flops=conv_flops * 10,
    )
    dn, dn_sums = call(
        lead_kernel,
        [((R + 2, T, C), F32), ((8, C), F32)],
        (lead_time, cotangent, lat_in, c_left, c_right),
        flats,
        flops=10**8,
        scalars=1,
    )
    block_two, two_back, one_back = call(
        weight_kernel, [((12 * C, 2 * C), BF16)] * 3, (block_one, *w2), flops=10**8
    )
    sums_one, dn, block_two = lax.optimization_barrier((sums_one, dn, block_two))
    got_one = spread(sums_one, ALL)
    n_all, pre_two, sums_two = call(
        lambda *refs: second_kernel(count, *refs),
        [((10, 2, T, W3), BF16), ((R + 2, T, C), F32), ((devices, 3, 4, C), F32)],
        (pre_one, got_one, dn, dn_sums, block_two, vec),
        flats,
        flops=conv_flops * 9,
    )
    got_two = spread(sums_two, ALL)
    grad_two, mid, sums_three = call(
        lambda *refs: back_two_kernel(count, *refs),
        [((R, TI, C), BF16), ((R + 2, T, C), F32), ((devices, 8, C), F32)],
        (pre_two, dn, got_two, pre_one, two_back, vec),
        [pltpu.VMEM((10, 2, T, W3), BF16)] + flats,
        flops=conv_flops * 9,
    )
    got_three = spread(sums_three, ALL)
    got_three, n_all, pre_two, dn = lax.optimization_barrier((got_three, n_all, pre_two, dn))
    grad_kinds = [((16, 36, C), F32)] * 2 if split else [((9, C, C), F32)]
    two_out = call(
        lambda *refs: wgrad_two_kernel(split, *refs), grad_kinds, (n_all, grad_two), flops=conv_flops * 8
    )
    g_inner, bias_one, *one_out = call(
        lambda *refs: back_one_kernel(split, count, *refs),
        [((9, 2, TI, W3), BF16), ((8, C), F32)] + grad_kinds,
        (pre_one, mid, got_one, got_three, x_all, vec),
        flats,
        flops=conv_flops * 9,
    )
    (outputs,) = call(
        lambda *refs: output_kernel(count, *refs),
        [((S, R, R, C), BF16)],
        (inputs, pre_two, got_two, vec),
        flops=10**8,
    )
    (grad_inputs,) = call(
        input_grad_kernel,
        [((S, R, R, C), BF16)],
        (g_inner, dn, one_back),
        flops=conv_flops * 6,
    )
    if split:
        lat_one, lat_two = turn(one_out[1], "lat", 1), turn(two_out[1], "lat", 1)
        (merged,) = call(merge_kernel, [((16, 80, C), BF16)], (one_out[0], lat_one, two_out[0], lat_two))
        parts = spread(merged, ("dp", "lon"))
        chunk, sums_four = call(
            owned_kernel, [((8, 72, C), F32), ((devices, 2, C), F32)], (parts, bias_one)
        )
        got_four = spread(sums_four, ALL)
        chunks = spread(chunk, ("lat", "lon"))
        kinds = [((1, 1), F32)] + [(conv_weight.shape, F32)] * 3 + [(conv_weight.shape, BF16)]
        norm, *news = call(
            lambda *refs: update_kernel(count, *refs),
            kinds + [(vectors.shape, F32)] * 3,
            (
                chunks,
                got_four,
                got_one,
                got_two,
                got_three,
                conv_weight,
                conv_first,
                conv_second,
                vectors,
                vec_first,
                vec_second,
            ),
            [pltpu.VMEM(conv_weight.shape, F32)],
        )
        return (outputs, grad_inputs, norm.reshape(()), *news)
    stacked = jnp.stack([one_out[0], two_out[0]]).transpose(0, 2, 1, 3).reshape(2, 9 * C, C)
    conv_total, bias_total = lax.psum((stacked, bias_one[0:1]), ALL)
    vec_total = vector_grads(got_one, got_two, got_three, bias_total, count)
    grad_norm = jnp.sqrt(jnp.sum(conv_total * conv_total) + jnp.sum(vec_total * vec_total))
    clip = jnp.minimum(1.0, CLIP / (grad_norm + 1e-06))
    index = lax.axis_index("dp")
    conv_own = lax.dynamic_slice_in_dim(conv_total, index * conv_weight.shape[1], conv_weight.shape[1], 1)
    vec_own = lax.dynamic_slice_in_dim(vec_total, index * vectors.shape[1], vectors.shape[1], 1)
    conv_news = adam(conv_weight, conv_first, conv_second, conv_own * clip, RATE_CONV, DECAY_CONV)
    vec_news = adam(vectors, vec_first, vec_second, vec_own * clip, RATE_VEC, 0.0)
    return (outputs, grad_inputs, grad_norm, *conv_news, conv_news[0].astype(BF16), *vec_news)


def solution(mesh):
    grid = P("dp", "lat", "lon", None)
    rows = P(None, "dp", None)
    columns = P(None, "dp")
    in_specs = (grid, P("dp"), grid, rows, rows, rows, columns, columns, columns)
    out_specs = (grid, grid, P(), rows, rows, rows, rows, columns, columns, columns)
    return jax.shard_map(body, mesh=mesh, in_specs=in_specs, out_specs=out_specs, check_vma=False)
```

```python
import math

import jax
import jax.numpy as jnp
from jax import lax
from jax.experimental import pallas as pl
from jax.experimental.pallas import tpu as pltpu
from jax.sharding import PartitionSpec as P

MB = 3
STEP = 5
EPS = 1e-05
CLIP = 1.0
BETA_ONE = 0.5
BETA_TWO = 0.5
RATE_CONV = 0.03
RATE_VEC = 0.3
DECAY_CONV = 0.01
ADAM_EPS = 1e-08
ALL = ("dp", "lat", "lon")
F32 = jnp.float32
BF16 = jnp.bfloat16
GELU_A = math.sqrt(2.0 / math.pi)
GELU_B = GELU_A * 0.044715

S, R, C = 12, 16, 128
TI = S * R
NH = S + 1
TH = 8 * (NH + NH % 2)
T = TI + TH
W3 = 3 * C
PER = S // MB
FLAT = 24 + 24 * S
VM = pl.BlockSpec(memory_space=pltpu.VMEM)
SM = pl.BlockSpec(memory_space=pltpu.SMEM)
FAR = pl.BlockSpec(memory_space=pltpu.HBM)


def call(kernel, outs, args, scratch=(), flops=0, limit=16, scalars=0, far=0, far_out=(), aliases=None):
    args = [
        pltpu.with_memory_space_constraint(arg, pltpu.HBM) if scalars <= n < scalars + far else arg
        for n, arg in enumerate(args)
    ]
    spaces = [SM] * scalars + [FAR] * far + [VM] * (len(args) - scalars - far)
    return pl.pallas_call(
        kernel,
        out_shape=tuple(
            pltpu.HBM(shape, kind) if n in far_out else jax.ShapeDtypeStruct(shape, kind)
            for n, (shape, kind) in enumerate(outs)
        ),
        in_specs=spaces,
        out_specs=tuple(FAR if n in far_out else VM for n in range(len(outs))),
        scratch_shapes=list(scratch),
        input_output_aliases=aliases or {},
        compiler_params=pltpu.CompilerParams(vmem_limit_bytes=limit << 20),
        cost_estimate=pl.CostEstimate(
            flops=flops,
            transcendentals=0,
            bytes_accessed=sum(math.prod(a.shape) * a.dtype.itemsize for a in args),
        ),
    )(*args)


def own_row(row):
    return jnp.where(lax.axis_index("lat") == 0, row, R - 1 - row)


def own_tap(tap):
    return jnp.where(lax.axis_index("lat") == 0, tap, 2 - tap)


def act(v):
    return 0.5 * v * (1.0 + jnp.tanh(v * (GELU_A + GELU_B * (v * v))))


def act_both(v):
    sq = v * v
    tan = jnp.tanh(v * (GELU_A + GELU_B * sq))
    half = 0.5 * (1.0 + tan)
    value = v * half
    slope = half + value * (1.0 - tan) * (GELU_A + (3.0 * GELU_B) * sq)
    return value, slope


def fold(v):
    return jnp.sum(v.reshape(v.shape[0] // 8, 8, C), axis=0)


def down(v):
    return jnp.sum(v, axis=0, keepdims=True)


def batch_sums(values):
    return [fold(values[PER * R * m : PER * R * (m + 1)]) for m in range(MB)]


def build(flat, out, place, tile, side):
    for n in range(S):
        value = tile(n)
        flat[16 + 24 * n : 32 + 24 * n, :] = value
        out[place + (slice(16 * n, 16 * n + 16), slice(C, 2 * C))] = value.astype(BF16)
    whole = out.shape[-2] == T
    for p in range(TH // 16):
        pair = [side(h) if h < NH else jnp.zeros((8, C), F32) for h in (2 * p, 2 * p + 1)]
        for h, value in zip((2 * p, 2 * p + 1), pair):
            if h < NH:
                flat[8 + 24 * h : 16 + 24 * h, :] = value
        if whole:
            at = TI + 16 * p
            out[place + (slice(at, at + 16), slice(C, 2 * C))] = jnp.concatenate(pair, axis=0).astype(BF16)
    emit_sides(flat, out, place)


def emit_sides(flat, out, place):
    for kx in (0, 2):
        columns = slice(C * kx, C * kx + C)
        for n in range(S):
            at = 15 + 24 * n + kx
            out[place + (slice(16 * n, 16 * n + 16), columns)] = flat[at : at + 16, :].astype(BF16)
        if out.shape[-2] != T:
            continue
        for p in range(TH // 16):
            at = 7 + 48 * p + kx
            first = flat[at : at + 8, :]
            second = flat[at + 24 : at + 32, :] if 2 * p + 1 < NH else jnp.zeros((8, C), F32)
            out[place + (slice(TI + 16 * p, TI + 16 * p + 16), columns)] = jnp.concatenate(
                [first, second], axis=0
            ).astype(BF16)


def place_of(i, odd):
    return (i + odd, 1 - odd)


def sided(rows):
    mixed = {}
    for h in range(NH):
        low, high = max(h - 1, 0) // PER, min(h, S - 1) // PER
        if low != high:
            mixed[h] = jnp.concatenate(
                [jnp.broadcast_to(rows[low], (4, C)), jnp.broadcast_to(rows[high], (4, C))], axis=0
            )
    return (
        lambda n: rows[n // PER],
        lambda h: mixed[h] if h in mixed else rows[min(h, S - 1) // PER],
    )


def put_all(ref, rows):
    block = jnp.concatenate(rows, axis=0)
    ref[...] = jnp.broadcast_to(block[None], ref.shape)


def taken(ref, count):
    return [ref[i : i + 1, :] for i in range(count)]


def vec_rows(ref):
    return [ref[i : i + 1, :] for i in range(6)]


def norm_of(sums, count):
    means = [sums[m] * (1.0 / count) for m in range(MB)]
    inverses = [lax.rsqrt(sums[MB + m] * (1.0 / count) - means[m] * means[m] + EPS) for m in range(MB)]
    return means, inverses


def piece_of(pieces, k, which, rows):
    if k == 0:
        return pieces[0][which, rows, :]
    mine, other = pieces[2 * k - 1], pieces[2 * k]
    return jnp.where(lax.axis_index("lat") == which, mine[rows, :], other[rows, :])


def fill_forward(block, pieces, which):
    count = (len(pieces) + 1) // 2
    size = C // count
    zero = jnp.zeros((C, C), BF16)
    for kx in range(3):
        block[C * kx : C * kx + C, C:] = zero
        block[C * (9 + kx) : C * (10 + kx), :C] = zero
        for ky in range(3):
            source = pl.multiple_of((3 * own_tap(ky) + kx) * size, size)
            for k in range(count):
                owner = lax.rem(lax.axis_index("dp") + (count - k), count) if count > 1 else 0
                part = piece_of(pieces, k, which, pl.ds(source, size))
                for a in range(2):
                    top = pl.multiple_of((3 * (ky + a) + kx) * C + owner * size, size)
                    block[pl.ds(top, size), a * C : a * C + C] = part


def fill_backward(block, forward):
    zero = jnp.zeros((C, C), BF16)
    for kx in range(3):
        block[C * kx : C * kx + C, C:] = zero
        block[C * (9 + kx) : C * (10 + kx), :C] = zero
        for ky in range(3):
            source = (3 * (2 - ky) + 2 - kx) * C
            part = forward[source : source + C, :C].T
            for a in range(2):
                top = (3 * (ky + a) + kx) * C
                block[top : top + C, a * C : a * C + C] = part


def conv_rows(ref, low, high, weight, rows=T):
    pairs = [
        jnp.concatenate([ref[i, 0, :rows], ref[i, 1, :rows], ref[i + 1, 0, :rows], ref[i + 1, 1, :rows]], axis=1)
        for i in range(low, high)
    ]
    got = jnp.dot(jnp.concatenate(pairs, axis=0), weight, preferred_element_type=F32)
    return [
        got[n * rows : n * rows + rows, a * C : a * C + C] for n in range(high - low) for a in range(2)
    ]


def added(total, new):
    return new if total is None else [old + more for old, more in zip(total, new)]


def pack_taps(weight, out):
    size = weight.shape[0] // 9
    for t in range(9):
        out[size * t : size * t + size, :] = weight[pl.ds(t, size, stride=9), :].astype(BF16)


def prep_kernel(x, cot, weight, vectors, packed, lat_out, x_near, cot_near, held, held_vec, sems):
    last = lax.axis_index("lat") == 0
    copies = [
        pltpu.make_async_copy(weight, held, sems.at[0]),
        pltpu.make_async_copy(vectors, held_vec, sems.at[1]),
        pltpu.make_async_copy(x.at[:, pl.ds(jnp.where(last, R - 4, 0), 4)], lat_out.at[:, 0:4], sems.at[2]),
        pltpu.make_async_copy(cot.at[:, pl.ds(jnp.where(last, R - 2, 0), 2)], lat_out.at[:, 4:6], sems.at[3]),
        pltpu.make_async_copy(x, x_near, sems.at[4]),
        pltpu.make_async_copy(cot, cot_near, sems.at[5]),
    ]
    for copy in copies:
        copy.start()
    for copy in copies[:2]:
        copy.wait()
    size = 9 * (weight.shape[1] // 9)
    width = vectors.shape[1]
    pick = lax.broadcasted_iota(jnp.int32, (width, C), 1) - lax.axis_index("dp") * width
    pick = jnp.where(pick == lax.broadcasted_iota(jnp.int32, (width, C), 0), 1.0, 0.0).astype(BF16)
    placed = jnp.dot(held_vec[...].astype(BF16), pick, preferred_element_type=F32)
    for k in range(2):
        pack_taps(held.at[k], packed.at[k])
        packed[k, size:, :] = jnp.concatenate([placed, jnp.zeros((10, C), F32)], axis=0).astype(BF16)
    for copy in copies[2:]:
        copy.wait()


def x_beyond(lat_in, n, k):
    return lat_in[n, jnp.where(lax.axis_index("lat") == 0, k, 3 - k)]


def cot_beyond(lat_in, n, k):
    return lat_in[n, jnp.where(lax.axis_index("lat") == 0, 4 + k, 5 - k)]


def cut_far(tile, far_r, far_l, at, columns, rows):
    for m in range(MB):
        tiles = [tile(q, n).astype(F32) for q in range(rows) for n in range(PER * m, PER * m + PER)]
        far_r[at, m] = jnp.concatenate([v[R - columns :] for v in tiles], axis=0).astype(BF16)
        far_l[at, m] = jnp.concatenate([v[:columns] for v in tiles], axis=0).astype(BF16)


def edge_kernel(x, far_r, far_l):
    @pl.loop(0, R // 2)
    def _(i):
        for q in range(2):
            cut_far(lambda _, n: x[n, own_row(2 * i + q)], far_r, far_l, 2 * i + q, 4, 1)


def beyond_kernel(lat_in, packed, right_in, left_in, mine, far_r, far_l):
    for k in range(4):
        cut_far(lambda _, n: x_beyond(lat_in, n, k), far_r, far_l, R + k, 4, 1)
    mine[...] = packed[lax.axis_index("lat")]


def later_kernel(after, cot, lat_in, far_r, far_l):
    @pl.loop(0, R // 2)
    def _(i):
        cut_far(lambda q, n: cot[n, own_row(2 * i + q)], far_r, far_l, i, 2, 2)

    cut_far(lambda q, n: cot_beyond(lat_in, n, q), far_r, far_l, R // 2, 2, 2)


def shift_kernel(x, lat_in, from_left, from_right, out, *flats):
    for edge in (0, R + 5):
        out[edge // 2, edge % 2] = jnp.zeros((TI, W3), BF16)

    def one(flat, tile, at, place):
        for m in range(MB):
            left, right = from_left[at, m].astype(F32), from_right[at, m].astype(F32)
            for n in range(PER):
                s = PER * m + n
                flat[15 + 24 * s : 16 + 24 * s, :] = left[4 * n + 3 : 4 * n + 4]
                flat[32 + 24 * s : 33 + 24 * s, :] = right[4 * n : 4 * n + 1]
        for n in range(S):
            value = tile(n)
            flat[16 + 24 * n : 32 + 24 * n, :] = value.astype(F32)
            out[place + (slice(16 * n, 16 * n + 16), slice(C, 2 * C))] = value
        emit_sides(flat, out, place)

    @pl.loop(0, R // 2)
    def _(i):
        for odd in range(2):
            source = own_row(2 * i + odd)
            one(flats[odd], lambda n: x[n, source], 2 * i + odd, place_of(i, odd))

    for k in range(4):
        one(flats[k % 2], lambda n: x_beyond(lat_in, n, k), R + k, place_of((R + k) // 2, k % 2))


def halo_kernel(after, x, lat_in, from_left, from_right, block, vec, pre, halo, *flats):
    for flat in flats:
        flat[...] = jnp.zeros(flat.shape, F32)
    for edge in (0, R + 5):
        halo[edge // 2, edge % 2] = jnp.zeros((TH, W3), BF16)

    def one(flat, tile, row, place):
        for m in range(MB):
            left, right = from_left[row, m].astype(F32), from_right[row, m].astype(F32)
            for n in range(PER):
                s = PER * m + n
                value = tile(s).astype(F32)
                flat[12 + 24 * s : 16 + 24 * s, :] = left[4 * n : 4 * n + 4]
                flat[16 + 24 * s : 24 + 24 * s, :] = value[:8]
                flat[24 + 24 * s : 32 + 24 * s, :] = value[8:]
                flat[32 + 24 * s : 36 + 24 * s, :] = right[4 * n : 4 * n + 4]
        for kx in range(3):
            for p in range(TH // 16):
                at = 7 + 48 * p + kx
                second = flat[at + 24 : at + 32, :] if 2 * p + 1 < NH else jnp.zeros((8, C), F32)
                halo[place + (slice(16 * p, 16 * p + 16), slice(C * kx, C * kx + C))] = jnp.concatenate(
                    [flat[at : at + 8, :], second], axis=0
                ).astype(BF16)

    @pl.loop(0, R // 2)
    def _(i):
        for odd in range(2):
            source = own_row(2 * i + odd)
            one(flats[odd], lambda n: x[n, source], 2 * i + odd, place_of(i, odd))

    for k in range(4):
        one(flats[k % 2], lambda n: x_beyond(lat_in, n, k), R + k, place_of((R + k) // 2, k % 2))
    for row, v in enumerate(conv_rows(halo, 0, R // 2 + 2, block[...], TH)):
        pre[row] = v + vec[0:1, :]


def lead_scales(lead):
    return [0.5 * jnp.sqrt(jnp.full((1, C), lead[n], jnp.int32).astype(F32)) for n in range(S)]


def lead_kernel(lead, cot, dn, sums):
    scale = lead_scales(lead)

    def body(i, total):
        for odd in range(2):
            row = 2 * i + odd
            source = own_row(row)
            values = [cot[n, source].astype(F32) * scale[n] for n in range(S)]
            for n in range(S):
                dn[row, 16 * n : 16 * n + 16, :] = values[n]
            new = [sum(fold(values[n]) for n in range(PER * m, PER * m + PER)) for m in range(MB)]
            total = added(total, new)
        return total

    total = lax.fori_loop(0, R // 2, body, [jnp.zeros((8, C), F32)] * MB)
    sums[...] = jnp.concatenate([down(v) for v in total] + [jnp.zeros((8 - MB, C), F32)], axis=0)


def lead_side_kernel(lead, after, lat_in, from_left, from_right, lat, side, *flats):
    scale = lead_scales(lead)
    for flat in flats:
        flat[...] = jnp.zeros(flat.shape, F32)
    for k in range(2):
        for n in range(S):
            lat[k, 16 * n : 16 * n + 16, :] = cot_beyond(lat_in, n, k).astype(F32) * scale[n]

    @pl.loop(0, R // 2 + 1)
    def _(i):
        for m in range(MB):
            left = from_left[i, m].astype(F32)
            right = from_right[i, m].astype(F32)
            for odd in range(2):
                for n in range(PER):
                    s, at = PER * m + n, 8 * odd + 2 * n
                    flats[odd][14 + 24 * s : 16 + 24 * s, :] = left[at : at + 2] * scale[s]
                    flats[odd][32 + 24 * s : 34 + 24 * s, :] = right[at : at + 2] * scale[s]
        for odd in range(2):
            row = 2 * i + odd
            flat = flats[odd]
            for h in range(NH):
                side[row, 8 * h : 8 * h + 8, :] = flat[8 + 24 * h : 16 + 24 * h, :]
            side[row, 8 * NH :, :] = jnp.zeros((TH - 8 * NH, C), F32)


def block_kernel(*rest):
    pieces, (block, vec) = rest[:-2], rest[-2:]
    fill_forward(block, pieces, 0)
    last = pieces[0].shape[1]
    vec[...] = sum(
        piece_of(pieces, k, 0, slice(last - 16, last)).astype(F32) for k in range((len(pieces) + 1) // 2)
    )


def weight_kernel(after, block_one, *rest):
    pieces, (block_two, two_back, one_far, one_back, sem) = rest[:-5], rest[-5:]
    fill_backward(one_back, block_one)
    copy = pltpu.make_async_copy(one_back, one_far, sem)
    copy.start()
    fill_forward(block_two, pieces, 1)
    fill_backward(two_back, block_two)
    copy.wait()


def first_kernel(x_all, block, vec, pre, sums):
    bias = vec[0:1, :]
    total = None
    for low, high in ((0, 4), (4, 8), (8, 10)):
        for n, v in enumerate(conv_rows(x_all, low, high, block[...], TI)):
            row = 2 * low + n
            pre[row] = v + bias
            if row < R:
                value = act(v + bias)
                total = added(total, batch_sums(value) + batch_sums(value * value))
    put_all(sums, [down(v) for v in total] + [jnp.zeros((2, C), F32)])


def second_kernel(count, pre, pre_side, sums_in, dn, dn_sums, block, vec_in, n_all, pre_two, sums, kept, *flats):
    vec = vec_rows(vec_in)
    kept[...] = jnp.sum(sums_in[...], axis=0)
    means, inverses = norm_of(taken(kept, 2 * MB), count)
    gains = [inverses[m] * vec[1] for m in range(MB)]
    gain, gain_side = sided(gains)
    shift, shift_side = sided([vec[2] - means[m] * gains[m] for m in range(MB)])
    for flat in flats:
        flat[...] = jnp.zeros(flat.shape, F32)
    n_all[0, 0] = jnp.zeros((T, W3), BF16)

    def one(i, odd):
        row = 2 * i + odd
        build(
            flats[odd],
            n_all,
            place_of(i, odd),
            lambda n: act(pre[row, 16 * n : 16 * n + 16, :]) * gain(n) + shift(n),
            lambda h: act(pre_side[row, 8 * h : 8 * h + 8, :]) * gain_side(h) + shift_side(h),
        )

    @pl.loop(0, R // 2 + 1)
    def _(i):
        for odd in range(2):
            one(i, odd)

    one(R // 2 + 1, 0)
    total = None
    for low, high in ((0, 5), (5, 9)):
        for n, v in enumerate(conv_rows(n_all, low, high, block[...])):
            row = 2 * low + n
            pre_two[row] = v + vec[3]
            if row < R:
                value = act(v[:TI] + vec[3])
                new = batch_sums(value) + batch_sums(value * value) + batch_sums(value * dn[row])
                total = added(total, new)
    block_out = jnp.concatenate([down(v) for v in total] + [dn_sums[0:MB, :]], axis=0)
    for g in range(3):
        part = block_out[4 * g : 4 * g + 4]
        for n in range(sums.shape[0]):
            sums[n, g] = part


def second_stats(sums_in, count):
    rows = taken(sums_in, 4 * MB)
    means, inverses = norm_of(rows[: 2 * MB], count)
    dots, plain = rows[2 * MB : 3 * MB], rows[3 * MB :]
    dgain = [inverses[m] * (dots[m] - means[m] * plain[m]) for m in range(MB)]
    return means, inverses, dgain, plain


def back_terms(means, inverses, gain, dgain, dshift, count):
    lin = [inverses[m] * gain for m in range(MB)]
    slope = [-lin[m] * inverses[m] * (dgain[m] * (1.0 / count)) for m in range(MB)]
    const = [-lin[m] * (dshift[m] * (1.0 / count)) - slope[m] * means[m] for m in range(MB)]
    return [sided(rows) for rows in (lin, const, slope)]


def build_back(flat, out, place, terms, pre_tile, tile, pre_side, side):
    def at(pre, incoming, which, index):
        value, deriv = act_both(pre(index))
        lin, const, slope = [term[which](index) for term in terms]
        return deriv * (lin * incoming(index) + const + slope * value)

    build(flat, out, place, lambda n: at(pre_tile, tile, 0, n), lambda h: at(pre_side, side, 1, h))


def back_two_kernel(
    count, pre_two, dn, dn_lat, dn_side, sums_in, pre, block, vec, grad, mid, sums, kept, g_all, *flats
):
    total = jnp.sum(sums_in[...], axis=0)
    kept[...] = jnp.concatenate([total[g, i : i + 1] for g in range(MB) for i in range(4)], axis=0)
    means, inverses, dgain, dshift = second_stats(kept, count)
    terms = back_terms(means, inverses, vec[4:5, :], dgain, dshift, count)
    for flat in flats:
        flat[...] = jnp.zeros(flat.shape, F32)
    for edge in (0, R + 3):
        g_all[edge // 2, edge % 2] = jnp.zeros((T, W3), BF16)

    def make(odd, place, row, inner, inner_row):
        build_back(
            flats[odd],
            g_all,
            place,
            terms,
            lambda n: pre_two[row, 16 * n : 16 * n + 16, :],
            lambda n: inner[inner_row, 16 * n : 16 * n + 16, :],
            lambda h: pre_two[row, TI + 8 * h : TI + 8 * h + 8, :],
            lambda h: dn_side[row, 8 * h : 8 * h + 8, :],
        )

    def body(i, total):
        for odd in range(2):
            place = place_of(i, odd)
            make(odd, place, 2 * i + odd, dn, 2 * i + odd)
            own = g_all[place + (slice(0, TI), slice(C, 2 * C))]
            grad[2 * i + odd] = own
            total = total + fold(own.astype(F32))
        return total

    bias = lax.fori_loop(0, R // 2, body, jnp.zeros((8, C), F32))
    for odd in range(2):
        make(odd, place_of(R // 2, odd), R + odd, dn_lat, odd)
    total = None
    for low, high in ((0, 5), (5, 9)):
        for n, v in enumerate(conv_rows(g_all, low, high, block[...])):
            row = 2 * low + n
            mid[row] = v
            if row < R:
                own = v[:TI]
                total = added(total, batch_sums(own) + batch_sums(own * act(pre[row])))
    put_all(sums, [down(v) for v in total] + [down(bias), jnp.zeros((1, C), F32)])


def wgrad_add(acc, inner, grad, low, high):
    left = jnp.concatenate([grad(row) for row in range(low, high)], axis=0)
    right = jnp.concatenate(
        [
            jnp.concatenate([inner[(row + ky) // 2, (row + ky) % 2, :TI] for ky in range(3)], axis=1)
            for row in range(low, high)
        ],
        axis=0,
    )
    part = lax.dot_general(left, right, (((0,), (0,)), ((), ())), preferred_element_type=F32)
    for ky in range(3):
        own = part[:, W3 * ky : W3 * ky + W3]
        acc[ky] = own if low == 0 else acc[ky] + own


def split_out(acc, which, keep, send):
    first = lax.axis_index("lat") == 0
    for ky in range(3):
        for kx in range(3):
            at = pl.ds(pl.multiple_of(144 * which + 16 * (3 * own_tap(ky) + kx), 16), 16)
            taps = acc[ky, :, C * kx : C * kx + C].T
            for d in range(4):
                low, high = taps[32 * d : 32 * d + 16], taps[32 * d + 16 : 32 * d + 32]
                keep[d, at, :] = jnp.where(first, low, high)
                send[d, at, :] = jnp.where(first, high, low).astype(BF16)


def plain_out(acc, which, out):
    for ky in range(3):
        for kx in range(3):
            out[which, 3 * own_tap(ky) + kx] = acc[ky, :, C * kx : C * kx + C].T


def output_kernel(count, after, x, pre_two, sums_in, vec_in, out):
    vec = vec_rows(vec_in)
    means, inverses, _, _ = second_stats(sums_in, count)
    gains = [inverses[m] * vec[4] for m in range(MB)]
    shifts = [vec[5] - means[m] * gains[m] for m in range(MB)]

    @pl.loop(0, R)
    def _(row):
        source = own_row(row)
        for s in range(S):
            value = act(pre_two[row, 16 * s : 16 * s + 16, :])
            out[s, source] = (x[s, source].astype(F32) + value * gains[s // PER] + shifts[s // PER]).astype(BF16)


def first_back_stats(first_in, sums_in, count):
    means, inverses = norm_of(taken(first_in, 2 * MB), count)
    rows = taken(sums_in, 2 * MB + 1)
    dshift = rows[:MB]
    dgain = [inverses[m] * (rows[MB + m] - means[m] * dshift[m]) for m in range(MB)]
    return means, inverses, dgain, dshift, rows[2 * MB]


def back_one_kernel(split, count, pre, pre_side, mid, first_in, sums_in, x_all, n_all, grad_two, vec, g_inner, bias, kept, *rest):
    outs, (acc_one, acc_two), flats = rest[:-4], rest[-4:-2], rest[-2:]
    kept[...] = jnp.sum(sums_in[...], axis=0)
    means, inverses, dgain, dshift, _ = first_back_stats(first_in, kept, count)
    terms = back_terms(means, inverses, vec[1:2, :], dgain, dshift, count)
    for flat in flats:
        flat[...] = jnp.zeros(flat.shape, F32)
    g_inner[0, 0] = jnp.zeros((TI, W3), BF16)

    def make(row):
        build_back(
            flats[row % 2],
            g_inner,
            ((row + 1) // 2, (row + 1) % 2),
            terms,
            lambda n: pre[row, 16 * n : 16 * n + 16, :],
            lambda n: mid[row, 16 * n : 16 * n + 16, :],
            lambda h: pre_side[row, 8 * h : 8 * h + 8, :],
            lambda h: mid[row, TI + 8 * h : TI + 8 * h + 8, :],
        )

    def made(row):
        return g_inner[(row + 1) // 2, (row + 1) % 2, :, C : 2 * C]

    total = jnp.zeros((8, C), F32)
    for n in range(4):
        for row in range(4 * n, 4 * n + 4):
            make(row)
            total = total + fold(made(row).astype(F32))
        wgrad_add(acc_two, n_all, lambda row: grad_two[row], 4 * n, 4 * n + 4)
        if n > 0:
            wgrad_add(acc_one, x_all, made, 4 * n - 4, 4 * n)
    make(R)
    wgrad_add(acc_one, x_all, made, R - 4, R)
    bias[...] = jnp.concatenate([down(total), jnp.zeros((7, C), F32)], axis=0)
    (split_out if split else plain_out)(acc_two, 1, *outs)
    (split_out if split else plain_out)(acc_one, 0, *outs)


def input_grad_kernel(lead, after, g_inner, cot, block, out):
    scale = lead_scales(lead)
    for row, v in enumerate(conv_rows(g_inner, 0, R // 2, block[...], TI)):
        source = own_row(row)
        for n in range(S):
            incoming = cot[n, source].astype(F32) * scale[n]
            out[n, source] = (v[16 * n : 16 * n + 16] + incoming).astype(BF16)


def merge_kernel(keep, got, out):
    for d in range(4):
        total = keep[d] + got[d].astype(F32)
        for n in range(4):
            parts = [total[144 * k + 36 * n : 144 * k + 36 * n + 36] for k in range(2)]
            out[4 * d + n] = jnp.concatenate(parts + [jnp.zeros((8, C), F32)], axis=0).astype(BF16)


def owned_kernel(outputs, grad_inputs, parts, bias, chunk, sums):
    total = parts[0].astype(F32)
    for n in range(1, parts.shape[0]):
        total = total + parts[n].astype(F32)
    own = total[:72]
    chunk[...] = total.astype(BF16)
    put_all(sums, [down(fold(own * own)), bias[0:1, :]])


def pair_kernel(own, other, out):
    first = lax.axis_index("lat") == 0
    mine, its = own[...].astype(F32), other[...].astype(F32)
    low, high = jnp.where(first, mine[:72], its[:72]), jnp.where(first, its[:72], mine[:72])
    out[...] = jnp.concatenate([low, high], axis=0).astype(BF16)


def fetch_kernel(*refs):
    far, near, sems = refs[:6], refs[7:13], refs[13]
    copies = [pltpu.make_async_copy(far[n], near[n], sems.at[n]) for n in range(6)]
    for copy in copies:
        copy.start()
    for copy in copies:
        copy.wait()


def adam(weight, first, second, grad, rate, decay):
    first_new = BETA_ONE * first + (1.0 - BETA_ONE) * grad
    second_new = BETA_TWO * second + (1.0 - BETA_TWO) * grad * grad
    first_hat = first_new * (1.0 / (1.0 - BETA_ONE**STEP))
    second_hat = second_new * (1.0 / (1.0 - BETA_TWO**STEP))
    weight_new = weight - rate * (first_hat / (jnp.sqrt(second_hat) + ADAM_EPS) + decay * weight)
    return weight_new, first_new, second_new


def vector_grads(first_in, second_in, third_in, bias_one, count):
    _, _, dgain_two, dshift_two = second_stats(second_in, count)
    _, _, dgain_one, dshift_one, bias_two = first_back_stats(first_in, third_in, count)
    rows = [bias_one, sum(dgain_one), sum(dshift_one), bias_two, sum(dgain_two), sum(dshift_two)]
    return jnp.concatenate(rows, axis=0)


def update_kernel(count, *refs):
    weight, first, second, vectors, vec_first, vec_second = refs[:6]
    chunks, (sums_in, first_in, second_in, third_in), refs = refs[6:10], refs[10:14], refs[14:]
    norm_out, weight_new, first_new, second_new, weight_low, vectors_new, vec_first_new, vec_second_new = refs[:8]
    slab, grad = refs[8:]
    total = jnp.sum(sums_in[...], axis=0)
    vec_grad = vector_grads(first_in, second_in, third_in, total[1:2], count)
    square = jnp.sum(total[0:1], axis=1, keepdims=True) + jnp.sum(
        down(vec_grad * vec_grad), axis=1, keepdims=True
    )
    norm = jnp.sqrt(square)
    norm_out[...] = norm
    clip = jnp.minimum(1.0, CLIP / (norm + 1e-06))
    for n, chunk in enumerate(chunks):
        at = pl.ds(36 * lax.rem(lax.axis_index("lon") + n, 4), 36)
        part = chunk[...].astype(F32)
        for lat in range(2):
            for k in range(2):
                slab[k, lat, at, :] = part[72 * lat + 36 * k : 72 * lat + 36 * k + 36]
    for k in range(2):
        for lat in range(2):
            for t in range(9):
                grad[k, pl.ds(144 * lat + t, 16, stride=9), :] = slab[k, lat, 16 * t : 16 * t + 16, :]
        new = adam(weight[k], first[k], second[k], grad[k] * clip, RATE_CONV, DECAY_CONV)
        weight_new[k], first_new[k], second_new[k] = new
        weight_low[k] = new[0].astype(BF16)
    width = vectors.shape[1]
    turned = pltpu.roll(
        jnp.concatenate([vec_grad, jnp.zeros((2, C), F32)], axis=0),
        lax.rem(C - lax.axis_index("dp") * width, C),
        axis=1,
    )
    new = adam(vectors[...], vec_first[...], vec_second[...], turned[:6, :width] * clip, RATE_VEC, 0.0)
    vectors_new[...], vec_first_new[...], vec_second_new[...] = new


def spread(block, axes):
    return lax.all_to_all(block, axes, 0, 0, tiled=True)


def turn(block, axis, by):
    size = lax.axis_size(axis)
    return lax.ppermute(block, axis, [(i, (i + by) % size) for i in range(size)])


def body(inputs, lead_time, cotangent, conv_weight, conv_first, conv_second, vectors, vec_first, vec_second):
    devices = lax.axis_size("dp") * lax.axis_size("lat") * lax.axis_size("lon")
    groups = lax.axis_size("dp")
    split = groups == 4 and lax.axis_size("lon") == 4
    count = float(PER * R * R * devices)
    size = conv_weight.shape[1] // 9
    flats = [pltpu.VMEM((FLAT, C), F32)] * 2
    conv_flops = 2 * T * 12 * C * 2 * C

    packed, lat_out, x_near, cot_near = call(
        prep_kernel,
        [
            ((2, 9 * size + 16, C), BF16),
            ((S, 6, R, C), BF16),
            (inputs.shape, BF16),
            (inputs.shape, BF16),
        ],
        (inputs, cotangent, conv_weight, vectors),
        [
            pltpu.VMEM(conv_weight.shape, F32),
            pltpu.VMEM(vectors.shape, F32),
            pltpu.SemaphoreType.DMA((6,)),
        ],
        far=4,
    )
    lat_in = turn(lat_out, "lat", 1)
    edge_kinds = [((R + 4, MB, 16, C), BF16)] * 2
    edges = call(edge_kernel, edge_kinds, (x_near,))
    mine, far_r, far_l = call(
        beyond_kernel,
        [((9 * size + 16, C), BF16)] + edge_kinds,
        (lat_in, packed, *edges),
        aliases={2: 1, 3: 2},
    )
    far_left, far_right = turn(far_r, "lon", 1), turn(far_l, "lon", -1)
    if split:
        pieces = [packed]
        for k in range(1, groups):
            fetched = turn(mine, "dp", k)
            pieces += [fetched, turn(fetched, "lat", 1)]
    else:
        whole = lax.all_gather(packed, "dp")
        taps = whole[:, :, : 9 * size].reshape(groups, 2, 9, size, C).transpose(1, 2, 0, 3, 4)
        tail = jnp.sum(whole[:, :, 9 * size :], axis=0)
        pieces = [jnp.concatenate([taps.reshape(2, 9 * C, C), tail], axis=1)]
    dn, dn_sums = call(
        lead_kernel, [((R, TI, C), F32), ((8, C), F32)], (lead_time, cot_near), flops=10**8, scalars=1
    )
    (x_all,) = call(
        shift_kernel, [((11, 2, TI, W3), BF16)], (x_near, lat_in, far_left, far_right), flats, flops=10**8
    )
    block_one, vec = call(block_kernel, [((12 * C, 2 * C), BF16), ((16, C), F32)], pieces, flops=10**8)
    pre_one, sums_one = call(
        first_kernel,
        [((R + 4, TI, C), F32), ((devices, 8, C), F32)],
        (x_all, block_one, vec),
        flops=conv_flops * 6,
    )
    sums_one, dn = lax.optimization_barrier((sums_one, dn))
    got_one = spread(sums_one, ALL)
    block_two, two_back, one_back = call(
        weight_kernel,
        [((12 * C, 2 * C), BF16)] * 3,
        (got_one, block_one, *pieces),
        [pltpu.VMEM((12 * C, 2 * C), BF16), pltpu.SemaphoreType.DMA(())],
        flops=10**8,
        far_out=(2,),
    )
    (pre_side,) = call(
        halo_kernel,
        [((R + 4, TH, C), F32)],
        (got_one, x_near, lat_in, far_left, far_right, block_one, vec),
        [pltpu.VMEM((11, 2, TH, W3), BF16)] + flats,
        flops=conv_flops * 4,
    )
    cot_r, cot_l = call(
        later_kernel, [((R // 2 + 1, MB, 16, C), BF16)] * 2, (got_one, cot_near, lat_in)
    )
    cot_left, cot_right = turn(cot_r, "lon", 1), turn(cot_l, "lon", -1)
    n_all, pre_two, sums_two, stat_one = call(
        lambda *refs: second_kernel(count, *refs),
        [((10, 2, T, W3), BF16), ((R + 2, T, C), F32), ((devices, 3, 4, C), F32), ((8, C), F32)],
        (pre_one, pre_side, got_one, dn, dn_sums, block_two, vec),
        flats,
        flops=conv_flops * 9,
    )
    dn_lat, dn_side = call(
        lead_side_kernel,
        [((2, TI, C), F32), ((R + 2, TH, C), F32)],
        (lead_time, sums_two, lat_in, cot_left, cot_right),
        flats,
        flops=10**8,
        scalars=1,
    )
    sums_two, dn_lat, dn_side = lax.optimization_barrier((sums_two, dn_lat, dn_side))
    got_two = spread(sums_two, ALL)
    grad_two, mid, sums_three, stat_two = call(
        lambda *refs: back_two_kernel(count, *refs),
        [((R, TI, C), BF16), ((R + 2, T, C), F32), ((devices, 8, C), F32), ((4 * MB, C), F32)],
        (pre_two, dn, dn_lat, dn_side, got_two, pre_one, two_back, vec),
        [pltpu.VMEM((10, 2, T, W3), BF16)] + flats,
        flops=conv_flops * 9,
    )
    got_three = spread(sums_three, ALL)
    grad_kinds = [((4, 288, C), F32), ((4, 288, C), BF16)] if split else [((2, 9, C, C), F32)]
    g_inner, bias_one, stat_three, *grads = call(
        lambda *refs: back_one_kernel(split, count, *refs),
        [((9, 2, TI, W3), BF16), ((8, C), F32), ((8, C), F32)] + grad_kinds,
        (pre_one, pre_side, mid, stat_one, got_three, x_all, n_all, grad_two, vec),
        [pltpu.VMEM((3, C, W3), F32)] * 2 + flats,
        flops=conv_flops * 9,
    )

    def finish(after):
        (outputs,) = call(
            lambda *refs: output_kernel(count, *refs),
            [((S, R, R, C), BF16)],
            (after, inputs, pre_two, stat_two, vec),
            flops=10**8,
        )
        (grad_inputs,) = call(
            input_grad_kernel,
            [((S, R, R, C), BF16)],
            (lead_time, after, g_inner, cotangent, one_back),
            flops=conv_flops * 6,
            scalars=1,
        )
        return outputs, grad_inputs

    if split:
        (merged,) = call(merge_kernel, [((16, 80, C), BF16)], (grads[0], turn(grads[1], "lat", 1)))
        parts = spread(merged, ("dp", "lon"))
        outputs, grad_inputs = finish(merged)
        chunk, sums_four = call(
            owned_kernel,
            [((80, C), BF16), ((devices, 2, C), F32)],
            (outputs, grad_inputs, parts, bias_one),
            far=2,
        )
        got_four = spread(sums_four, ALL)
        (pair,) = call(pair_kernel, [((144, C), BF16)], (chunk, turn(chunk, "lat", 1)), flops=10**10)
        chunks = [pair] + [turn(pair, "lon", -k) for k in range(1, 4)]
        kinds = [((1, 1), F32)] + [(conv_weight.shape, F32)] * 3 + [(conv_weight.shape, BF16)]
        moments = (conv_weight, conv_first, conv_second, vectors, vec_first, vec_second)
        moments = call(
            fetch_kernel,
            [(moment.shape, F32) for moment in moments],
            (*moments, pair),
            [pltpu.SemaphoreType.DMA((6,))],
            flops=10**10,
            far=6,
        )
        norm, *news = call(
            lambda *refs: update_kernel(count, *refs),
            kinds + [(vectors.shape, F32)] * 3,
            (*moments, *chunks, got_four, stat_one, stat_two, stat_three),
            [pltpu.VMEM((2, 2, 144, C), F32), pltpu.VMEM(conv_weight.shape, F32)],
        )
        return (outputs, grad_inputs, norm.reshape(()), *news)
    outputs, grad_inputs = finish(bias_one)
    stacked = grads[0].transpose(0, 2, 1, 3).reshape(2, 9 * C, C)
    conv_total, bias_total = lax.psum((stacked, bias_one[0:1]), ALL)
    vec_total = vector_grads(stat_one, stat_two, stat_three, bias_total, count)
    grad_norm = jnp.sqrt(jnp.sum(conv_total * conv_total) + jnp.sum(vec_total * vec_total))
    clip = jnp.minimum(1.0, CLIP / (grad_norm + 1e-06))
    index = lax.axis_index("dp")
    conv_own = lax.dynamic_slice_in_dim(conv_total, index * conv_weight.shape[1], conv_weight.shape[1], 1)
    vec_own = lax.dynamic_slice_in_dim(vec_total, index * vectors.shape[1], vectors.shape[1], 1)
    conv_news = adam(conv_weight, conv_first, conv_second, conv_own * clip, RATE_CONV, DECAY_CONV)
    vec_news = adam(vectors, vec_first, vec_second, vec_own * clip, RATE_VEC, 0.0)
    return (outputs, grad_inputs, grad_norm, *conv_news, conv_news[0].astype(BF16), *vec_news)


def solution(mesh):
    grid = P("dp", "lat", "lon", None)
    rows = P(None, "dp", None)
    columns = P(None, "dp")
    in_specs = (grid, P("dp"), grid, rows, rows, rows, columns, columns, columns)
    out_specs = (grid, grid, P(), rows, rows, rows, rows, columns, columns, columns)
    return jax.shard_map(body, mesh=mesh, in_specs=in_specs, out_specs=out_specs, check_vma=False)
```

```python
import math

import jax
import jax.numpy as jnp
from jax import lax
from jax.experimental import pallas as pl
from jax.experimental.pallas import tpu as pltpu
from jax.sharding import PartitionSpec as P

MB = 3
STEP = 5
EPS = 1e-05
CLIP = 1.0
BETA_ONE = 0.5
BETA_TWO = 0.5
RATE_CONV = 0.03
RATE_VEC = 0.3
DECAY_CONV = 0.01
ADAM_EPS = 1e-08
ALL = ("dp", "lat", "lon")
F32 = jnp.float32
BF16 = jnp.bfloat16
GELU_A = math.sqrt(2.0 / math.pi)
GELU_B = GELU_A * 0.044715

S, R, C = 12, 16, 128
TI = S * R
NH = S + 1
TH = 8 * (NH + NH % 2)
T = TI + TH
W3 = 3 * C
PER = S // MB
FLAT = 24 + 24 * S
VM = pl.BlockSpec(memory_space=pltpu.VMEM)
SM = pl.BlockSpec(memory_space=pltpu.SMEM)
FAR = pl.BlockSpec(memory_space=pltpu.HBM)


def call(kernel, outs, args, scratch=(), flops=0, limit=16, scalars=0, far=0, far_out=(), aliases=None):
    args = [
        pltpu.with_memory_space_constraint(arg, pltpu.HBM) if scalars <= n < scalars + far else arg
        for n, arg in enumerate(args)
    ]
    spaces = [SM] * scalars + [FAR] * far + [VM] * (len(args) - scalars - far)
    return pl.pallas_call(
        kernel,
        out_shape=tuple(
            pltpu.HBM(shape, kind) if n in far_out else jax.ShapeDtypeStruct(shape, kind)
            for n, (shape, kind) in enumerate(outs)
        ),
        in_specs=spaces,
        out_specs=tuple(FAR if n in far_out else VM for n in range(len(outs))),
        scratch_shapes=list(scratch),
        input_output_aliases=aliases or {},
        compiler_params=pltpu.CompilerParams(vmem_limit_bytes=limit << 20),
        cost_estimate=pl.CostEstimate(
            flops=flops,
            transcendentals=0,
            bytes_accessed=sum(math.prod(a.shape) * a.dtype.itemsize for a in args),
        ),
    )(*args)


def own_row(row):
    return jnp.where(lax.axis_index("lat") == 0, row, R - 1 - row)


def own_tap(tap):
    return jnp.where(lax.axis_index("lat") == 0, tap, 2 - tap)


def act(v):
    return 0.5 * v * (1.0 + jnp.tanh(v * (GELU_A + GELU_B * (v * v))))


def act_both(v):
    sq = v * v
    tan = jnp.tanh(v * (GELU_A + GELU_B * sq))
    half = 0.5 * (1.0 + tan)
    value = v * half
    slope = half + value * (1.0 - tan) * (GELU_A + (3.0 * GELU_B) * sq)
    return value, slope


def fold(v):
    return jnp.sum(v.reshape(v.shape[0] // 8, 8, C), axis=0)


def down(v):
    return jnp.sum(v, axis=0, keepdims=True)


def batch_sums(values):
    return [fold(values[PER * R * m : PER * R * (m + 1)]) for m in range(MB)]


def build(flat, out, place, tile, side):
    for n in range(S):
        value = tile(n)
        flat[16 + 24 * n : 32 + 24 * n, :] = value
        out[place + (slice(16 * n, 16 * n + 16), slice(C, 2 * C))] = value.astype(BF16)
    whole = out.shape[-2] == T
    for p in range(TH // 16):
        pair = [side(h) if h < NH else jnp.zeros((8, C), F32) for h in (2 * p, 2 * p + 1)]
        for h, value in zip((2 * p, 2 * p + 1), pair):
            if h < NH:
                flat[8 + 24 * h : 16 + 24 * h, :] = value
        if whole:
            at = TI + 16 * p
            out[place + (slice(at, at + 16), slice(C, 2 * C))] = jnp.concatenate(pair, axis=0).astype(BF16)
    emit_sides(flat, out, place)


def emit_sides(flat, out, place):
    for kx in (0, 2):
        columns = slice(C * kx, C * kx + C)
        for n in range(S):
            at = 15 + 24 * n + kx
            out[place + (slice(16 * n, 16 * n + 16), columns)] = flat[at : at + 16, :].astype(BF16)
        if out.shape[-2] != T:
            continue
        for p in range(TH // 16):
            at = 7 + 48 * p + kx
            first = flat[at : at + 8, :]
            second = flat[at + 24 : at + 32, :] if 2 * p + 1 < NH else jnp.zeros((8, C), F32)
            out[place + (slice(TI + 16 * p, TI + 16 * p + 16), columns)] = jnp.concatenate(
                [first, second], axis=0
            ).astype(BF16)


def place_of(i, odd):
    return (i + odd, 1 - odd)


def sided(rows):
    mixed = {}
    for h in range(NH):
        low, high = max(h - 1, 0) // PER, min(h, S - 1) // PER
        if low != high:
            mixed[h] = jnp.concatenate(
                [jnp.broadcast_to(rows[low], (4, C)), jnp.broadcast_to(rows[high], (4, C))], axis=0
            )
    return (
        lambda n: rows[n // PER],
        lambda h: mixed[h] if h in mixed else rows[min(h, S - 1) // PER],
    )


def put_all(ref, rows):
    block = jnp.concatenate(rows, axis=0)
    ref[...] = jnp.broadcast_to(block[None], ref.shape)


def put_pairs(ref, rows):
    for g in range(ref.shape[1]):
        part = jnp.concatenate(rows[2 * g : 2 * g + 2], axis=0)
        for n in range(ref.shape[0]):
            ref[n, g] = part


def got_pairs(ref):
    total = jnp.sum(ref[...], axis=0)
    return [total[g, i : i + 1] for g in range(total.shape[0]) for i in range(2)]


def taken(ref, count):
    return [ref[i : i + 1, :] for i in range(count)]


def vec_rows(ref):
    return [ref[i : i + 1, :] for i in range(6)]


def norm_of(sums, count):
    means = [sums[m] * (1.0 / count) for m in range(MB)]
    inverses = [lax.rsqrt(sums[MB + m] * (1.0 / count) - means[m] * means[m] + EPS) for m in range(MB)]
    return means, inverses


def piece_of(pieces, k, which, rows):
    if k == 0:
        return pieces[0][which, rows, :]
    mine, other = pieces[2 * k - 1], pieces[2 * k]
    return jnp.where(lax.axis_index("lat") == which, mine[rows, :], other[rows, :])


def fill_forward(block, pieces, which):
    count = (len(pieces) + 1) // 2
    size = C // count
    zero = jnp.zeros((C, C), BF16)
    for kx in range(3):
        block[C * kx : C * kx + C, C:] = zero
        block[C * (9 + kx) : C * (10 + kx), :C] = zero
        for ky in range(3):
            source = pl.multiple_of((3 * own_tap(ky) + kx) * size, size)
            for k in range(count):
                owner = lax.rem(lax.axis_index("dp") + (count - k), count) if count > 1 else 0
                part = piece_of(pieces, k, which, pl.ds(source, size))
                for a in range(2):
                    top = pl.multiple_of((3 * (ky + a) + kx) * C + owner * size, size)
                    block[pl.ds(top, size), a * C : a * C + C] = part


def fill_backward(block, forward):
    zero = jnp.zeros((C, C), BF16)
    for kx in range(3):
        block[C * kx : C * kx + C, C:] = zero
        block[C * (9 + kx) : C * (10 + kx), :C] = zero
        for ky in range(3):
            source = (3 * (2 - ky) + 2 - kx) * C
            part = forward[source : source + C, :C].T
            for a in range(2):
                top = (3 * (ky + a) + kx) * C
                block[top : top + C, a * C : a * C + C] = part


def conv_rows(ref, low, high, weight, rows=T):
    pairs = [
        jnp.concatenate([ref[i, 0, :rows], ref[i, 1, :rows], ref[i + 1, 0, :rows], ref[i + 1, 1, :rows]], axis=1)
        for i in range(low, high)
    ]
    got = jnp.dot(jnp.concatenate(pairs, axis=0), weight, preferred_element_type=F32)
    return [
        got[n * rows : n * rows + rows, a * C : a * C + C] for n in range(high - low) for a in range(2)
    ]


def staggered(make, conv, rows, groups):
    total, done = None, 0
    stops = [min(2 * high + 1, rows) for _, high in groups]
    for n, (low, high) in enumerate(groups):
        for row in range(done, stops[n]):
            make(row)
        done = max(done, stops[n])
        total = conv(low, high, total)
        for row in range(done, stops[min(n + 1, len(groups) - 1)]):
            make(row)
        done = stops[min(n + 1, len(groups) - 1)]
    return total


def in_pairs(high):
    return [(low, min(low + 2, high)) for low in range(0, high, 2)]


def added(total, new):
    return new if total is None else [old + more for old, more in zip(total, new)]


def pack_taps(weight, out):
    size = weight.shape[0] // 9
    for t in range(9):
        out[size * t : size * t + size, :] = weight[pl.ds(t, size, stride=9), :].astype(BF16)


def prep_kernel(x, cot, weight, vectors, packed, lat_out, x_near, cot_near, held, held_vec, sems):
    last = lax.axis_index("lat") == 0
    copies = [
        pltpu.make_async_copy(weight, held, sems.at[0]),
        pltpu.make_async_copy(vectors, held_vec, sems.at[1]),
        pltpu.make_async_copy(x.at[:, pl.ds(jnp.where(last, R - 4, 0), 4)], lat_out.at[:, 0:4], sems.at[2]),
        pltpu.make_async_copy(cot.at[:, pl.ds(jnp.where(last, R - 2, 0), 2)], lat_out.at[:, 4:6], sems.at[3]),
        pltpu.make_async_copy(x, x_near, sems.at[4]),
        pltpu.make_async_copy(cot, cot_near, sems.at[5]),
    ]
    for copy in copies:
        copy.start()
    for copy in copies[:2]:
        copy.wait()
    size = 9 * (weight.shape[1] // 9)
    width = vectors.shape[1]
    pick = lax.broadcasted_iota(jnp.int32, (width, C), 1) - lax.axis_index("dp") * width
    pick = jnp.where(pick == lax.broadcasted_iota(jnp.int32, (width, C), 0), 1.0, 0.0).astype(BF16)
    placed = jnp.dot(held_vec[...].astype(BF16), pick, preferred_element_type=F32)
    for k in range(2):
        pack_taps(held.at[k], packed.at[k])
        packed[k, size:, :] = jnp.concatenate([placed, jnp.zeros((10, C), F32)], axis=0).astype(BF16)
    for copy in copies[2:]:
        copy.wait()


def x_beyond(lat_in, n, k):
    return lat_in[n, jnp.where(lax.axis_index("lat") == 0, k, 3 - k)]


def cot_beyond(lat_in, n, k):
    return lat_in[n, jnp.where(lax.axis_index("lat") == 0, 4 + k, 5 - k)]


def cut_far(tile, far_r, far_l, at, columns, rows):
    for m in range(MB):
        tiles = [tile(q, n).astype(F32) for q in range(rows) for n in range(PER * m, PER * m + PER)]
        far_r[at, m] = jnp.concatenate([v[R - columns :] for v in tiles], axis=0).astype(BF16)
        far_l[at, m] = jnp.concatenate([v[:columns] for v in tiles], axis=0).astype(BF16)


def edge_kernel(x, far_r, far_l):
    @pl.loop(0, R // 2)
    def _(i):
        for q in range(2):
            cut_far(lambda _, n: x[n, own_row(2 * i + q)], far_r, far_l, 2 * i + q, 4, 1)


def beyond_kernel(lat_in, packed, right_in, left_in, mine, far_r, far_l):
    for k in range(4):
        cut_far(lambda _, n: x_beyond(lat_in, n, k), far_r, far_l, R + k, 4, 1)
    mine[...] = packed[lax.axis_index("lat")]


def later_kernel(after, cot, lat_in, far_r, far_l):
    @pl.loop(0, R // 2)
    def _(i):
        cut_far(lambda q, n: cot[n, own_row(2 * i + q)], far_r, far_l, i, 2, 2)

    cut_far(lambda q, n: cot_beyond(lat_in, n, q), far_r, far_l, R // 2, 2, 2)


def own_tile(x, lat_in, row):
    if row < R:
        return lambda n: x[n, own_row(row)]
    return lambda n: x_beyond(lat_in, n, row - R)


def first_kernel(x, lat_in, from_left, from_right, block, vec, out, pre, sums, *flats):
    for edge in (0, R + 5):
        out[edge // 2, edge % 2] = jnp.zeros((TI, W3), BF16)
    bias = vec[0:1, :]

    def make(row):
        flat, place, tile = flats[row % 2], place_of(row // 2, row % 2), own_tile(x, lat_in, row)
        for m in range(MB):
            left, right = from_left[row, m].astype(F32), from_right[row, m].astype(F32)
            for n in range(PER):
                s = PER * m + n
                flat[15 + 24 * s : 16 + 24 * s, :] = left[4 * n + 3 : 4 * n + 4]
                flat[32 + 24 * s : 33 + 24 * s, :] = right[4 * n : 4 * n + 1]
        for n in range(S):
            value = tile(n)
            flat[16 + 24 * n : 32 + 24 * n, :] = value.astype(F32)
            out[place + (slice(16 * n, 16 * n + 16), slice(C, 2 * C))] = value
        emit_sides(flat, out, place)

    def conv(low, high, total):
        for n, v in enumerate(conv_rows(out, low, high, block[...], TI)):
            row = 2 * low + n
            pre[row] = v + bias
            if row < R:
                value = act(v + bias)
                total = added(total, batch_sums(value) + batch_sums(value * value))
        return total

    total = staggered(make, conv, R + 4, in_pairs(R // 2 + 2))
    put_pairs(sums, [down(v) for v in total])


def halo_kernel(after, x, lat_in, from_left, from_right, block, vec, pre, halo, *flats):
    for flat in flats:
        flat[...] = jnp.zeros(flat.shape, F32)
    for edge in (0, R + 5):
        halo[edge // 2, edge % 2] = jnp.zeros((TH, W3), BF16)

    def make(row):
        flat, place, tile = flats[row % 2], place_of(row // 2, row % 2), own_tile(x, lat_in, row)
        for m in range(MB):
            left, right = from_left[row, m].astype(F32), from_right[row, m].astype(F32)
            for n in range(PER):
                s = PER * m + n
                value = tile(s).astype(F32)
                flat[12 + 24 * s : 16 + 24 * s, :] = left[4 * n : 4 * n + 4]
                flat[16 + 24 * s : 24 + 24 * s, :] = value[:8]
                flat[24 + 24 * s : 32 + 24 * s, :] = value[8:]
                flat[32 + 24 * s : 36 + 24 * s, :] = right[4 * n : 4 * n + 4]
        for kx in range(3):
            for p in range(TH // 16):
                at = 7 + 48 * p + kx
                second = flat[at + 24 : at + 32, :] if 2 * p + 1 < NH else jnp.zeros((8, C), F32)
                halo[place + (slice(16 * p, 16 * p + 16), slice(C * kx, C * kx + C))] = jnp.concatenate(
                    [flat[at : at + 8, :], second], axis=0
                ).astype(BF16)

    def conv(low, high, total):
        for n, v in enumerate(conv_rows(halo, low, high, block[...], TH)):
            pre[2 * low + n] = v + vec[0:1, :]
        return total

    staggered(make, conv, R + 4, ((0, 3), (3, 6), (6, 10)))


def lead_scales(lead):
    return [0.5 * jnp.sqrt(jnp.full((1, C), lead[n], jnp.int32).astype(F32)) for n in range(S)]


def lead_kernel(lead, cot, dn, sums):
    scale = lead_scales(lead)

    def body(i, total):
        for odd in range(2):
            row = 2 * i + odd
            source = own_row(row)
            values = [cot[n, source].astype(F32) * scale[n] for n in range(S)]
            for n in range(S):
                dn[row, 16 * n : 16 * n + 16, :] = values[n]
            new = [sum(fold(values[n]) for n in range(PER * m, PER * m + PER)) for m in range(MB)]
            total = added(total, new)
        return total

    total = lax.fori_loop(0, R // 2, body, [jnp.zeros((8, C), F32)] * MB)
    sums[...] = jnp.concatenate([down(v) for v in total] + [jnp.zeros((8 - MB, C), F32)], axis=0)


def lead_side_kernel(lead, after, lat_in, from_left, from_right, lat, side, *flats):
    scale = lead_scales(lead)
    for flat in flats:
        flat[...] = jnp.zeros(flat.shape, F32)
    for k in range(2):
        for n in range(S):
            lat[k, 16 * n : 16 * n + 16, :] = cot_beyond(lat_in, n, k).astype(F32) * scale[n]

    @pl.loop(0, R // 2 + 1)
    def _(i):
        for m in range(MB):
            left = from_left[i, m].astype(F32)
            right = from_right[i, m].astype(F32)
            for odd in range(2):
                for n in range(PER):
                    s, at = PER * m + n, 8 * odd + 2 * n
                    flats[odd][14 + 24 * s : 16 + 24 * s, :] = left[at : at + 2] * scale[s]
                    flats[odd][32 + 24 * s : 34 + 24 * s, :] = right[at : at + 2] * scale[s]
        for odd in range(2):
            row = 2 * i + odd
            flat = flats[odd]
            for h in range(NH):
                side[row, 8 * h : 8 * h + 8, :] = flat[8 + 24 * h : 16 + 24 * h, :]
            side[row, 8 * NH :, :] = jnp.zeros((TH - 8 * NH, C), F32)


def block_kernel(*rest):
    pieces, (block, vec) = rest[:-2], rest[-2:]
    fill_forward(block, pieces, 0)
    last = pieces[0].shape[1]
    vec[...] = sum(
        piece_of(pieces, k, 0, slice(last - 16, last)).astype(F32) for k in range((len(pieces) + 1) // 2)
    )


def weight_kernel(after, block_one, *rest):
    pieces, (block_two, two_back, one_back) = rest[:-3], rest[-3:]
    fill_forward(block_two, pieces, 1)
    fill_backward(two_back, block_two)
    fill_backward(one_back, block_one)


def second_kernel(count, pre, pre_side, sums_in, dn, dn_sums, block, vec_in, n_all, pre_two, sums, kept, *flats):
    vec = vec_rows(vec_in)
    kept[...] = jnp.concatenate(got_pairs(sums_in) + [jnp.zeros((2, C), F32)], axis=0)
    means, inverses = norm_of(taken(kept, 2 * MB), count)
    gains = [inverses[m] * vec[1] for m in range(MB)]
    gain, gain_side = sided(gains)
    shift, shift_side = sided([vec[2] - means[m] * gains[m] for m in range(MB)])
    for flat in flats:
        flat[...] = jnp.zeros(flat.shape, F32)
    n_all[0, 0] = jnp.zeros((T, W3), BF16)

    def one(i, odd):
        row = 2 * i + odd
        build(
            flats[odd],
            n_all,
            place_of(i, odd),
            lambda n: act(pre[row, 16 * n : 16 * n + 16, :]) * gain(n) + shift(n),
            lambda h: act(pre_side[row, 8 * h : 8 * h + 8, :]) * gain_side(h) + shift_side(h),
        )

    def conv(low, high, total):
        for n, v in enumerate(conv_rows(n_all, low, high, block[...])):
            row = 2 * low + n
            pre_two[row] = v + vec[3]
            if row < R:
                value = act(v[:TI] + vec[3])
                new = batch_sums(value) + batch_sums(value * value) + batch_sums(value * dn[row])
                total = added(total, new)
        return total

    total = staggered(lambda row: one(row // 2, row % 2), conv, R + 3, in_pairs(R // 2 + 1))
    block_out = jnp.concatenate([down(v) for v in total] + [dn_sums[0:MB, :]], axis=0)
    for g in range(3):
        part = block_out[4 * g : 4 * g + 4]
        for n in range(sums.shape[0]):
            sums[n, g] = part


def second_stats(sums_in, count):
    rows = taken(sums_in, 4 * MB)
    means, inverses = norm_of(rows[: 2 * MB], count)
    dots, plain = rows[2 * MB : 3 * MB], rows[3 * MB :]
    dgain = [inverses[m] * (dots[m] - means[m] * plain[m]) for m in range(MB)]
    return means, inverses, dgain, plain


def back_terms(means, inverses, gain, dgain, dshift, count):
    lin = [inverses[m] * gain for m in range(MB)]
    slope = [-lin[m] * inverses[m] * (dgain[m] * (1.0 / count)) for m in range(MB)]
    const = [-lin[m] * (dshift[m] * (1.0 / count)) - slope[m] * means[m] for m in range(MB)]
    return [sided(rows) for rows in (lin, const, slope)]


def build_back(flat, out, place, terms, pre_tile, tile, pre_side, side):
    def at(pre, incoming, which, index):
        value, deriv = act_both(pre(index))
        lin, const, slope = [term[which](index) for term in terms]
        return deriv * (lin * incoming(index) + const + slope * value)

    build(flat, out, place, lambda n: at(pre_tile, tile, 0, n), lambda h: at(pre_side, side, 1, h))


def back_two_kernel(
    count, pre_two, dn, dn_lat, dn_side, sums_in, pre, block, vec, grad, mid, sums, kept, bias_two, g_all, *flats
):
    total = jnp.sum(sums_in[...], axis=0)
    kept[...] = jnp.concatenate([total[g, i : i + 1] for g in range(MB) for i in range(4)], axis=0)
    means, inverses, dgain, dshift = second_stats(kept, count)
    terms = back_terms(means, inverses, vec[4:5, :], dgain, dshift, count)
    for flat in flats:
        flat[...] = jnp.zeros(flat.shape, F32)
    for edge in (0, R + 3):
        g_all[edge // 2, edge % 2] = jnp.zeros((T, W3), BF16)

    def make(odd, place, row, inner, inner_row):
        build_back(
            flats[odd],
            g_all,
            place,
            terms,
            lambda n: pre_two[row, 16 * n : 16 * n + 16, :],
            lambda n: inner[inner_row, 16 * n : 16 * n + 16, :],
            lambda h: pre_two[row, TI + 8 * h : TI + 8 * h + 8, :],
            lambda h: dn_side[row, 8 * h : 8 * h + 8, :],
        )

    biases = []

    def row_of(row):
        place = place_of(row // 2, row % 2)
        if row < R:
            make(row % 2, place, row, dn, row)
            own = g_all[place + (slice(0, TI), slice(C, 2 * C))]
            grad[row] = own
            biases.append(fold(own.astype(F32)))
        else:
            make(row % 2, place, row, dn_lat, row - R)

    def conv(low, high, total):
        for n, v in enumerate(conv_rows(g_all, low, high, block[...])):
            row = 2 * low + n
            mid[row] = v
            if row < R:
                own = v[:TI]
                total = added(total, batch_sums(own) + batch_sums(own * act(pre[row])))
        return total

    total = staggered(row_of, conv, R + 2, in_pairs(R // 2 + 1))
    bias = sum(biases)
    put_pairs(sums, [down(v) for v in total])
    bias_two[...] = jnp.concatenate([down(bias), jnp.zeros((7, C), F32)], axis=0)


def wgrad_add(acc, inner, grad, low, high):
    left = jnp.concatenate([grad(row) for row in range(low, high)], axis=0)
    right = jnp.concatenate(
        [
            jnp.concatenate([inner[(row + ky) // 2, (row + ky) % 2, :TI] for ky in range(3)], axis=1)
            for row in range(low, high)
        ],
        axis=0,
    )
    part = lax.dot_general(left, right, (((0,), (0,)), ((), ())), preferred_element_type=F32)
    for ky in range(3):
        own = part[:, W3 * ky : W3 * ky + W3]
        acc[ky] = own if low == 0 else acc[ky] + own


def split_out(acc, which, keep, send):
    first = lax.axis_index("lat") == 0
    for ky in range(3):
        for kx in range(3):
            at = pl.ds(pl.multiple_of(144 * which + 16 * (3 * own_tap(ky) + kx), 16), 16)
            taps = acc[ky, :, C * kx : C * kx + C].T
            for d in range(4):
                low, high = taps[32 * d : 32 * d + 16], taps[32 * d + 16 : 32 * d + 32]
                keep[d, at, :] = jnp.where(first, low, high)
                send[d, at, :] = jnp.where(first, high, low).astype(BF16)


def plain_out(acc, which, out):
    for ky in range(3):
        for kx in range(3):
            out[which, 3 * own_tap(ky) + kx] = acc[ky, :, C * kx : C * kx + C].T


def output_kernel(count, after, x, pre_two, sums_in, vec_in, out):
    vec = vec_rows(vec_in)
    means, inverses, _, _ = second_stats(sums_in, count)
    gains = [inverses[m] * vec[4] for m in range(MB)]
    shifts = [vec[5] - means[m] * gains[m] for m in range(MB)]

    @pl.loop(0, R)
    def _(row):
        source = own_row(row)
        for s in range(S):
            value = act(pre_two[row, 16 * s : 16 * s + 16, :])
            out[s, source] = (x[s, source].astype(F32) + value * gains[s // PER] + shifts[s // PER]).astype(BF16)


def first_back_stats(first_in, sums_in, count):
    means, inverses = norm_of(taken(first_in, 2 * MB), count)
    rows = taken(sums_in, 2 * MB)
    dshift = rows[:MB]
    dgain = [inverses[m] * (rows[MB + m] - means[m] * dshift[m]) for m in range(MB)]
    return means, inverses, dgain, dshift


def back_one_kernel(split, count, pre, pre_side, mid, first_in, sums_in, x_all, n_all, grad_two, bias_two, vec, g_inner, bias, kept, *rest):
    outs, (acc_one, acc_two), flats = rest[:-4], rest[-4:-2], rest[-2:]
    kept[...] = jnp.concatenate(got_pairs(sums_in) + [jnp.zeros((2, C), F32)], axis=0)
    means, inverses, dgain, dshift = first_back_stats(first_in, kept, count)
    terms = back_terms(means, inverses, vec[1:2, :], dgain, dshift, count)
    for flat in flats:
        flat[...] = jnp.zeros(flat.shape, F32)
    g_inner[0, 0] = jnp.zeros((TI, W3), BF16)

    def make(row):
        build_back(
            flats[row % 2],
            g_inner,
            ((row + 1) // 2, (row + 1) % 2),
            terms,
            lambda n: pre[row, 16 * n : 16 * n + 16, :],
            lambda n: mid[row, 16 * n : 16 * n + 16, :],
            lambda h: pre_side[row, 8 * h : 8 * h + 8, :],
            lambda h: mid[row, TI + 8 * h : TI + 8 * h + 8, :],
        )

    def made(row):
        return g_inner[(row + 1) // 2, (row + 1) % 2, :, C : 2 * C]

    total = jnp.zeros((8, C), F32)
    for row in range(R + 1):
        make(row)
        if row < R:
            total = total + fold(made(row).astype(F32))
    for low in range(0, R, 4):
        wgrad_add(acc_two, n_all, lambda row: grad_two[row], low, low + 4)
        wgrad_add(acc_one, x_all, made, low, low + 4)
    bias[...] = jnp.concatenate([down(total), jnp.zeros((7, C), F32)], axis=0)
    (split_out if split else plain_out)(acc_two, 1, *outs)
    (split_out if split else plain_out)(acc_one, 0, *outs)
    if split:
        keep, send = outs
        parts = jnp.concatenate(two_of(down(total)) + two_of(bias_two[0:1, :]) + [jnp.zeros((12, C), F32)], axis=0)
        for d in range(4):
            keep[d, 288:, :] = parts
            send[d, 288:, :] = parts.astype(BF16)


def input_grad_kernel(lead, after, g_inner, cot, block, out):
    scale = lead_scales(lead)
    for row, v in enumerate(conv_rows(g_inner, 0, R // 2, block[...], TI)):
        source = own_row(row)
        for n in range(S):
            incoming = cot[n, source].astype(F32) * scale[n]
            out[n, source] = (v[16 * n : 16 * n + 16] + incoming).astype(BF16)


def two_of(v):
    high = v.astype(BF16).astype(F32)
    return [high, (v - high).astype(BF16).astype(F32)]


def bias_rows(total):
    return total[288:289] + total[289:290], total[290:291] + total[291:292]


def message(total):
    one, two = bias_rows(total)
    tail = two_of(one) + two_of(two) + [jnp.zeros((12, C), F32)]
    return jnp.concatenate([total[:288]] + tail, axis=0).astype(BF16)


def merge_kernel(keep, got, *outs):
    for k, out in enumerate(outs):
        d = lax.rem(lax.axis_index("dp") + k, 4)
        total = keep[d] + got[d].astype(F32)
        out[...] = message(total)


def column_kernel(*refs):
    total = sum(ref[...].astype(F32) for ref in refs[:-1])
    refs[-1][...] = message(total)


def plane_kernel(outputs, grad_inputs, *refs):
    parts, (own, sums, slots) = refs[:4], refs[4:]
    for n, part in enumerate(parts):
        slots[lax.rem(lax.axis_index("lon") + (4 - n), 4)] = part[...].astype(F32)
    total = sum(slots[n] for n in range(4))
    own[...] = total[:288]
    put_all(sums, [down(fold(total[:288] * total[:288])), *bias_rows(total), jnp.zeros((1, C), F32)])


def fetch_kernel(*refs):
    far, near, sems = refs[:6], refs[7:13], refs[13]
    copies = [pltpu.make_async_copy(far[n], near[n], sems.at[n]) for n in range(6)]
    for copy in copies:
        copy.start()
    for copy in copies:
        copy.wait()


def adam(weight, first, second, grad, rate, decay):
    first_new = BETA_ONE * first + (1.0 - BETA_ONE) * grad
    second_new = BETA_TWO * second + (1.0 - BETA_TWO) * grad * grad
    first_hat = first_new * (1.0 / (1.0 - BETA_ONE**STEP))
    second_hat = second_new * (1.0 / (1.0 - BETA_TWO**STEP))
    weight_new = weight - rate * (first_hat / (jnp.sqrt(second_hat) + ADAM_EPS) + decay * weight)
    return weight_new, first_new, second_new


def vector_grads(first_in, second_in, third_in, bias_one, bias_two, count):
    _, _, dgain_two, dshift_two = second_stats(second_in, count)
    _, _, dgain_one, dshift_one = first_back_stats(first_in, third_in, count)
    rows = [bias_one, sum(dgain_one), sum(dshift_one), bias_two, sum(dgain_two), sum(dshift_two)]
    return jnp.concatenate(rows, axis=0)


def update_kernel(count, *refs):
    weight, first, second, vectors, vec_first, vec_second = refs[:6]
    (mine, its), (sums_in, first_in, second_in, third_in), refs = refs[6:8], refs[8:12], refs[12:]
    norm_out, weight_new, first_new, second_new, weight_low, vectors_new, vec_first_new, vec_second_new = refs[:8]
    grad = refs[8]
    total = jnp.sum(sums_in[...], axis=0)
    half = sums_in[0]
    vec_grad = vector_grads(first_in, second_in, third_in, half[1:2], half[2:3], count)
    square = jnp.sum(total[0:1], axis=1, keepdims=True) + jnp.sum(
        down(vec_grad * vec_grad), axis=1, keepdims=True
    )
    norm = jnp.sqrt(square)
    norm_out[...] = norm
    clip = jnp.minimum(1.0, CLIP / (norm + 1e-06))
    core = lax.axis_index("lat")
    for k in range(2):
        for lat in range(2):
            for t in range(9):
                at = slice(144 * k + 16 * t, 144 * k + 16 * t + 16)
                grad[k, pl.ds(144 * lat + t, 16, stride=9), :] = jnp.where(core == lat, mine[at, :], its[at, :])
        new = adam(weight[k], first[k], second[k], grad[k] * clip, RATE_CONV, DECAY_CONV)
        weight_new[k], first_new[k], second_new[k] = new
        weight_low[k] = new[0].astype(BF16)
    width = vectors.shape[1]
    turned = pltpu.roll(
        jnp.concatenate([vec_grad, jnp.zeros((2, C), F32)], axis=0),
        lax.rem(C - lax.axis_index("dp") * width, C),
        axis=1,
    )
    new = adam(vectors[...], vec_first[...], vec_second[...], turned[:6, :width] * clip, RATE_VEC, 0.0)
    vectors_new[...], vec_first_new[...], vec_second_new[...] = new


def spread(block, axes):
    return lax.all_to_all(block, axes, 0, 0, tiled=True)


def turn(block, axis, by):
    size = lax.axis_size(axis)
    return lax.ppermute(block, axis, [(i, (i + by) % size) for i in range(size)])


def body(inputs, lead_time, cotangent, conv_weight, conv_first, conv_second, vectors, vec_first, vec_second):
    devices = lax.axis_size("dp") * lax.axis_size("lat") * lax.axis_size("lon")
    groups = lax.axis_size("dp")
    split = groups == 4 and lax.axis_size("lon") == 4
    count = float(PER * R * R * devices)
    size = conv_weight.shape[1] // 9
    flats = [pltpu.VMEM((FLAT, C), F32)] * 2
    conv_flops = 2 * T * 12 * C * 2 * C

    packed, lat_out, x_near, cot_near = call(
        prep_kernel,
        [
            ((2, 9 * size + 16, C), BF16),
            ((S, 6, R, C), BF16),
            (inputs.shape, BF16),
            (inputs.shape, BF16),
        ],
        (inputs, cotangent, conv_weight, vectors),
        [
            pltpu.VMEM(conv_weight.shape, F32),
            pltpu.VMEM(vectors.shape, F32),
            pltpu.SemaphoreType.DMA((6,)),
        ],
        far=4,
    )
    lat_in = turn(lat_out, "lat", 1)
    edge_kinds = [((R + 4, MB, 16, C), BF16)] * 2
    edges = call(edge_kernel, edge_kinds, (x_near,))
    mine, far_r, far_l = call(
        beyond_kernel,
        [((9 * size + 16, C), BF16)] + edge_kinds,
        (lat_in, packed, *edges),
        aliases={2: 1, 3: 2},
    )
    far_left, far_right = turn(far_r, "lon", 1), turn(far_l, "lon", -1)
    dn, dn_sums = call(
        lead_kernel, [((R, TI, C), F32), ((8, C), F32)], (lead_time, cot_near), flops=10**8, scalars=1
    )
    if split:
        fetched = [turn(mine, "dp", k) for k in range(1, groups)]
        *fetched, dn = lax.optimization_barrier((*fetched, dn))
        pieces = [packed]
        for piece in fetched:
            pieces += [piece, turn(piece, "lat", 1)]
    else:
        whole = lax.all_gather(packed, "dp")
        taps = whole[:, :, : 9 * size].reshape(groups, 2, 9, size, C).transpose(1, 2, 0, 3, 4)
        tail = jnp.sum(whole[:, :, 9 * size :], axis=0)
        pieces = [jnp.concatenate([taps.reshape(2, 9 * C, C), tail], axis=1)]
    block_one, vec = call(block_kernel, [((12 * C, 2 * C), BF16), ((16, C), F32)], pieces, flops=10**8)
    x_all, pre_one, sums_one = call(
        first_kernel,
        [((11, 2, TI, W3), BF16), ((R + 4, TI, C), F32), ((devices, MB, 2, C), F32)],
        (x_near, lat_in, far_left, far_right, block_one, vec),
        flats,
        flops=conv_flops * 6,
    )
    sums_one, dn = lax.optimization_barrier((sums_one, dn))
    got_one = spread(sums_one, ALL)
    block_two, two_back, one_back = call(
        weight_kernel,
        [((12 * C, 2 * C), BF16)] * 3,
        (got_one, block_one, *pieces),
        flops=10**8,
    )
    (pre_side,) = call(
        halo_kernel,
        [((R + 4, TH, C), F32)],
        (got_one, x_near, lat_in, far_left, far_right, block_one, vec),
        [pltpu.VMEM((11, 2, TH, W3), BF16)] + flats,
        flops=conv_flops * 4,
    )
    cot_r, cot_l = call(
        later_kernel, [((R // 2 + 1, MB, 16, C), BF16)] * 2, (got_one, cot_near, lat_in)
    )
    cot_left, cot_right = turn(cot_r, "lon", 1), turn(cot_l, "lon", -1)
    n_all, pre_two, sums_two, stat_one = call(
        lambda *refs: second_kernel(count, *refs),
        [((10, 2, T, W3), BF16), ((R + 2, T, C), F32), ((devices, 3, 4, C), F32), ((8, C), F32)],
        (pre_one, pre_side, got_one, dn, dn_sums, block_two, vec),
        flats,
        flops=conv_flops * 9,
    )
    dn_lat, dn_side = call(
        lead_side_kernel,
        [((2, TI, C), F32), ((R + 2, TH, C), F32)],
        (lead_time, sums_two, lat_in, cot_left, cot_right),
        flats,
        flops=10**8,
        scalars=1,
    )
    sums_two, dn_lat, dn_side = lax.optimization_barrier((sums_two, dn_lat, dn_side))
    got_two = spread(sums_two, ALL)
    grad_two, mid, sums_three, stat_two, bias_two = call(
        lambda *refs: back_two_kernel(count, *refs),
        [((R, TI, C), BF16), ((R + 2, T, C), F32), ((devices, MB, 2, C), F32), ((4 * MB, C), F32), ((8, C), F32)],
        (pre_two, dn, dn_lat, dn_side, got_two, pre_one, two_back, vec),
        [pltpu.VMEM((10, 2, T, W3), BF16)] + flats,
        flops=conv_flops * 9,
    )
    got_three = spread(sums_three, ALL)
    grad_kinds = [((4, 304, C), F32), ((4, 304, C), BF16)] if split else [((2, 9, C, C), F32)]
    g_inner, bias_one, stat_three, *grads = call(
        lambda *refs: back_one_kernel(split, count, *refs),
        [((9, 2, TI, W3), BF16), ((8, C), F32), ((8, C), F32)] + grad_kinds,
        (pre_one, pre_side, mid, stat_one, got_three, x_all, n_all, grad_two, bias_two, vec),
        [pltpu.VMEM((3, C, W3), F32)] * 2 + flats,
        flops=conv_flops * 9,
    )

    def finish(after):
        (outputs,) = call(
            lambda *refs: output_kernel(count, *refs),
            [((S, R, R, C), BF16)],
            (after, inputs, pre_two, stat_two, vec),
            flops=10**8,
        )
        (grad_inputs,) = call(
            input_grad_kernel,
            [((S, R, R, C), BF16)],
            (lead_time, after, g_inner, cotangent, one_back),
            flops=conv_flops * 6,
            scalars=1,
        )
        return outputs, grad_inputs

    if split:
        merged = call(merge_kernel, [((304, C), BF16)] * 4, (grads[0], turn(grads[1], "lat", 1)))
        column = [merged[0]] + [turn(merged[k], "dp", k) for k in range(1, 4)]
        outputs, grad_inputs = finish(merged[0])
        (added_up,) = call(column_kernel, [((304, C), BF16)], column)
        row = [added_up] + [turn(added_up, "lon", k) for k in range(1, 4)]
        own, sums_four = call(
            plane_kernel,
            [((288, C), F32), ((2 * groups, 4, C), F32)],
            (outputs, grad_inputs, *row),
            [pltpu.VMEM((4, 304, C), F32)],
            far=2,
        )
        got_four = spread(sums_four, ("dp", "lat"))
        its = turn(own, "lat", 1)
        kinds = [((1, 1), F32)] + [(conv_weight.shape, F32)] * 3 + [(conv_weight.shape, BF16)]
        moments = (conv_weight, conv_first, conv_second, vectors, vec_first, vec_second)
        moments = call(
            fetch_kernel,
            [(moment.shape, F32) for moment in moments],
            (*moments, own),
            [pltpu.SemaphoreType.DMA((6,))],
            flops=10**10,
            far=6,
        )
        norm, *news = call(
            lambda *refs: update_kernel(count, *refs),
            kinds + [(vectors.shape, F32)] * 3,
            (*moments, own, its, got_four, stat_one, stat_two, stat_three),
            [pltpu.VMEM(conv_weight.shape, F32)],
        )
        return (outputs, grad_inputs, norm.reshape(()), *news)
    outputs, grad_inputs = finish(bias_one)
    stacked = grads[0].transpose(0, 2, 1, 3).reshape(2, 9 * C, C)
    conv_total, total_one, total_two = lax.psum((stacked, bias_one[0:1], bias_two[0:1]), ALL)
    vec_total = vector_grads(stat_one, stat_two, stat_three, total_one, total_two, count)
    grad_norm = jnp.sqrt(jnp.sum(conv_total * conv_total) + jnp.sum(vec_total * vec_total))
    clip = jnp.minimum(1.0, CLIP / (grad_norm + 1e-06))
    index = lax.axis_index("dp")
    conv_own = lax.dynamic_slice_in_dim(conv_total, index * conv_weight.shape[1], conv_weight.shape[1], 1)
    vec_own = lax.dynamic_slice_in_dim(vec_total, index * vectors.shape[1], vectors.shape[1], 1)
    conv_news = adam(conv_weight, conv_first, conv_second, conv_own * clip, RATE_CONV, DECAY_CONV)
    vec_news = adam(vectors, vec_first, vec_second, vec_own * clip, RATE_VEC, 0.0)
    return (outputs, grad_inputs, grad_norm, *conv_news, conv_news[0].astype(BF16), *vec_news)


def solution(mesh):
    grid = P("dp", "lat", "lon", None)
    rows = P(None, "dp", None)
    columns = P(None, "dp")
    in_specs = (grid, P("dp"), grid, rows, rows, rows, columns, columns, columns)
    out_specs = (grid, grid, P(), rows, rows, rows, rows, columns, columns, columns)
    return jax.shard_map(body, mesh=mesh, in_specs=in_specs, out_specs=out_specs, check_vma=False)
```

```python
import math

import jax
import jax.numpy as jnp
from jax import lax
from jax.experimental import pallas as pl
from jax.experimental.pallas import tpu as pltpu
from jax.sharding import PartitionSpec as P

MB = 3
STEP = 5
EPS = 1e-05
CLIP = 1.0
BETA_ONE = 0.5
BETA_TWO = 0.5
RATE_CONV = 0.03
RATE_VEC = 0.3
DECAY_CONV = 0.01
ADAM_EPS = 1e-08
ALL = ("dp", "lat", "lon")
F32 = jnp.float32
BF16 = jnp.bfloat16
GELU_A = math.sqrt(2.0 / math.pi)
GELU_B = GELU_A * 0.044715

S, R, C = 12, 16, 128
TI = S * R
NH = S + 1
TH = 8 * (NH + NH % 2)
T = TI + TH
W3 = 3 * C
PER = S // MB
FLAT = 24 + 24 * S
VM = pl.BlockSpec(memory_space=pltpu.VMEM)
SM = pl.BlockSpec(memory_space=pltpu.SMEM)
FAR = pl.BlockSpec(memory_space=pltpu.HBM)


def call(kernel, outs, args, scratch=(), flops=0, limit=16, scalars=0, far=0, far_out=(), aliases=None):
    args = [
        pltpu.with_memory_space_constraint(arg, pltpu.HBM) if scalars <= n < scalars + far else arg
        for n, arg in enumerate(args)
    ]
    spaces = [SM] * scalars + [FAR] * far + [VM] * (len(args) - scalars - far)
    return pl.pallas_call(
        kernel,
        out_shape=tuple(
            pltpu.HBM(shape, kind) if n in far_out else jax.ShapeDtypeStruct(shape, kind)
            for n, (shape, kind) in enumerate(outs)
        ),
        in_specs=spaces,
        out_specs=tuple(FAR if n in far_out else VM for n in range(len(outs))),
        scratch_shapes=list(scratch),
        input_output_aliases=aliases or {},
        compiler_params=pltpu.CompilerParams(vmem_limit_bytes=limit << 20),
        cost_estimate=pl.CostEstimate(
            flops=flops,
            transcendentals=0,
            bytes_accessed=sum(math.prod(a.shape) * a.dtype.itemsize for a in args),
        ),
    )(*args)


def own_row(row):
    return jnp.where(lax.axis_index("lat") == 0, row, R - 1 - row)


def own_tap(tap):
    return jnp.where(lax.axis_index("lat") == 0, tap, 2 - tap)


def act(v):
    return 0.5 * v * (1.0 + jnp.tanh(v * (GELU_A + GELU_B * (v * v))))


def act_both(v):
    sq = v * v
    tan = jnp.tanh(v * (GELU_A + GELU_B * sq))
    half = 0.5 * (1.0 + tan)
    value = v * half
    slope = half + value * (1.0 - tan) * (GELU_A + (3.0 * GELU_B) * sq)
    return value, slope


def fold(v):
    return jnp.sum(v.reshape(v.shape[0] // 8, 8, C), axis=0)


def down(v):
    return jnp.sum(v, axis=0, keepdims=True)


def batch_sums(values):
    return [fold(values[PER * R * m : PER * R * (m + 1)]) for m in range(MB)]


def build(flat, out, place, tile, side):
    for n in range(S):
        value = tile(n)
        flat[16 + 24 * n : 32 + 24 * n, :] = value
        out[place + (slice(16 * n, 16 * n + 16), slice(C, 2 * C))] = value.astype(BF16)
    whole = out.shape[-2] == T
    for p in range(TH // 16):
        pair = [side(h) if h < NH else jnp.zeros((8, C), F32) for h in (2 * p, 2 * p + 1)]
        for h, value in zip((2 * p, 2 * p + 1), pair):
            if h < NH:
                flat[8 + 24 * h : 16 + 24 * h, :] = value
        if whole:
            at = TI + 16 * p
            out[place + (slice(at, at + 16), slice(C, 2 * C))] = jnp.concatenate(pair, axis=0).astype(BF16)
    emit_sides(flat, out, place)


def emit_sides(flat, out, place):
    for kx in (0, 2):
        columns = slice(C * kx, C * kx + C)
        for n in range(S):
            at = 15 + 24 * n + kx
            out[place + (slice(16 * n, 16 * n + 16), columns)] = flat[at : at + 16, :].astype(BF16)
        if out.shape[-2] != T:
            continue
        for p in range(TH // 16):
            at = 7 + 48 * p + kx
            first = flat[at : at + 8, :]
            second = flat[at + 24 : at + 32, :] if 2 * p + 1 < NH else jnp.zeros((8, C), F32)
            out[place + (slice(TI + 16 * p, TI + 16 * p + 16), columns)] = jnp.concatenate(
                [first, second], axis=0
            ).astype(BF16)


def place_of(i, odd):
    return (i + odd, 1 - odd)


def sided(rows):
    mixed = {}
    for h in range(NH):
        low, high = max(h - 1, 0) // PER, min(h, S - 1) // PER
        if low != high:
            mixed[h] = jnp.concatenate(
                [jnp.broadcast_to(rows[low], (4, C)), jnp.broadcast_to(rows[high], (4, C))], axis=0
            )
    return (
        lambda n: rows[n // PER],
        lambda h: mixed[h] if h in mixed else rows[min(h, S - 1) // PER],
    )


def put_all(ref, rows):
    block = jnp.concatenate(rows, axis=0)
    ref[...] = jnp.broadcast_to(block[None], ref.shape)


def put_pairs(ref, rows):
    for g in range(ref.shape[1]):
        part = jnp.concatenate(rows[2 * g : 2 * g + 2], axis=0)
        for n in range(ref.shape[0]):
            ref[n, g] = part


def got_pairs(ref):
    total = jnp.sum(ref[...], axis=0)
    return [total[g, i : i + 1] for g in range(total.shape[0]) for i in range(2)]


def taken(ref, count):
    return [ref[i : i + 1, :] for i in range(count)]


def vec_rows(ref):
    return [ref[i : i + 1, :] for i in range(6)]


def norm_of(sums, count):
    means = [sums[m] * (1.0 / count) for m in range(MB)]
    inverses = [lax.rsqrt(sums[MB + m] * (1.0 / count) - means[m] * means[m] + EPS) for m in range(MB)]
    return means, inverses


def piece_of(pieces, k, which, rows):
    if k == 0:
        return pieces[0][which, rows, :]
    mine, other = pieces[2 * k - 1], pieces[2 * k]
    return jnp.where(lax.axis_index("lat") == which, mine[rows, :], other[rows, :])


def fill_forward(block, pieces, which):
    count = (len(pieces) + 1) // 2
    size = C // count
    zero = jnp.zeros((C, C), BF16)
    for kx in range(3):
        block[C * kx : C * kx + C, C:] = zero
        block[C * (9 + kx) : C * (10 + kx), :C] = zero
        for ky in range(3):
            source = pl.multiple_of((3 * own_tap(ky) + kx) * size, size)
            for k in range(count):
                owner = lax.rem(lax.axis_index("dp") + (count - k), count) if count > 1 else 0
                part = piece_of(pieces, k, which, pl.ds(source, size))
                for a in range(2):
                    top = pl.multiple_of((3 * (ky + a) + kx) * C + owner * size, size)
                    block[pl.ds(top, size), a * C : a * C + C] = part


def fill_backward(block, forward):
    zero = jnp.zeros((C, C), BF16)
    for kx in range(3):
        block[C * kx : C * kx + C, C:] = zero
        block[C * (9 + kx) : C * (10 + kx), :C] = zero
        for ky in range(3):
            source = (3 * (2 - ky) + 2 - kx) * C
            part = forward[source : source + C, :C].T
            for a in range(2):
                top = (3 * (ky + a) + kx) * C
                block[top : top + C, a * C : a * C + C] = part


def conv_rows(ref, low, high, weight, rows=T):
    pairs = [
        jnp.concatenate([ref[i, 0, :rows], ref[i, 1, :rows], ref[i + 1, 0, :rows], ref[i + 1, 1, :rows]], axis=1)
        for i in range(low, high)
    ]
    got = jnp.dot(jnp.concatenate(pairs, axis=0), weight, preferred_element_type=F32)
    return [
        got[n * rows : n * rows + rows, a * C : a * C + C] for n in range(high - low) for a in range(2)
    ]


def staggered(make, conv, rows, groups):
    total, done = None, 0
    stops = [min(2 * high + 1, rows) for _, high in groups]
    for n, (low, high) in enumerate(groups):
        for row in range(done, stops[n]):
            make(row)
        done = max(done, stops[n])
        total = conv(low, high, total)
        for row in range(done, stops[min(n + 1, len(groups) - 1)]):
            make(row)
        done = stops[min(n + 1, len(groups) - 1)]
    return total


def in_pairs(high):
    return [(low, min(low + 2, high)) for low in range(0, high, 2)]


def added(total, new):
    return new if total is None else [old + more for old, more in zip(total, new)]


def pack_taps(weight, out):
    size = weight.shape[0] // 9
    for t in range(9):
        out[size * t : size * t + size, :] = weight[pl.ds(t, size, stride=9), :].astype(BF16)


def prep_kernel(x, cot, weight, vectors, packed, lat_out, held, held_vec, sems):
    last = lax.axis_index("lat") == 0
    copies = [
        pltpu.make_async_copy(weight, held, sems.at[0]),
        pltpu.make_async_copy(vectors, held_vec, sems.at[1]),
        pltpu.make_async_copy(x.at[:, pl.ds(jnp.where(last, R - 4, 0), 4)], lat_out.at[:, 0:4], sems.at[2]),
        pltpu.make_async_copy(cot.at[:, pl.ds(jnp.where(last, R - 2, 0), 2)], lat_out.at[:, 4:6], sems.at[3]),
    ]
    for copy in copies:
        copy.start()
    for copy in copies[:2]:
        copy.wait()
    size = 9 * (weight.shape[1] // 9)
    width = vectors.shape[1]
    pick = lax.broadcasted_iota(jnp.int32, (width, C), 1) - lax.axis_index("dp") * width
    pick = jnp.where(pick == lax.broadcasted_iota(jnp.int32, (width, C), 0), 1.0, 0.0).astype(BF16)
    placed = jnp.dot(held_vec[...].astype(BF16), pick, preferred_element_type=F32)
    for k in range(2):
        pack_taps(held.at[k], packed.at[k])
        packed[k, size:, :] = jnp.concatenate([placed, jnp.zeros((10, C), F32)], axis=0).astype(BF16)
    for copy in copies[2:]:
        copy.wait()


def x_beyond(lat_in, n, k):
    return lat_in[n, jnp.where(lax.axis_index("lat") == 0, k, 3 - k)]


def cot_beyond(lat_in, n, k):
    return lat_in[n, jnp.where(lax.axis_index("lat") == 0, 4 + k, 5 - k)]


def cut_far(tile, far_r, far_l, at, columns, rows):
    for m in range(MB):
        tiles = [tile(q, n).astype(F32) for q in range(rows) for n in range(PER * m, PER * m + PER)]
        far_r[at, m] = jnp.concatenate([v[R - columns :] for v in tiles], axis=0).astype(BF16)
        far_l[at, m] = jnp.concatenate([v[:columns] for v in tiles], axis=0).astype(BF16)


def edge_kernel(x_far, cot_far, x, cot, far_r, far_l, sems):
    copies = [pltpu.make_async_copy(x_far, x, sems.at[0]), pltpu.make_async_copy(cot_far, cot, sems.at[1])]
    for copy in copies:
        copy.start()
    copies[0].wait()

    @pl.loop(0, R // 2)
    def _(i):
        for q in range(2):
            cut_far(lambda _, n: x[n, own_row(2 * i + q)], far_r, far_l, 2 * i + q, 4, 1)

    copies[1].wait()


def beyond_kernel(lat_in, packed, right_in, left_in, mine, far_r, far_l):
    for k in range(4):
        cut_far(lambda _, n: x_beyond(lat_in, n, k), far_r, far_l, R + k, 4, 1)
    mine[...] = packed[lax.axis_index("lat")]


def later_kernel(cot, lat_in, far_r, far_l):
    @pl.loop(0, R // 2)
    def _(i):
        cut_far(lambda q, n: cot[n, own_row(2 * i + q)], far_r, far_l, i, 2, 2)

    cut_far(lambda q, n: cot_beyond(lat_in, n, q), far_r, far_l, R // 2, 2, 2)


def own_tile(x, lat_in, row):
    if row < R:
        return lambda n: x[n, own_row(row)]
    return lambda n: x_beyond(lat_in, n, row - R)


def first_kernel(x, lat_in, from_left, from_right, block, vec, out, pre, sums, *flats):
    for edge in (0, R + 5):
        out[edge // 2, edge % 2] = jnp.zeros((TI, W3), BF16)
    bias = vec[0:1, :]

    def make(row):
        flat, place, tile = flats[row % 2], place_of(row // 2, row % 2), own_tile(x, lat_in, row)
        for m in range(MB):
            left, right = from_left[row, m].astype(F32), from_right[row, m].astype(F32)
            for n in range(PER):
                s = PER * m + n
                flat[15 + 24 * s : 16 + 24 * s, :] = left[4 * n + 3 : 4 * n + 4]
                flat[32 + 24 * s : 33 + 24 * s, :] = right[4 * n : 4 * n + 1]
        for n in range(S):
            value = tile(n)
            flat[16 + 24 * n : 32 + 24 * n, :] = value.astype(F32)
            out[place + (slice(16 * n, 16 * n + 16), slice(C, 2 * C))] = value
        emit_sides(flat, out, place)

    def conv(low, high, total):
        for n, v in enumerate(conv_rows(out, low, high, block[...], TI)):
            row = 2 * low + n
            pre[row] = v + bias
            if row < R:
                value = act(v + bias)
                total = added(total, batch_sums(value) + batch_sums(value * value))
        return total

    total = staggered(make, conv, R + 4, in_pairs(R // 2 + 2))
    put_pairs(sums, [down(v) for v in total])


def halo_kernel(after, x, lat_in, from_left, from_right, block, vec, pre, halo, *flats):
    for flat in flats:
        flat[...] = jnp.zeros(flat.shape, F32)
    for edge in (0, R + 5):
        halo[edge // 2, edge % 2] = jnp.zeros((TH, W3), BF16)

    def make(row):
        flat, place, tile = flats[row % 2], place_of(row // 2, row % 2), own_tile(x, lat_in, row)
        for m in range(MB):
            left, right = from_left[row, m].astype(F32), from_right[row, m].astype(F32)
            for n in range(PER):
                s = PER * m + n
                value = tile(s).astype(F32)
                flat[12 + 24 * s : 16 + 24 * s, :] = left[4 * n : 4 * n + 4]
                flat[16 + 24 * s : 24 + 24 * s, :] = value[:8]
                flat[24 + 24 * s : 32 + 24 * s, :] = value[8:]
                flat[32 + 24 * s : 36 + 24 * s, :] = right[4 * n : 4 * n + 4]
        for kx in range(3):
            for p in range(TH // 16):
                at = 7 + 48 * p + kx
                second = flat[at + 24 : at + 32, :] if 2 * p + 1 < NH else jnp.zeros((8, C), F32)
                halo[place + (slice(16 * p, 16 * p + 16), slice(C * kx, C * kx + C))] = jnp.concatenate(
                    [flat[at : at + 8, :], second], axis=0
                ).astype(BF16)

    def conv(low, high, total):
        for n, v in enumerate(conv_rows(halo, low, high, block[...], TH)):
            pre[2 * low + n] = v + vec[0:1, :]
        return total

    staggered(make, conv, R + 4, ((0, 3), (3, 6), (6, 10)))


def lead_scales(lead):
    return [0.5 * jnp.sqrt(jnp.full((1, C), lead[n], jnp.int32).astype(F32)) for n in range(S)]


def lead_kernel(lead, cot, dn, sums):
    scale = lead_scales(lead)

    def body(i, total):
        for odd in range(2):
            row = 2 * i + odd
            source = own_row(row)
            values = [cot[n, source].astype(F32) * scale[n] for n in range(S)]
            for n in range(S):
                dn[row, 16 * n : 16 * n + 16, :] = values[n]
            new = [sum(fold(values[n]) for n in range(PER * m, PER * m + PER)) for m in range(MB)]
            total = added(total, new)
        return total

    total = lax.fori_loop(0, R // 2, body, [jnp.zeros((8, C), F32)] * MB)
    sums[...] = jnp.concatenate([down(v) for v in total] + [jnp.zeros((8 - MB, C), F32)], axis=0)


def lead_side_kernel(lead, after, lat_in, from_left, from_right, lat, side, *flats):
    scale = lead_scales(lead)
    for flat in flats:
        flat[...] = jnp.zeros(flat.shape, F32)
    for k in range(2):
        for n in range(S):
            lat[k, 16 * n : 16 * n + 16, :] = cot_beyond(lat_in, n, k).astype(F32) * scale[n]

    @pl.loop(0, R // 2 + 1)
    def _(i):
        for m in range(MB):
            left = from_left[i, m].astype(F32)
            right = from_right[i, m].astype(F32)
            for odd in range(2):
                for n in range(PER):
                    s, at = PER * m + n, 8 * odd + 2 * n
                    flats[odd][14 + 24 * s : 16 + 24 * s, :] = left[at : at + 2] * scale[s]
                    flats[odd][32 + 24 * s : 34 + 24 * s, :] = right[at : at + 2] * scale[s]
        for odd in range(2):
            row = 2 * i + odd
            flat = flats[odd]
            for h in range(NH):
                side[row, 8 * h : 8 * h + 8, :] = flat[8 + 24 * h : 16 + 24 * h, :]
            side[row, 8 * NH :, :] = jnp.zeros((TH - 8 * NH, C), F32)


def block_kernel(*rest):
    pieces, (block, vec) = rest[:-2], rest[-2:]
    fill_forward(block, pieces, 0)
    last = pieces[0].shape[1]
    vec[...] = sum(
        piece_of(pieces, k, 0, slice(last - 16, last)).astype(F32) for k in range((len(pieces) + 1) // 2)
    )


def weight_kernel(after, block_one, *rest):
    pieces, (block_two, two_back, one_back) = rest[:-3], rest[-3:]
    fill_forward(block_two, pieces, 1)
    fill_backward(two_back, block_two)
    fill_backward(one_back, block_one)


def second_kernel(count, pre, pre_side, sums_in, dn, dn_sums, block, vec_in, n_all, pre_two, sums, kept, *flats):
    vec = vec_rows(vec_in)
    kept[...] = jnp.concatenate(got_pairs(sums_in) + [jnp.zeros((2, C), F32)], axis=0)
    means, inverses = norm_of(taken(kept, 2 * MB), count)
    gains = [inverses[m] * vec[1] for m in range(MB)]
    gain, gain_side = sided(gains)
    shift, shift_side = sided([vec[2] - means[m] * gains[m] for m in range(MB)])
    for flat in flats:
        flat[...] = jnp.zeros(flat.shape, F32)
    n_all[0, 0] = jnp.zeros((T, W3), BF16)

    def one(i, odd):
        row = 2 * i + odd
        build(
            flats[odd],
            n_all,
            place_of(i, odd),
            lambda n: act(pre[row, 16 * n : 16 * n + 16, :]) * gain(n) + shift(n),
            lambda h: act(pre_side[row, 8 * h : 8 * h + 8, :]) * gain_side(h) + shift_side(h),
        )

    def conv(low, high, total):
        for n, v in enumerate(conv_rows(n_all, low, high, block[...])):
            row = 2 * low + n
            pre_two[row] = v + vec[3]
            if row < R:
                value = act(v[:TI] + vec[3])
                new = batch_sums(value) + batch_sums(value * value) + batch_sums(value * dn[row])
                total = added(total, new)
        return total

    total = staggered(lambda row: one(row // 2, row % 2), conv, R + 3, in_pairs(R // 2 + 1))
    block_out = jnp.concatenate([down(v) for v in total] + [dn_sums[0:MB, :]], axis=0)
    for g in range(3):
        part = block_out[4 * g : 4 * g + 4]
        for n in range(sums.shape[0]):
            sums[n, g] = part


def second_stats(sums_in, count):
    rows = taken(sums_in, 4 * MB)
    means, inverses = norm_of(rows[: 2 * MB], count)
    dots, plain = rows[2 * MB : 3 * MB], rows[3 * MB :]
    dgain = [inverses[m] * (dots[m] - means[m] * plain[m]) for m in range(MB)]
    return means, inverses, dgain, plain


def back_terms(means, inverses, gain, dgain, dshift, count):
    lin = [inverses[m] * gain for m in range(MB)]
    slope = [-lin[m] * inverses[m] * (dgain[m] * (1.0 / count)) for m in range(MB)]
    const = [-lin[m] * (dshift[m] * (1.0 / count)) - slope[m] * means[m] for m in range(MB)]
    return [sided(rows) for rows in (lin, const, slope)]


def build_back(flat, out, place, terms, pre_tile, tile, pre_side, side):
    def at(pre, incoming, which, index):
        value, deriv = act_both(pre(index))
        lin, const, slope = [term[which](index) for term in terms]
        return deriv * (lin * incoming(index) + const + slope * value)

    build(flat, out, place, lambda n: at(pre_tile, tile, 0, n), lambda h: at(pre_side, side, 1, h))


def back_two_kernel(
    count, pre_two, dn, dn_lat, dn_side, sums_in, pre, block, vec, grad, mid, sums, kept, bias_two, g_all, *flats
):
    total = jnp.sum(sums_in[...], axis=0)
    kept[...] = jnp.concatenate([total[g, i : i + 1] for g in range(MB) for i in range(4)], axis=0)
    means, inverses, dgain, dshift = second_stats(kept, count)
    terms = back_terms(means, inverses, vec[4:5, :], dgain, dshift, count)
    for flat in flats:
        flat[...] = jnp.zeros(flat.shape, F32)
    for edge in (0, R + 3):
        g_all[edge // 2, edge % 2] = jnp.zeros((T, W3), BF16)

    def make(odd, place, row, inner, inner_row):
        build_back(
            flats[odd],
            g_all,
            place,
            terms,
            lambda n: pre_two[row, 16 * n : 16 * n + 16, :],
            lambda n: inner[inner_row, 16 * n : 16 * n + 16, :],
            lambda h: pre_two[row, TI + 8 * h : TI + 8 * h + 8, :],
            lambda h: dn_side[row, 8 * h : 8 * h + 8, :],
        )

    biases = []

    def row_of(row):
        place = place_of(row // 2, row % 2)
        if row < R:
            make(row % 2, place, row, dn, row)
            own = g_all[place + (slice(0, TI), slice(C, 2 * C))]
            grad[row] = own
            biases.append(fold(own.astype(F32)))
        else:
            make(row % 2, place, row, dn_lat, row - R)

    def conv(low, high, total):
        for n, v in enumerate(conv_rows(g_all, low, high, block[...])):
            row = 2 * low + n
            mid[row] = v
            if row < R:
                own = v[:TI]
                total = added(total, batch_sums(own) + batch_sums(own * act(pre[row])))
        return total

    total = staggered(row_of, conv, R + 2, in_pairs(R // 2 + 1))
    bias = sum(biases)
    put_pairs(sums, [down(v) for v in total])
    bias_two[...] = jnp.concatenate([down(bias), jnp.zeros((7, C), F32)], axis=0)


def wgrad_add(acc, inner, grad, low, high):
    left = jnp.concatenate([grad(row) for row in range(low, high)], axis=0)
    right = jnp.concatenate(
        [
            jnp.concatenate([inner[(row + ky) // 2, (row + ky) % 2, :TI] for ky in range(3)], axis=1)
            for row in range(low, high)
        ],
        axis=0,
    )
    part = lax.dot_general(left, right, (((0,), (0,)), ((), ())), preferred_element_type=F32)
    for ky in range(3):
        own = part[:, W3 * ky : W3 * ky + W3]
        acc[ky] = own if low == 0 else acc[ky] + own


def split_out(acc, which, keep, send):
    first = lax.axis_index("lat") == 0
    for ky in range(3):
        for kx in range(3):
            at = pl.ds(pl.multiple_of(144 * which + 16 * (3 * own_tap(ky) + kx), 16), 16)
            taps = acc[ky, :, C * kx : C * kx + C].T
            for d in range(4):
                low, high = taps[32 * d : 32 * d + 16], taps[32 * d + 16 : 32 * d + 32]
                keep[d, at, :] = jnp.where(first, low, high)
                send[d, at, :] = jnp.where(first, high, low).astype(BF16)


def plain_out(acc, which, out):
    for ky in range(3):
        for kx in range(3):
            out[which, 3 * own_tap(ky) + kx] = acc[ky, :, C * kx : C * kx + C].T


def output_kernel(count, after, x, pre_two, sums_in, vec_in, out):
    vec = vec_rows(vec_in)
    means, inverses, _, _ = second_stats(sums_in, count)
    gains = [inverses[m] * vec[4] for m in range(MB)]
    shifts = [vec[5] - means[m] * gains[m] for m in range(MB)]

    @pl.loop(0, R)
    def _(row):
        source = own_row(row)
        for s in range(S):
            value = act(pre_two[row, 16 * s : 16 * s + 16, :])
            out[s, source] = (x[s, source].astype(F32) + value * gains[s // PER] + shifts[s // PER]).astype(BF16)


def first_back_stats(first_in, sums_in, count):
    means, inverses = norm_of(taken(first_in, 2 * MB), count)
    rows = taken(sums_in, 2 * MB)
    dshift = rows[:MB]
    dgain = [inverses[m] * (rows[MB + m] - means[m] * dshift[m]) for m in range(MB)]
    return means, inverses, dgain, dshift


def back_one_kernel(split, count, pre, pre_side, mid, first_in, sums_in, x_all, n_all, grad_two, bias_two, vec, g_inner, bias, kept, *rest):
    outs, (acc_one, acc_two), flats = rest[:-4], rest[-4:-2], rest[-2:]
    kept[...] = jnp.concatenate(got_pairs(sums_in) + [jnp.zeros((2, C), F32)], axis=0)
    means, inverses, dgain, dshift = first_back_stats(first_in, kept, count)
    terms = back_terms(means, inverses, vec[1:2, :], dgain, dshift, count)
    for flat in flats:
        flat[...] = jnp.zeros(flat.shape, F32)
    g_inner[0, 0] = jnp.zeros((TI, W3), BF16)

    def make(row):
        build_back(
            flats[row % 2],
            g_inner,
            ((row + 1) // 2, (row + 1) % 2),
            terms,
            lambda n: pre[row, 16 * n : 16 * n + 16, :],
            lambda n: mid[row, 16 * n : 16 * n + 16, :],
            lambda h: pre_side[row, 8 * h : 8 * h + 8, :],
            lambda h: mid[row, TI + 8 * h : TI + 8 * h + 8, :],
        )

    def made(row):
        return g_inner[(row + 1) // 2, (row + 1) % 2, :, C : 2 * C]

    total = jnp.zeros((8, C), F32)
    for row in range(R + 1):
        make(row)
        if row < R:
            total = total + fold(made(row).astype(F32))
    for low in range(0, R, 4):
        wgrad_add(acc_two, n_all, lambda row: grad_two[row], low, low + 4)
        wgrad_add(acc_one, x_all, made, low, low + 4)
    bias[...] = jnp.concatenate([down(total), jnp.zeros((7, C), F32)], axis=0)
    (split_out if split else plain_out)(acc_two, 1, *outs)
    (split_out if split else plain_out)(acc_one, 0, *outs)
    if split:
        keep, send = outs
        parts = jnp.concatenate(two_of(down(total)) + two_of(bias_two[0:1, :]) + [jnp.zeros((12, C), F32)], axis=0)
        for d in range(4):
            keep[d, 288:, :] = parts
            send[d, 288:, :] = parts.astype(BF16)


def input_grad_kernel(lead, after, g_inner, cot, block, out):
    scale = lead_scales(lead)
    for row, v in enumerate(conv_rows(g_inner, 0, R // 2, block[...], TI)):
        source = own_row(row)
        for n in range(S):
            incoming = cot[n, source].astype(F32) * scale[n]
            out[n, source] = (v[16 * n : 16 * n + 16] + incoming).astype(BF16)


def two_of(v):
    high = v.astype(BF16).astype(F32)
    return [high, (v - high).astype(BF16).astype(F32)]


def bias_rows(total):
    return total[288:289] + total[289:290], total[290:291] + total[291:292]


def message(total):
    one, two = bias_rows(total)
    tail = two_of(one) + two_of(two) + [jnp.zeros((12, C), F32)]
    return jnp.concatenate([total[:288]] + tail, axis=0).astype(BF16)


def merge_kernel(keep, got, *outs):
    for k, out in enumerate(outs):
        d = lax.rem(lax.axis_index("dp") + k, 4)
        total = keep[d] + got[d].astype(F32)
        out[...] = message(total)


def column_kernel(*refs):
    total = sum(ref[...].astype(F32) for ref in refs[:-1])
    refs[-1][...] = message(total)


def plane_kernel(outputs, grad_inputs, *refs):
    parts, (own, sums, slots) = refs[:4], refs[4:]
    for n, part in enumerate(parts):
        slots[lax.rem(lax.axis_index("lon") + (4 - n), 4)] = part[...].astype(F32)
    total = sum(slots[n] for n in range(4))
    own[...] = total[:288]
    put_all(sums, [down(fold(total[:288] * total[:288])), *bias_rows(total), jnp.zeros((1, C), F32)])


def fetch_kernel(*refs):
    far, near, sems = refs[:6], refs[7:13], refs[13]
    copies = [pltpu.make_async_copy(far[n], near[n], sems.at[n]) for n in range(6)]
    for copy in copies:
        copy.start()
    for copy in copies:
        copy.wait()


def adam(weight, first, second, grad, rate, decay):
    first_new = BETA_ONE * first + (1.0 - BETA_ONE) * grad
    second_new = BETA_TWO * second + (1.0 - BETA_TWO) * grad * grad
    first_hat = first_new * (1.0 / (1.0 - BETA_ONE**STEP))
    second_hat = second_new * (1.0 / (1.0 - BETA_TWO**STEP))
    weight_new = weight - rate * (first_hat / (jnp.sqrt(second_hat) + ADAM_EPS) + decay * weight)
    return weight_new, first_new, second_new


def vector_grads(first_in, second_in, third_in, bias_one, bias_two, count):
    _, _, dgain_two, dshift_two = second_stats(second_in, count)
    _, _, dgain_one, dshift_one = first_back_stats(first_in, third_in, count)
    rows = [bias_one, sum(dgain_one), sum(dshift_one), bias_two, sum(dgain_two), sum(dshift_two)]
    return jnp.concatenate(rows, axis=0)


def update_kernel(count, *refs):
    weight, first, second, vectors, vec_first, vec_second = refs[:6]
    (mine, its), (sums_in, first_in, second_in, third_in), refs = refs[6:8], refs[8:12], refs[12:]
    norm_out, weight_new, first_new, second_new, weight_low, vectors_new, vec_first_new, vec_second_new = refs[:8]
    grad = refs[8]
    total = jnp.sum(sums_in[...], axis=0)
    half = sums_in[0]
    vec_grad = vector_grads(first_in, second_in, third_in, half[1:2], half[2:3], count)
    square = jnp.sum(total[0:1], axis=1, keepdims=True) + jnp.sum(
        down(vec_grad * vec_grad), axis=1, keepdims=True
    )
    norm = jnp.sqrt(square)
    norm_out[...] = norm
    clip = jnp.minimum(1.0, CLIP / (norm + 1e-06))
    core = lax.axis_index("lat")
    for k in range(2):
        for lat in range(2):
            for t in range(9):
                at = slice(144 * k + 16 * t, 144 * k + 16 * t + 16)
                grad[k, pl.ds(144 * lat + t, 16, stride=9), :] = jnp.where(core == lat, mine[at, :], its[at, :])
        new = adam(weight[k], first[k], second[k], grad[k] * clip, RATE_CONV, DECAY_CONV)
        weight_new[k], first_new[k], second_new[k] = new
        weight_low[k] = new[0].astype(BF16)
    width = vectors.shape[1]
    turned = pltpu.roll(
        jnp.concatenate([vec_grad, jnp.zeros((2, C), F32)], axis=0),
        lax.rem(C - lax.axis_index("dp") * width, C),
        axis=1,
    )
    new = adam(vectors[...], vec_first[...], vec_second[...], turned[:6, :width] * clip, RATE_VEC, 0.0)
    vectors_new[...], vec_first_new[...], vec_second_new[...] = new


def spread(block, axes):
    return lax.all_to_all(block, axes, 0, 0, tiled=True)


def turn(block, axis, by):
    size = lax.axis_size(axis)
    return lax.ppermute(block, axis, [(i, (i + by) % size) for i in range(size)])


def body(inputs, lead_time, cotangent, conv_weight, conv_first, conv_second, vectors, vec_first, vec_second):
    devices = lax.axis_size("dp") * lax.axis_size("lat") * lax.axis_size("lon")
    groups = lax.axis_size("dp")
    split = groups == 4 and lax.axis_size("lon") == 4
    count = float(PER * R * R * devices)
    size = conv_weight.shape[1] // 9
    flats = [pltpu.VMEM((FLAT, C), F32)] * 2
    conv_flops = 2 * T * 12 * C * 2 * C

    packed, lat_out = call(
        prep_kernel,
        [
            ((2, 9 * size + 16, C), BF16),
            ((S, 6, R, C), BF16),
        ],
        (inputs, cotangent, conv_weight, vectors),
        [
            pltpu.VMEM(conv_weight.shape, F32),
            pltpu.VMEM(vectors.shape, F32),
            pltpu.SemaphoreType.DMA((4,)),
        ],
        far=4,
    )
    lat_in = turn(lat_out, "lat", 1)
    edge_kinds = [((R + 4, MB, 16, C), BF16)] * 2
    x_near, cot_near, *edges = call(
        edge_kernel,
        [(inputs.shape, BF16)] * 2 + edge_kinds,
        (inputs, cotangent),
        [pltpu.SemaphoreType.DMA((2,))],
        far=2,
    )
    mine, far_r, far_l = call(
        beyond_kernel,
        [((9 * size + 16, C), BF16)] + edge_kinds,
        (lat_in, packed, *edges),
        aliases={2: 1, 3: 2},
    )
    far_left, far_right = turn(far_r, "lon", 1), turn(far_l, "lon", -1)
    dn, dn_sums = call(
        lead_kernel, [((R, TI, C), F32), ((8, C), F32)], (lead_time, cot_near), flops=10**8, scalars=1
    )
    cot_r, cot_l = call(later_kernel, [((R // 2 + 1, MB, 16, C), BF16)] * 2, (cot_near, lat_in))
    if split:
        fetched = [turn(mine, "dp", k) for k in range(1, groups)]
        *fetched, dn, cot_r, cot_l = lax.optimization_barrier((*fetched, dn, cot_r, cot_l))
        pieces = [packed]
        for piece in fetched:
            pieces += [piece, turn(piece, "lat", 1)]
    else:
        whole = lax.all_gather(packed, "dp")
        taps = whole[:, :, : 9 * size].reshape(groups, 2, 9, size, C).transpose(1, 2, 0, 3, 4)
        tail = jnp.sum(whole[:, :, 9 * size :], axis=0)
        pieces = [jnp.concatenate([taps.reshape(2, 9 * C, C), tail], axis=1)]
    block_one, vec = call(block_kernel, [((12 * C, 2 * C), BF16), ((16, C), F32)], pieces, flops=10**8)
    x_all, pre_one, sums_one = call(
        first_kernel,
        [((11, 2, TI, W3), BF16), ((R + 4, TI, C), F32), ((devices, MB, 2, C), F32)],
        (x_near, lat_in, far_left, far_right, block_one, vec),
        flats,
        flops=conv_flops * 6,
    )
    sums_one, dn = lax.optimization_barrier((sums_one, dn))
    got_one = spread(sums_one, ALL)
    block_two, two_back, one_back = call(
        weight_kernel,
        [((12 * C, 2 * C), BF16)] * 3,
        (got_one, block_one, *pieces),
        flops=10**8,
    )
    (pre_side,) = call(
        halo_kernel,
        [((R + 4, TH, C), F32)],
        (got_one, x_near, lat_in, far_left, far_right, block_one, vec),
        [pltpu.VMEM((11, 2, TH, W3), BF16)] + flats,
        flops=conv_flops * 4,
    )
    got_one, cot_r, cot_l = lax.optimization_barrier((got_one, cot_r, cot_l))
    cot_left, cot_right = turn(cot_r, "lon", 1), turn(cot_l, "lon", -1)
    n_all, pre_two, sums_two, stat_one = call(
        lambda *refs: second_kernel(count, *refs),
        [((10, 2, T, W3), BF16), ((R + 2, T, C), F32), ((devices, 3, 4, C), F32), ((8, C), F32)],
        (pre_one, pre_side, got_one, dn, dn_sums, block_two, vec),
        flats,
        flops=conv_flops * 9,
    )
    dn_lat, dn_side = call(
        lead_side_kernel,
        [((2, TI, C), F32), ((R + 2, TH, C), F32)],
        (lead_time, sums_two, lat_in, cot_left, cot_right),
        flats,
        flops=10**8,
        scalars=1,
    )
    sums_two, dn_lat, dn_side = lax.optimization_barrier((sums_two, dn_lat, dn_side))
    got_two = spread(sums_two, ALL)
    grad_two, mid, sums_three, stat_two, bias_two = call(
        lambda *refs: back_two_kernel(count, *refs),
        [((R, TI, C), BF16), ((R + 2, T, C), F32), ((devices, MB, 2, C), F32), ((4 * MB, C), F32), ((8, C), F32)],
        (pre_two, dn, dn_lat, dn_side, got_two, pre_one, two_back, vec),
        [pltpu.VMEM((10, 2, T, W3), BF16)] + flats,
        flops=conv_flops * 9,
    )
    got_three = spread(sums_three, ALL)
    grad_kinds = [((4, 304, C), F32), ((4, 304, C), BF16)] if split else [((2, 9, C, C), F32)]
    g_inner, bias_one, stat_three, *grads = call(
        lambda *refs: back_one_kernel(split, count, *refs),
        [((9, 2, TI, W3), BF16), ((8, C), F32), ((8, C), F32)] + grad_kinds,
        (pre_one, pre_side, mid, stat_one, got_three, x_all, n_all, grad_two, bias_two, vec),
        [pltpu.VMEM((3, C, W3), F32)] * 2 + flats,
        flops=conv_flops * 9,
    )

    def finish(after):
        (outputs,) = call(
            lambda *refs: output_kernel(count, *refs),
            [((S, R, R, C), BF16)],
            (after, inputs, pre_two, stat_two, vec),
            flops=10**8,
        )
        (grad_inputs,) = call(
            input_grad_kernel,
            [((S, R, R, C), BF16)],
            (lead_time, after, g_inner, cotangent, one_back),
            flops=conv_flops * 6,
            scalars=1,
        )
        return outputs, grad_inputs

    if split:
        merged = call(merge_kernel, [((304, C), BF16)] * 4, (grads[0], turn(grads[1], "lat", 1)))
        column = [merged[0]] + [turn(merged[k], "dp", k) for k in range(1, 4)]
        outputs, grad_inputs = finish(merged[0])
        (added_up,) = call(column_kernel, [((304, C), BF16)], column)
        row = [added_up] + [turn(added_up, "lon", k) for k in range(1, 4)]
        own, sums_four = call(
            plane_kernel,
            [((288, C), F32), ((2 * groups, 4, C), F32)],
            (outputs, grad_inputs, *row),
            [pltpu.VMEM((4, 304, C), F32)],
            far=2,
        )
        got_four = spread(sums_four, ("dp", "lat"))
        its = turn(own, "lat", 1)
        kinds = [((1, 1), F32)] + [(conv_weight.shape, F32)] * 3 + [(conv_weight.shape, BF16)]
        moments = (conv_weight, conv_first, conv_second, vectors, vec_first, vec_second)
        moments = call(
            fetch_kernel,
            [(moment.shape, F32) for moment in moments],
            (*moments, own),
            [pltpu.SemaphoreType.DMA((6,))],
            flops=10**10,
            far=6,
        )
        norm, *news = call(
            lambda *refs: update_kernel(count, *refs),
            kinds + [(vectors.shape, F32)] * 3,
            (*moments, own, its, got_four, stat_one, stat_two, stat_three),
            [pltpu.VMEM(conv_weight.shape, F32)],
        )
        return (outputs, grad_inputs, norm.reshape(()), *news)
    outputs, grad_inputs = finish(bias_one)
    stacked = grads[0].transpose(0, 2, 1, 3).reshape(2, 9 * C, C)
    conv_total, total_one, total_two = lax.psum((stacked, bias_one[0:1], bias_two[0:1]), ALL)
    vec_total = vector_grads(stat_one, stat_two, stat_three, total_one, total_two, count)
    grad_norm = jnp.sqrt(jnp.sum(conv_total * conv_total) + jnp.sum(vec_total * vec_total))
    clip = jnp.minimum(1.0, CLIP / (grad_norm + 1e-06))
    index = lax.axis_index("dp")
    conv_own = lax.dynamic_slice_in_dim(conv_total, index * conv_weight.shape[1], conv_weight.shape[1], 1)
    vec_own = lax.dynamic_slice_in_dim(vec_total, index * vectors.shape[1], vectors.shape[1], 1)
    conv_news = adam(conv_weight, conv_first, conv_second, conv_own * clip, RATE_CONV, DECAY_CONV)
    vec_news = adam(vectors, vec_first, vec_second, vec_own * clip, RATE_VEC, 0.0)
    return (outputs, grad_inputs, grad_norm, *conv_news, conv_news[0].astype(BF16), *vec_news)


def solution(mesh):
    grid = P("dp", "lat", "lon", None)
    rows = P(None, "dp", None)
    columns = P(None, "dp")
    in_specs = (grid, P("dp"), grid, rows, rows, rows, columns, columns, columns)
    out_specs = (grid, grid, P(), rows, rows, rows, rows, columns, columns, columns)
    return jax.shard_map(body, mesh=mesh, in_specs=in_specs, out_specs=out_specs, check_vma=False)
```

```python
import math

import jax
import jax.numpy as jnp
from jax import lax
from jax.experimental import pallas as pl
from jax.experimental.pallas import tpu as pltpu
from jax.sharding import PartitionSpec as P

MB = 3
STEP = 5
EPS = 1e-05
CLIP = 1.0
BETA_ONE = 0.5
BETA_TWO = 0.5
RATE_CONV = 0.03
RATE_VEC = 0.3
DECAY_CONV = 0.01
ADAM_EPS = 1e-08
ALL = ("dp", "lat", "lon")
F32 = jnp.float32
BF16 = jnp.bfloat16
GELU_A = math.sqrt(2.0 / math.pi)
GELU_B = GELU_A * 0.044715

S, R, C = 12, 16, 128
TI = S * R
NH = S + 1
TH = 8 * (NH + NH % 2)
T = TI + TH
W3 = 3 * C
PER = S // MB
FLAT = 24 + 24 * S
VM = pl.BlockSpec(memory_space=pltpu.VMEM)
SM = pl.BlockSpec(memory_space=pltpu.SMEM)
FAR = pl.BlockSpec(memory_space=pltpu.HBM)


def call(kernel, outs, args, scratch=(), flops=0, limit=16, scalars=0, far=0, far_out=(), aliases=None):
    args = [
        pltpu.with_memory_space_constraint(arg, pltpu.HBM) if scalars <= n < scalars + far else arg
        for n, arg in enumerate(args)
    ]
    spaces = [SM] * scalars + [FAR] * far + [VM] * (len(args) - scalars - far)
    return pl.pallas_call(
        kernel,
        out_shape=tuple(
            pltpu.HBM(shape, kind) if n in far_out else jax.ShapeDtypeStruct(shape, kind)
            for n, (shape, kind) in enumerate(outs)
        ),
        in_specs=spaces,
        out_specs=tuple(FAR if n in far_out else VM for n in range(len(outs))),
        scratch_shapes=list(scratch),
        input_output_aliases=aliases or {},
        compiler_params=pltpu.CompilerParams(vmem_limit_bytes=limit << 20),
        cost_estimate=pl.CostEstimate(
            flops=flops,
            transcendentals=0,
            bytes_accessed=sum(math.prod(a.shape) * a.dtype.itemsize for a in args),
        ),
    )(*args)


def own_row(row):
    return jnp.where(lax.axis_index("lat") == 0, row, R - 1 - row)


def own_tap(tap):
    return jnp.where(lax.axis_index("lat") == 0, tap, 2 - tap)


def act(v):
    return 0.5 * v * (1.0 + jnp.tanh(v * (GELU_A + GELU_B * (v * v))))


def act_both(v):
    sq = v * v
    tan = jnp.tanh(v * (GELU_A + GELU_B * sq))
    half = 0.5 * (1.0 + tan)
    value = v * half
    slope = half + value * (1.0 - tan) * (GELU_A + (3.0 * GELU_B) * sq)
    return value, slope


def fold(v):
    return jnp.sum(v.reshape(v.shape[0] // 8, 8, C), axis=0)


def down(v):
    return jnp.sum(v, axis=0, keepdims=True)


def batch_sums(values):
    return [fold(values[PER * R * m : PER * R * (m + 1)]) for m in range(MB)]


def build(flat, out, place, tile, side):
    for n in range(S):
        value = tile(n)
        flat[16 + 24 * n : 32 + 24 * n, :] = value
        out[place + (slice(16 * n, 16 * n + 16), slice(C, 2 * C))] = value.astype(BF16)
    whole = out.shape[-2] == T
    for p in range(TH // 16):
        pair = [side(h) if h < NH else jnp.zeros((8, C), F32) for h in (2 * p, 2 * p + 1)]
        for h, value in zip((2 * p, 2 * p + 1), pair):
            if h < NH:
                flat[8 + 24 * h : 16 + 24 * h, :] = value
        if whole:
            at = TI + 16 * p
            out[place + (slice(at, at + 16), slice(C, 2 * C))] = jnp.concatenate(pair, axis=0).astype(BF16)
    emit_sides(flat, out, place)


def emit_sides(flat, out, place):
    for kx in (0, 2):
        columns = slice(C * kx, C * kx + C)
        for n in range(S):
            at = 15 + 24 * n + kx
            out[place + (slice(16 * n, 16 * n + 16), columns)] = flat[at : at + 16, :].astype(BF16)
        if out.shape[-2] != T:
            continue
        for p in range(TH // 16):
            at = 7 + 48 * p + kx
            first = flat[at : at + 8, :]
            second = flat[at + 24 : at + 32, :] if 2 * p + 1 < NH else jnp.zeros((8, C), F32)
            out[place + (slice(TI + 16 * p, TI + 16 * p + 16), columns)] = jnp.concatenate(
                [first, second], axis=0
            ).astype(BF16)


def place_of(i, odd):
    return (i + odd, 1 - odd)


def sided(rows):
    mixed = {}
    for h in range(NH):
        low, high = max(h - 1, 0) // PER, min(h, S - 1) // PER
        if low != high:
            mixed[h] = jnp.concatenate(
                [jnp.broadcast_to(rows[low], (4, C)), jnp.broadcast_to(rows[high], (4, C))], axis=0
            )
    return (
        lambda n: rows[n // PER],
        lambda h: mixed[h] if h in mixed else rows[min(h, S - 1) // PER],
    )


def put_all(ref, rows):
    block = jnp.concatenate(rows, axis=0)
    ref[...] = jnp.broadcast_to(block[None], ref.shape)


def put_pairs(ref, rows):
    for g in range(ref.shape[1]):
        part = jnp.concatenate(rows[2 * g : 2 * g + 2], axis=0)
        for n in range(ref.shape[0]):
            ref[n, g] = part


def got_pairs(ref):
    total = jnp.sum(ref[...], axis=0)
    return [total[g, i : i + 1] for g in range(total.shape[0]) for i in range(2)]


def taken(ref, count):
    return [ref[i : i + 1, :] for i in range(count)]


def vec_rows(ref):
    return [ref[i : i + 1, :] for i in range(6)]


def norm_of(sums, count):
    means = [sums[m] * (1.0 / count) for m in range(MB)]
    inverses = [lax.rsqrt(sums[MB + m] * (1.0 / count) - means[m] * means[m] + EPS) for m in range(MB)]
    return means, inverses


def piece_of(pieces, k, which, rows):
    if k == 0:
        return pieces[0][which, rows, :]
    mine, other = pieces[2 * k - 1], pieces[2 * k]
    return jnp.where(lax.axis_index("lat") == which, mine[rows, :], other[rows, :])


def fill_forward(block, pieces, which):
    count = (len(pieces) + 1) // 2
    size = C // count
    zero = jnp.zeros((C, C), BF16)
    for kx in range(3):
        block[C * kx : C * kx + C, C:] = zero
        block[C * (9 + kx) : C * (10 + kx), :C] = zero
        for ky in range(3):
            source = pl.multiple_of((3 * own_tap(ky) + kx) * size, size)
            for k in range(count):
                owner = lax.rem(lax.axis_index("dp") + (count - k), count) if count > 1 else 0
                part = piece_of(pieces, k, which, pl.ds(source, size))
                for a in range(2):
                    top = pl.multiple_of((3 * (ky + a) + kx) * C + owner * size, size)
                    block[pl.ds(top, size), a * C : a * C + C] = part


def fill_backward(block, forward):
    zero = jnp.zeros((C, C), BF16)
    for kx in range(3):
        block[C * kx : C * kx + C, C:] = zero
        block[C * (9 + kx) : C * (10 + kx), :C] = zero
        for ky in range(3):
            source = (3 * (2 - ky) + 2 - kx) * C
            part = forward[source : source + C, :C].T
            for a in range(2):
                top = (3 * (ky + a) + kx) * C
                block[top : top + C, a * C : a * C + C] = part


def conv_rows(ref, low, high, weight, rows=T):
    pairs = [
        jnp.concatenate([ref[i, 0, :rows], ref[i, 1, :rows], ref[i + 1, 0, :rows], ref[i + 1, 1, :rows]], axis=1)
        for i in range(low, high)
    ]
    got = jnp.dot(jnp.concatenate(pairs, axis=0), weight, preferred_element_type=F32)
    return [
        got[n * rows : n * rows + rows, a * C : a * C + C] for n in range(high - low) for a in range(2)
    ]


def staggered(make, conv, rows, groups):
    total, done = None, 0
    stops = [min(2 * high + 1, rows) for _, high in groups]
    for n, (low, high) in enumerate(groups):
        for row in range(done, stops[n]):
            make(row)
        done = max(done, stops[n])
        total = conv(low, high, total)
        for row in range(done, stops[min(n + 1, len(groups) - 1)]):
            make(row)
        done = stops[min(n + 1, len(groups) - 1)]
    return total


def in_pairs(high):
    return [(low, min(low + 2, high)) for low in range(0, high, 2)]


def added(total, new):
    return new if total is None else [old + more for old, more in zip(total, new)]


def pack_taps(weight, out):
    size = weight.shape[0] // 9
    for t in range(9):
        out[size * t : size * t + size, :] = weight[pl.ds(t, size, stride=9), :].astype(BF16)


def prep_kernel(x, cot, weight, vectors, packed, lat_out, held, held_vec, sems):
    last = lax.axis_index("lat") == 0
    copies = [
        pltpu.make_async_copy(weight, held, sems.at[0]),
        pltpu.make_async_copy(vectors, held_vec, sems.at[1]),
        pltpu.make_async_copy(x.at[:, pl.ds(jnp.where(last, R - 4, 0), 4)], lat_out.at[:, 0:4], sems.at[2]),
        pltpu.make_async_copy(cot.at[:, pl.ds(jnp.where(last, R - 2, 0), 2)], lat_out.at[:, 4:6], sems.at[3]),
    ]
    for copy in copies:
        copy.start()
    for copy in copies[:2]:
        copy.wait()
    size = 9 * (weight.shape[1] // 9)
    width = vectors.shape[1]
    pick = lax.broadcasted_iota(jnp.int32, (width, C), 1) - lax.axis_index("dp") * width
    pick = jnp.where(pick == lax.broadcasted_iota(jnp.int32, (width, C), 0), 1.0, 0.0).astype(BF16)
    placed = jnp.dot(held_vec[...].astype(BF16), pick, preferred_element_type=F32)
    for k in range(2):
        pack_taps(held.at[k], packed.at[k])
        packed[k, size:, :] = jnp.concatenate([placed, jnp.zeros((10, C), F32)], axis=0).astype(BF16)
    for copy in copies[2:]:
        copy.wait()


def x_beyond(lat_in, n, k):
    return lat_in[n, jnp.where(lax.axis_index("lat") == 0, k, 3 - k)]


def cot_beyond(lat_in, n, k):
    return lat_in[n, jnp.where(lax.axis_index("lat") == 0, 4 + k, 5 - k)]


def cut_far(tile, far_r, far_l, at, columns, rows):
    for m in range(MB):
        tiles = [tile(q, n).astype(F32) for q in range(rows) for n in range(PER * m, PER * m + PER)]
        far_r[at, m] = jnp.concatenate([v[R - columns :] for v in tiles], axis=0).astype(BF16)
        far_l[at, m] = jnp.concatenate([v[:columns] for v in tiles], axis=0).astype(BF16)


def edge_kernel(x_far, cot_far, x, cot, far_r, far_l, sems):
    copies = [pltpu.make_async_copy(x_far, x, sems.at[0]), pltpu.make_async_copy(cot_far, cot, sems.at[1])]
    for copy in copies:
        copy.start()
    copies[0].wait()

    @pl.loop(0, R // 2)
    def _(i):
        for q in range(2):
            cut_far(lambda _, n: x[n, own_row(2 * i + q)], far_r, far_l, 2 * i + q, 4, 1)

    copies[1].wait()


def beyond_kernel(lat_in, packed, right_in, left_in, mine, far_r, far_l):
    for k in range(4):
        cut_far(lambda _, n: x_beyond(lat_in, n, k), far_r, far_l, R + k, 4, 1)
    mine[...] = packed[lax.axis_index("lat")]


def later_kernel(cot, lat_in, far_r, far_l):
    @pl.loop(0, R // 2)
    def _(i):
        cut_far(lambda q, n: cot[n, own_row(2 * i + q)], far_r, far_l, i, 2, 2)

    cut_far(lambda q, n: cot_beyond(lat_in, n, q), far_r, far_l, R // 2, 2, 2)


def own_tile(x, lat_in, row):
    if row < R:
        return lambda n: x[n, own_row(row)]
    return lambda n: x_beyond(lat_in, n, row - R)


def first_kernel(x, lat_in, from_left, from_right, block, vec, out, pre, sums, *flats):
    for edge in (0, R + 5):
        out[edge // 2, edge % 2] = jnp.zeros((TI, W3), BF16)
    bias = vec[0:1, :]

    def make(row):
        flat, place, tile = flats[row % 2], place_of(row // 2, row % 2), own_tile(x, lat_in, row)
        for m in range(MB):
            left, right = from_left[row, m].astype(F32), from_right[row, m].astype(F32)
            for n in range(PER):
                s = PER * m + n
                flat[15 + 24 * s : 16 + 24 * s, :] = left[4 * n + 3 : 4 * n + 4]
                flat[32 + 24 * s : 33 + 24 * s, :] = right[4 * n : 4 * n + 1]
        for n in range(S):
            value = tile(n)
            flat[16 + 24 * n : 32 + 24 * n, :] = value.astype(F32)
            out[place + (slice(16 * n, 16 * n + 16), slice(C, 2 * C))] = value
        emit_sides(flat, out, place)

    def conv(low, high, total):
        for n, v in enumerate(conv_rows(out, low, high, block[...], TI)):
            row = 2 * low + n
            pre[row] = v + bias
            if row < R:
                value = act(v + bias)
                total = added(total, batch_sums(value) + batch_sums(value * value))
        return total

    total = staggered(make, conv, R + 4, in_pairs(R // 2 + 2))
    put_pairs(sums, [down(v) for v in total])


def halo_kernel(after, x, lat_in, from_left, from_right, block, vec, pre, halo, *flats):
    for flat in flats:
        flat[...] = jnp.zeros(flat.shape, F32)
    for edge in (0, R + 5):
        halo[edge // 2, edge % 2] = jnp.zeros((TH, W3), BF16)

    def make(row):
        flat, place, tile = flats[row % 2], place_of(row // 2, row % 2), own_tile(x, lat_in, row)
        for m in range(MB):
            left, right = from_left[row, m].astype(F32), from_right[row, m].astype(F32)
            for n in range(PER):
                s = PER * m + n
                value = tile(s).astype(F32)
                flat[12 + 24 * s : 16 + 24 * s, :] = left[4 * n : 4 * n + 4]
                flat[16 + 24 * s : 24 + 24 * s, :] = value[:8]
                flat[24 + 24 * s : 32 + 24 * s, :] = value[8:]
                flat[32 + 24 * s : 36 + 24 * s, :] = right[4 * n : 4 * n + 4]
        for kx in range(3):
            for p in range(TH // 16):
                at = 7 + 48 * p + kx
                second = flat[at + 24 : at + 32, :] if 2 * p + 1 < NH else jnp.zeros((8, C), F32)
                halo[place + (slice(16 * p, 16 * p + 16), slice(C * kx, C * kx + C))] = jnp.concatenate(
                    [flat[at : at + 8, :], second], axis=0
                ).astype(BF16)

    def conv(low, high, total):
        for n, v in enumerate(conv_rows(halo, low, high, block[...], TH)):
            pre[2 * low + n] = v + vec[0:1, :]
        return total

    staggered(make, conv, R + 4, ((0, 3), (3, 6), (6, 10)))


def lead_scales(lead):
    return [0.5 * jnp.sqrt(jnp.full((1, C), lead[n], jnp.int32).astype(F32)) for n in range(S)]


def lead_kernel(lead, cot, dn, sums):
    scale = lead_scales(lead)

    def body(i, total):
        for odd in range(2):
            row = 2 * i + odd
            source = own_row(row)
            values = [cot[n, source].astype(F32) * scale[n] for n in range(S)]
            for n in range(S):
                dn[row, 16 * n : 16 * n + 16, :] = values[n]
            new = [sum(fold(values[n]) for n in range(PER * m, PER * m + PER)) for m in range(MB)]
            total = added(total, new)
        return total

    total = lax.fori_loop(0, R // 2, body, [jnp.zeros((8, C), F32)] * MB)
    sums[...] = jnp.concatenate([down(v) for v in total] + [jnp.zeros((8 - MB, C), F32)], axis=0)


def block_kernel(*rest):
    pieces, (block, vec) = rest[:-2], rest[-2:]
    fill_forward(block, pieces, 0)
    last = pieces[0].shape[1]
    vec[...] = sum(
        piece_of(pieces, k, 0, slice(last - 16, last)).astype(F32) for k in range((len(pieces) + 1) // 2)
    )


def weight_kernel(after, block_one, *rest):
    pieces, (block_two, two_back, one_back) = rest[:-3], rest[-3:]
    fill_forward(block_two, pieces, 1)
    fill_backward(two_back, block_two)
    fill_backward(one_back, block_one)


def second_kernel(count, pre, pre_side, sums_in, dn, dn_sums, block, vec_in, n_all, pre_two, sums, kept, *flats):
    vec = vec_rows(vec_in)
    kept[...] = jnp.concatenate(got_pairs(sums_in) + [jnp.zeros((2, C), F32)], axis=0)
    means, inverses = norm_of(taken(kept, 2 * MB), count)
    gains = [inverses[m] * vec[1] for m in range(MB)]
    gain, gain_side = sided(gains)
    shift, shift_side = sided([vec[2] - means[m] * gains[m] for m in range(MB)])
    for flat in flats:
        flat[...] = jnp.zeros(flat.shape, F32)
    n_all[0, 0] = jnp.zeros((T, W3), BF16)

    def one(i, odd):
        row = 2 * i + odd
        build(
            flats[odd],
            n_all,
            place_of(i, odd),
            lambda n: act(pre[row, 16 * n : 16 * n + 16, :]) * gain(n) + shift(n),
            lambda h: act(pre_side[row, 8 * h : 8 * h + 8, :]) * gain_side(h) + shift_side(h),
        )

    def conv(low, high, total):
        for n, v in enumerate(conv_rows(n_all, low, high, block[...])):
            row = 2 * low + n
            pre_two[row] = v + vec[3]
            if row < R:
                value = act(v[:TI] + vec[3])
                new = batch_sums(value) + batch_sums(value * value) + batch_sums(value * dn[row])
                total = added(total, new)
        return total

    total = staggered(lambda row: one(row // 2, row % 2), conv, R + 3, in_pairs(R // 2 + 1))
    block_out = jnp.concatenate([down(v) for v in total] + [dn_sums[0:MB, :]], axis=0)
    for g in range(3):
        part = block_out[4 * g : 4 * g + 4]
        for n in range(sums.shape[0]):
            sums[n, g] = part


def second_stats(sums_in, count):
    rows = taken(sums_in, 4 * MB)
    means, inverses = norm_of(rows[: 2 * MB], count)
    dots, plain = rows[2 * MB : 3 * MB], rows[3 * MB :]
    dgain = [inverses[m] * (dots[m] - means[m] * plain[m]) for m in range(MB)]
    return means, inverses, dgain, plain


def back_terms(means, inverses, gain, dgain, dshift, count):
    lin = [inverses[m] * gain for m in range(MB)]
    slope = [-lin[m] * inverses[m] * (dgain[m] * (1.0 / count)) for m in range(MB)]
    const = [-lin[m] * (dshift[m] * (1.0 / count)) - slope[m] * means[m] for m in range(MB)]
    return [sided(rows) for rows in (lin, const, slope)]


def build_back(flat, out, place, terms, pre_tile, tile, pre_side, side):
    def at(pre, incoming, which, index):
        value, deriv = act_both(pre(index))
        lin, const, slope = [term[which](index) for term in terms]
        return deriv * (lin * incoming(index) + const + slope * value)

    build(flat, out, place, lambda n: at(pre_tile, tile, 0, n), lambda h: at(pre_side, side, 1, h))


def back_two_kernel(
    count, lead, pre_two, dn, lat_in, from_left, from_right, sums_in, pre, block, vec, grad, mid, sums, kept, bias_two, g_all, *flats
):
    total = jnp.sum(sums_in[...], axis=0)
    kept[...] = jnp.concatenate([total[g, i : i + 1] for g in range(MB) for i in range(4)], axis=0)
    means, inverses, dgain, dshift = second_stats(kept, count)
    terms = back_terms(means, inverses, vec[4:5, :], dgain, dshift, count)
    for flat in flats:
        flat[...] = jnp.zeros(flat.shape, F32)
    for edge in (0, R + 3):
        g_all[edge // 2, edge % 2] = jnp.zeros((T, W3), BF16)

    scale = lead_scales(lead)
    sides = flats[2:]

    def make(row):
        odd, i = row % 2, row // 2
        for m in range(MB):
            left, right = from_left[i, m].astype(F32), from_right[i, m].astype(F32)
            for n in range(PER):
                s, at = PER * m + n, 8 * odd + 2 * n
                sides[odd][14 + 24 * s : 16 + 24 * s, :] = left[at : at + 2] * scale[s]
                sides[odd][32 + 24 * s : 34 + 24 * s, :] = right[at : at + 2] * scale[s]
        if row < R:
            incoming = lambda n: dn[row, 16 * n : 16 * n + 16, :]
        else:
            incoming = lambda n: cot_beyond(lat_in, n, row - R).astype(F32) * scale[n]
        build_back(
            flats[odd],
            g_all,
            place_of(i, odd),
            terms,
            lambda n: pre_two[row, 16 * n : 16 * n + 16, :],
            incoming,
            lambda h: pre_two[row, TI + 8 * h : TI + 8 * h + 8, :],
            lambda h: sides[odd][8 + 24 * h : 16 + 24 * h, :],
        )

    biases = []

    def row_of(row):
        make(row)
        if row < R:
            own = g_all[place_of(row // 2, row % 2) + (slice(0, TI), slice(C, 2 * C))]
            grad[row] = own
            biases.append(fold(own.astype(F32)))

    def conv(low, high, total):
        for n, v in enumerate(conv_rows(g_all, low, high, block[...])):
            row = 2 * low + n
            mid[row] = v
            if row < R:
                own = v[:TI]
                total = added(total, batch_sums(own) + batch_sums(own * act(pre[row])))
        return total

    total = staggered(row_of, conv, R + 2, in_pairs(R // 2 + 1))
    bias = sum(biases)
    put_pairs(sums, [down(v) for v in total])
    bias_two[...] = jnp.concatenate([down(bias), jnp.zeros((7, C), F32)], axis=0)


def wgrad_add(acc, inner, grad, low, high):
    left = jnp.concatenate([grad(row) for row in range(low, high)], axis=0)
    right = jnp.concatenate(
        [
            jnp.concatenate([inner[(row + ky) // 2, (row + ky) % 2, :TI] for ky in range(3)], axis=1)
            for row in range(low, high)
        ],
        axis=0,
    )
    part = lax.dot_general(left, right, (((0,), (0,)), ((), ())), preferred_element_type=F32)
    for ky in range(3):
        own = part[:, W3 * ky : W3 * ky + W3]
        acc[ky] = own if low == 0 else acc[ky] + own


def split_out(acc, which, keep, send):
    first = lax.axis_index("lat") == 0
    for ky in range(3):
        for kx in range(3):
            at = pl.ds(pl.multiple_of(144 * which + 16 * (3 * own_tap(ky) + kx), 16), 16)
            taps = acc[ky, :, C * kx : C * kx + C].T
            for d in range(4):
                low, high = taps[32 * d : 32 * d + 16], taps[32 * d + 16 : 32 * d + 32]
                keep[d, at, :] = jnp.where(first, low, high)
                send[d, at, :] = jnp.where(first, high, low).astype(BF16)


def plain_out(acc, which, out):
    for ky in range(3):
        for kx in range(3):
            out[which, 3 * own_tap(ky) + kx] = acc[ky, :, C * kx : C * kx + C].T


def output_kernel(count, after, x, pre_two, sums_in, vec_in, out):
    vec = vec_rows(vec_in)
    means, inverses, _, _ = second_stats(sums_in, count)
    gains = [inverses[m] * vec[4] for m in range(MB)]
    shifts = [vec[5] - means[m] * gains[m] for m in range(MB)]

    @pl.loop(0, R)
    def _(row):
        source = own_row(row)
        for s in range(S):
            value = act(pre_two[row, 16 * s : 16 * s + 16, :])
            out[s, source] = (x[s, source].astype(F32) + value * gains[s // PER] + shifts[s // PER]).astype(BF16)


def first_back_stats(first_in, sums_in, count):
    means, inverses = norm_of(taken(first_in, 2 * MB), count)
    rows = taken(sums_in, 2 * MB)
    dshift = rows[:MB]
    dgain = [inverses[m] * (rows[MB + m] - means[m] * dshift[m]) for m in range(MB)]
    return means, inverses, dgain, dshift


def back_one_kernel(split, count, pre, pre_side, mid, first_in, sums_in, x_all, n_all, grad_two, bias_two, vec, g_inner, bias, kept, *rest):
    outs, (acc_one, acc_two), flats = rest[:-4], rest[-4:-2], rest[-2:]
    kept[...] = jnp.concatenate(got_pairs(sums_in) + [jnp.zeros((2, C), F32)], axis=0)
    means, inverses, dgain, dshift = first_back_stats(first_in, kept, count)
    terms = back_terms(means, inverses, vec[1:2, :], dgain, dshift, count)
    for flat in flats:
        flat[...] = jnp.zeros(flat.shape, F32)
    g_inner[0, 0] = jnp.zeros((TI, W3), BF16)

    def make(row):
        build_back(
            flats[row % 2],
            g_inner,
            ((row + 1) // 2, (row + 1) % 2),
            terms,
            lambda n: pre[row, 16 * n : 16 * n + 16, :],
            lambda n: mid[row, 16 * n : 16 * n + 16, :],
            lambda h: pre_side[row, 8 * h : 8 * h + 8, :],
            lambda h: mid[row, TI + 8 * h : TI + 8 * h + 8, :],
        )

    def made(row):
        return g_inner[(row + 1) // 2, (row + 1) % 2, :, C : 2 * C]

    total = jnp.zeros((8, C), F32)
    for row in range(R + 1):
        make(row)
        if row < R:
            total = total + fold(made(row).astype(F32))
    for low in range(0, R, 4):
        wgrad_add(acc_two, n_all, lambda row: grad_two[row], low, low + 4)
        wgrad_add(acc_one, x_all, made, low, low + 4)
    bias[...] = jnp.concatenate([down(total), jnp.zeros((7, C), F32)], axis=0)
    (split_out if split else plain_out)(acc_two, 1, *outs)
    (split_out if split else plain_out)(acc_one, 0, *outs)
    if split:
        keep, send = outs
        parts = jnp.concatenate(two_of(down(total)) + two_of(bias_two[0:1, :]) + [jnp.zeros((12, C), F32)], axis=0)
        for d in range(4):
            keep[d, 288:, :] = parts
            send[d, 288:, :] = parts.astype(BF16)


def input_grad_kernel(lead, after, g_inner, cot, block, out):
    scale = lead_scales(lead)
    for row, v in enumerate(conv_rows(g_inner, 0, R // 2, block[...], TI)):
        source = own_row(row)
        for n in range(S):
            incoming = cot[n, source].astype(F32) * scale[n]
            out[n, source] = (v[16 * n : 16 * n + 16] + incoming).astype(BF16)


def two_of(v):
    high = v.astype(BF16).astype(F32)
    return [high, (v - high).astype(BF16).astype(F32)]


def bias_rows(total):
    return total[288:289] + total[289:290], total[290:291] + total[291:292]


def message(total):
    one, two = bias_rows(total)
    tail = two_of(one) + two_of(two) + [jnp.zeros((12, C), F32)]
    return jnp.concatenate([total[:288]] + tail, axis=0).astype(BF16)


def merge_kernel(keep, got, *outs):
    for k, out in enumerate(outs):
        d = lax.rem(lax.axis_index("dp") + k, 4)
        total = keep[d] + got[d].astype(F32)
        out[...] = message(total)


def column_kernel(*refs):
    total = sum(ref[...].astype(F32) for ref in refs[:-1])
    refs[-1][...] = message(total)


def plane_kernel(outputs, grad_inputs, *refs):
    parts, (own, sums, slots) = refs[:4], refs[4:]
    for n, part in enumerate(parts):
        slots[lax.rem(lax.axis_index("lon") + (4 - n), 4)] = part[...].astype(F32)
    total = sum(slots[n] for n in range(4))
    own[...] = total[:288]
    put_all(sums, [down(fold(total[:288] * total[:288])), *bias_rows(total), jnp.zeros((1, C), F32)])


def fetch_kernel(*refs):
    far, near, sems = refs[:6], refs[7:13], refs[13]
    copies = [pltpu.make_async_copy(far[n], near[n], sems.at[n]) for n in range(6)]
    for copy in copies:
        copy.start()
    for copy in copies:
        copy.wait()


def adam(weight, first, second, grad, rate, decay):
    first_new = BETA_ONE * first + (1.0 - BETA_ONE) * grad
    second_new = BETA_TWO * second + (1.0 - BETA_TWO) * grad * grad
    first_hat = first_new * (1.0 / (1.0 - BETA_ONE**STEP))
    second_hat = second_new * (1.0 / (1.0 - BETA_TWO**STEP))
    weight_new = weight - rate * (first_hat / (jnp.sqrt(second_hat) + ADAM_EPS) + decay * weight)
    return weight_new, first_new, second_new


def vector_grads(first_in, second_in, third_in, bias_one, bias_two, count):
    _, _, dgain_two, dshift_two = second_stats(second_in, count)
    _, _, dgain_one, dshift_one = first_back_stats(first_in, third_in, count)
    rows = [bias_one, sum(dgain_one), sum(dshift_one), bias_two, sum(dgain_two), sum(dshift_two)]
    return jnp.concatenate(rows, axis=0)


def update_kernel(count, *refs):
    weight, first, second, vectors, vec_first, vec_second = refs[:6]
    (mine, its), (sums_in, first_in, second_in, third_in), refs = refs[6:8], refs[8:12], refs[12:]
    norm_out, weight_new, first_new, second_new, weight_low, vectors_new, vec_first_new, vec_second_new = refs[:8]
    grad = refs[8]
    total = jnp.sum(sums_in[...], axis=0)
    half = sums_in[0]
    vec_grad = vector_grads(first_in, second_in, third_in, half[1:2], half[2:3], count)
    square = jnp.sum(total[0:1], axis=1, keepdims=True) + jnp.sum(
        down(vec_grad * vec_grad), axis=1, keepdims=True
    )
    norm = jnp.sqrt(square)
    norm_out[...] = norm
    clip = jnp.minimum(1.0, CLIP / (norm + 1e-06))
    core = lax.axis_index("lat")
    for k in range(2):
        for lat in range(2):
            for t in range(9):
                at = slice(144 * k + 16 * t, 144 * k + 16 * t + 16)
                grad[k, pl.ds(144 * lat + t, 16, stride=9), :] = jnp.where(core == lat, mine[at, :], its[at, :])
        new = adam(weight[k], first[k], second[k], grad[k] * clip, RATE_CONV, DECAY_CONV)
        weight_new[k], first_new[k], second_new[k] = new
        weight_low[k] = new[0].astype(BF16)
    width = vectors.shape[1]
    turned = pltpu.roll(
        jnp.concatenate([vec_grad, jnp.zeros((2, C), F32)], axis=0),
        lax.rem(C - lax.axis_index("dp") * width, C),
        axis=1,
    )
    new = adam(vectors[...], vec_first[...], vec_second[...], turned[:6, :width] * clip, RATE_VEC, 0.0)
    vectors_new[...], vec_first_new[...], vec_second_new[...] = new


def spread(block, axes):
    return lax.all_to_all(block, axes, 0, 0, tiled=True)


def turn(block, axis, by):
    size = lax.axis_size(axis)
    return lax.ppermute(block, axis, [(i, (i + by) % size) for i in range(size)])


def body(inputs, lead_time, cotangent, conv_weight, conv_first, conv_second, vectors, vec_first, vec_second):
    devices = lax.axis_size("dp") * lax.axis_size("lat") * lax.axis_size("lon")
    groups = lax.axis_size("dp")
    split = groups == 4 and lax.axis_size("lon") == 4
    count = float(PER * R * R * devices)
    size = conv_weight.shape[1] // 9
    flats = [pltpu.VMEM((FLAT, C), F32)] * 2
    conv_flops = 2 * T * 12 * C * 2 * C

    packed, lat_out = call(
        prep_kernel,
        [
            ((2, 9 * size + 16, C), BF16),
            ((S, 6, R, C), BF16),
        ],
        (inputs, cotangent, conv_weight, vectors),
        [
            pltpu.VMEM(conv_weight.shape, F32),
            pltpu.VMEM(vectors.shape, F32),
            pltpu.SemaphoreType.DMA((4,)),
        ],
        far=4,
    )
    lat_in = turn(lat_out, "lat", 1)
    edge_kinds = [((R + 4, MB, 16, C), BF16)] * 2
    x_near, cot_near, *edges = call(
        edge_kernel,
        [(inputs.shape, BF16)] * 2 + edge_kinds,
        (inputs, cotangent),
        [pltpu.SemaphoreType.DMA((2,))],
        far=2,
    )
    mine, far_r, far_l = call(
        beyond_kernel,
        [((9 * size + 16, C), BF16)] + edge_kinds,
        (lat_in, packed, *edges),
        aliases={2: 1, 3: 2},
    )
    far_left, far_right = turn(far_r, "lon", 1), turn(far_l, "lon", -1)
    dn, dn_sums = call(
        lead_kernel, [((R, TI, C), F32), ((8, C), F32)], (lead_time, cot_near), flops=10**8, scalars=1
    )
    cot_r, cot_l = call(later_kernel, [((R // 2 + 1, MB, 16, C), BF16)] * 2, (cot_near, lat_in))
    if split:
        fetched = [turn(mine, "dp", k) for k in range(1, groups)]
        *fetched, dn, cot_r, cot_l = lax.optimization_barrier((*fetched, dn, cot_r, cot_l))
        pieces = [packed]
        for piece in fetched:
            pieces += [piece, turn(piece, "lat", 1)]
    else:
        whole = lax.all_gather(packed, "dp")
        taps = whole[:, :, : 9 * size].reshape(groups, 2, 9, size, C).transpose(1, 2, 0, 3, 4)
        tail = jnp.sum(whole[:, :, 9 * size :], axis=0)
        pieces = [jnp.concatenate([taps.reshape(2, 9 * C, C), tail], axis=1)]
    block_one, vec = call(block_kernel, [((12 * C, 2 * C), BF16), ((16, C), F32)], pieces, flops=10**8)
    x_all, pre_one, sums_one = call(
        first_kernel,
        [((11, 2, TI, W3), BF16), ((R + 4, TI, C), F32), ((devices, MB, 2, C), F32)],
        (x_near, lat_in, far_left, far_right, block_one, vec),
        flats,
        flops=conv_flops * 6,
    )
    sums_one, dn = lax.optimization_barrier((sums_one, dn))
    got_one = spread(sums_one, ALL)
    block_two, two_back, one_back = call(
        weight_kernel,
        [((12 * C, 2 * C), BF16)] * 3,
        (got_one, block_one, *pieces),
        flops=10**8,
    )
    (pre_side,) = call(
        halo_kernel,
        [((R + 4, TH, C), F32)],
        (got_one, x_near, lat_in, far_left, far_right, block_one, vec),
        [pltpu.VMEM((11, 2, TH, W3), BF16)] + flats,
        flops=conv_flops * 4,
    )
    got_one, cot_r, cot_l = lax.optimization_barrier((got_one, cot_r, cot_l))
    cot_left, cot_right = turn(cot_r, "lon", 1), turn(cot_l, "lon", -1)
    n_all, pre_two, sums_two, stat_one = call(
        lambda *refs: second_kernel(count, *refs),
        [((10, 2, T, W3), BF16), ((R + 2, T, C), F32), ((devices, 3, 4, C), F32), ((8, C), F32)],
        (pre_one, pre_side, got_one, dn, dn_sums, block_two, vec),
        flats,
        flops=conv_flops * 9,
    )
    sums_two, cot_left, cot_right = lax.optimization_barrier((sums_two, cot_left, cot_right))
    got_two = spread(sums_two, ALL)
    grad_two, mid, sums_three, stat_two, bias_two = call(
        lambda *refs: back_two_kernel(count, *refs),
        [((R, TI, C), BF16), ((R + 2, T, C), F32), ((devices, MB, 2, C), F32), ((4 * MB, C), F32), ((8, C), F32)],
        (lead_time, pre_two, dn, lat_in, cot_left, cot_right, got_two, pre_one, two_back, vec),
        [pltpu.VMEM((10, 2, T, W3), BF16)] + flats * 2,
        scalars=1,
        flops=conv_flops * 9,
    )
    got_three = spread(sums_three, ALL)
    grad_kinds = [((4, 304, C), F32), ((4, 304, C), BF16)] if split else [((2, 9, C, C), F32)]
    g_inner, bias_one, stat_three, *grads = call(
        lambda *refs: back_one_kernel(split, count, *refs),
        [((9, 2, TI, W3), BF16), ((8, C), F32), ((8, C), F32)] + grad_kinds,
        (pre_one, pre_side, mid, stat_one, got_three, x_all, n_all, grad_two, bias_two, vec),
        [pltpu.VMEM((3, C, W3), F32)] * 2 + flats,
        flops=conv_flops * 9,
    )

    def finish(after):
        (outputs,) = call(
            lambda *refs: output_kernel(count, *refs),
            [((S, R, R, C), BF16)],
            (after, inputs, pre_two, stat_two, vec),
            flops=10**8,
        )
        (grad_inputs,) = call(
            input_grad_kernel,
            [((S, R, R, C), BF16)],
            (lead_time, after, g_inner, cotangent, one_back),
            flops=conv_flops * 6,
            scalars=1,
        )
        return outputs, grad_inputs

    if split:
        merged = call(merge_kernel, [((304, C), BF16)] * 4, (grads[0], turn(grads[1], "lat", 1)))
        column = [merged[0]] + [turn(merged[k], "dp", k) for k in range(1, 4)]
        outputs, grad_inputs = finish(merged[0])
        (added_up,) = call(column_kernel, [((304, C), BF16)], column)
        row = [added_up] + [turn(added_up, "lon", k) for k in range(1, 4)]
        own, sums_four = call(
            plane_kernel,
            [((288, C), F32), ((2 * groups, 4, C), F32)],
            (outputs, grad_inputs, *row),
            [pltpu.VMEM((4, 304, C), F32)],
            far=2,
        )
        got_four = spread(sums_four, ("dp", "lat"))
        its = turn(own, "lat", 1)
        kinds = [((1, 1), F32)] + [(conv_weight.shape, F32)] * 3 + [(conv_weight.shape, BF16)]
        moments = (conv_weight, conv_first, conv_second, vectors, vec_first, vec_second)
        moments = call(
            fetch_kernel,
            [(moment.shape, F32) for moment in moments],
            (*moments, own),
            [pltpu.SemaphoreType.DMA((6,))],
            flops=10**10,
            far=6,
        )
        norm, *news = call(
            lambda *refs: update_kernel(count, *refs),
            kinds + [(vectors.shape, F32)] * 3,
            (*moments, own, its, got_four, stat_one, stat_two, stat_three),
            [pltpu.VMEM(conv_weight.shape, F32)],
        )
        return (outputs, grad_inputs, norm.reshape(()), *news)
    outputs, grad_inputs = finish(bias_one)
    stacked = grads[0].transpose(0, 2, 1, 3).reshape(2, 9 * C, C)
    conv_total, total_one, total_two = lax.psum((stacked, bias_one[0:1], bias_two[0:1]), ALL)
    vec_total = vector_grads(stat_one, stat_two, stat_three, total_one, total_two, count)
    grad_norm = jnp.sqrt(jnp.sum(conv_total * conv_total) + jnp.sum(vec_total * vec_total))
    clip = jnp.minimum(1.0, CLIP / (grad_norm + 1e-06))
    index = lax.axis_index("dp")
    conv_own = lax.dynamic_slice_in_dim(conv_total, index * conv_weight.shape[1], conv_weight.shape[1], 1)
    vec_own = lax.dynamic_slice_in_dim(vec_total, index * vectors.shape[1], vectors.shape[1], 1)
    conv_news = adam(conv_weight, conv_first, conv_second, conv_own * clip, RATE_CONV, DECAY_CONV)
    vec_news = adam(vectors, vec_first, vec_second, vec_own * clip, RATE_VEC, 0.0)
    return (outputs, grad_inputs, grad_norm, *conv_news, conv_news[0].astype(BF16), *vec_news)


def solution(mesh):
    grid = P("dp", "lat", "lon", None)
    rows = P(None, "dp", None)
    columns = P(None, "dp")
    in_specs = (grid, P("dp"), grid, rows, rows, rows, columns, columns, columns)
    out_specs = (grid, grid, P(), rows, rows, rows, rows, columns, columns, columns)
    return jax.shard_map(body, mesh=mesh, in_specs=in_specs, out_specs=out_specs, check_vma=False)
```
